256 devices in a mesh: gx: 16 (over x, z_hi), gy: 4 (over y), gz: 4 (over z_lo, core).
Axes of the slice: x: 4, y: 4, z: 8 (z_hi: 4, z_lo: 2; z = z_hi * 2 + z_lo), core: 2. Of those that a mesh axis runs over, the one named last changes fastest.
Arguments:
- solid_state: float32 [9, 32, 128, 512], P(None, 'gz', 'gx', 'gy'), may hold values from -6 to 6
- material: float32 [4, 32, 128, 512], P(None, 'gz', 'gx', 'gy'), may hold values from 0.5 to 2
- ocean_state: float32 [4, 16, 256, 1024], P(None, None, 'gx', ('gy', 'gz')), may hold values from -6 to 6
- ocean_medium: float32 [2, 16], replicated, may hold values from 0.5 to 2
- offset_x: int32 [256], P('gx'), may hold values from -1 to 1
- offset_y: int32 [1024], P(('gy', 'gz')), may hold values from -1 to 1
Outputs:
- solid_next: float32 [9, 32, 128, 512], P(None, 'gz', 'gx', 'gy')
- solid_rate: float32 [9, 32, 128, 512], P(None, 'gz', 'gx', 'gy')
- ocean_next: float32 [4, 16, 256, 1024], P(None, None, 'gx', ('gy', 'gz'))
- ocean_rate: float32 [4, 16, 256, 1024], P(None, None, 'gx', ('gy', 'gz'))
The draws below stay inside these ranges and needn't reach their ends.
All inputs are finite; a program needn't handle non-finite values.
Results may differ from the reference program's by a relative error of at most 0.000059.
Values sent between devices are 32-bit elements; how exact they have to be, the bound alone decides.
A program may use at most 64 MiB of HBM per device.

```python
import math
import jax
import jax.numpy as jnp
from jax import lax

OZ = 16
NX = 128
NY = 512
NZ = 32
FX = 256
FY = 1024


def plant(array, rng, least, top_value):
    place = [jax.random.randint(jax.random.fold_in(rng, axis), (), 0, length) for axis, length in enumerate(array.shape)]
    widest = array.shape.index(max(array.shape))
    beside = place[:widest] + [(place[widest] + 1) % array.shape[widest]] + place[widest + 1:]
    return array.at[tuple(place)].set(least).at[tuple(beside)].set(top_value)


def shard_levels(own_key, shape, shards, smallest, top_value):
    def one(axis_at, parts):
        draws = jax.random.uniform(jax.random.fold_in(jax.random.fold_in(own_key, 6), axis_at), (parts,), jnp.float32, smallest / len(shards), top_value / len(shards))
        return jnp.repeat(jnp.exp(draws), shape[axis_at] // parts).reshape((-1,) + (1,) * (len(shape) - axis_at - 1))

    loudness = one(*shards[0])
    for cut in shards[1:]:
        loudness = loudness * one(*cut)
    return loudness


def bell_draw(rng, dims, width, limit, cuts=(), held_as=jnp.bfloat16):
    drawn = jax.random.normal(rng, dims, jnp.float32) * width
    if len(cuts) > 0:
        drawn = shard_levels(rng, dims, cuts, -0.22, 0.18) * drawn
    return jnp.clip(drawn, min=-limit, max=limit).astype(held_as)


def setup_inputs(seed: int = 0) -> dict:
    keys = jax.random.split(jax.random.key(seed), 7)
    solid_state = bell_draw(keys[0], (9, NZ, NX, NY), 1.0, 6.0, ((1, 4), (2, 16), (3, 4)), jnp.float32)
    material = jnp.clip(jnp.exp(math.log(2.0) - 1.3862944 * jax.random.uniform(keys[1], (4, NZ, NX, NY), jnp.float32) ** shard_levels(keys[1], (4, NZ, NX, NY), ((1, 4), (2, 16), (3, 4)), -0.2, 0.2)), 0.5, 2.0)
    ocean_state = bell_draw(keys[2], (4, OZ, FX, FY), 1.0, 6.0, ((2, 16), (3, 16)), jnp.float32)
    ocean_medium = jnp.clip(jnp.exp(jax.random.uniform(keys[3], (2, OZ), jnp.float32, math.log(0.5), math.log(2.0))), 0.5, 2.0)
    offset_x = plant(jax.random.randint(keys[4], (FX,), -1, 2), jax.random.fold_in(keys[4], 1), -1, 1).astype(jnp.int32)
    offset_y = plant(jax.random.randint(keys[5], (FY,), -1, 2), jax.random.fold_in(keys[5], 1), -1, 1).astype(jnp.int32)
    return dict(solid_state=solid_state, material=material, ocean_state=ocean_state, ocean_medium=ocean_medium, offset_x=offset_x, offset_y=offset_y)


closure_rows = ((-24.0 / 17.0, 59.0 / 34.0, -4.0 / 17.0, -3.0 / 34.0, 0.0, 0.0),
                (-0.5, 0.0, 0.5, 0.0, 0.0, 0.0),
                (4.0 / 43.0, -59.0 / 86.0, 0.0, 59.0 / 86.0, -4.0 / 43.0, 0.0),
                (3.0 / 98.0, 0.0, -59.0 / 98.0, 0.0, 32.0 / 49.0, -4.0 / 49.0))
inv_norm = 48.0 / 17.0
step_size = 0.25
section_weight = 0.1496590219993
gravity = 0.4


def take_slab(field, first_index, length, dimension):
    return lax.slice_in_dim(field, first_index, first_index + length, axis=dimension)


def closure(field, dimension, at_end):
    extent = field.shape[dimension]
    pieces = []
    for row_index in range(4):
        running = jnp.zeros_like(take_slab(field, 0, 1, dimension))
        for col_index in range(6):
            weight = closure_rows[row_index][col_index]
            if weight != 0.0:
                if at_end:
                    running = running - weight * take_slab(field, extent - 1 - col_index, 1, dimension)
                else:
                    running = running + weight * take_slab(field, col_index, 1, dimension)
        pieces.append(running)
    if at_end:
        pieces = pieces[::-1]
    return jnp.concatenate(pieces, axis=dimension)


def interior(padded, dimension, extent):
    return (take_slab(padded, 0, extent, dimension) - 8.0 * take_slab(padded, 1, extent, dimension)
            + 8.0 * take_slab(padded, 3, extent, dimension) - take_slab(padded, 4, extent, dimension)) / 12.0


def derivative(field, dimension):
    extent = field.shape[dimension]
    widths = [(0, 0)] * field.ndim
    widths[dimension] = (2, 2)
    middle = interior(jnp.pad(field, widths), dimension, extent)
    return jnp.concatenate([closure(field, dimension, False), take_slab(middle, 4, extent - 8, dimension),
                            closure(field, dimension, True)], axis=dimension)


def blend_matrix(offsets, fine_first, coarse_first, columns, coarse_total):
    fine_index = fine_first + jnp.arange(offsets.shape[0], dtype=jnp.int32)
    coarse = fine_index // 2
    target = jnp.clip(coarse + offsets, 0, coarse_total - 1)
    column = jnp.arange(columns, dtype=jnp.int32)[None, :]
    nearest = (column == (coarse - coarse_first)[:, None]).astype(jnp.float32)
    farther = (column == (target - coarse_first)[:, None]).astype(jnp.float32)
    return 0.75 * nearest + 0.25 * farther


def restrict(bottom):
    fine_rows, fine_cols = bottom.shape
    return bottom.reshape(fine_rows // 2, 2, fine_cols // 2, 2).mean(axis=(1, 3))


def solid_rates(material, diff_x, diff_y, diff_z):
    buoyancy = material[0]
    lame_one = material[1]
    lame_two = material[2]
    metric = material[3]

    def vertical(member):
        return metric * diff_z(member)

    strain_xx = diff_x(0)
    strain_yy = diff_y(1)
    strain_zz = vertical(2)
    dilation = strain_xx + strain_yy + strain_zz
    return [buoyancy * (diff_x(3) + diff_y(8) + vertical(7)),
            buoyancy * (diff_x(8) + diff_y(4) + vertical(6)),
            buoyancy * (diff_x(7) + diff_y(6) + vertical(5)),
            lame_one * dilation + 2.0 * lame_two * strain_xx,
            lame_one * dilation + 2.0 * lame_two * strain_yy,
            lame_one * dilation + 2.0 * lame_two * strain_zz,
            lame_two * (vertical(1) + diff_y(2)),
            lame_two * (vertical(0) + diff_x(2)),
            lame_two * (diff_y(0) + diff_x(1))]


def seafloor_terms(state, material, bed_pressure):
    factor = inv_norm * material[0, 0] * material[3, 0]
    return factor * state[7, 0], factor * state[6, 0], factor * (state[5, 0] + bed_pressure)


def ocean_rates(state, medium, diff_x, diff_y, bed_speed):
    bulk = medium[0][:, None, None]
    light = medium[1][:, None, None]
    pressure = state[0]
    flow_z = state[3]
    rate_p = -bulk * (2.0 * diff_x(1) + 2.0 * diff_y(2) + derivative(flow_z, 0)) + gravity * flow_z / light
    rate_p = rate_p.at[-1].add(inv_norm * bulk[-1] * (flow_z[-1] - bed_speed))
    rate_u = -2.0 * light * diff_x(0)
    rate_v = -2.0 * light * diff_y(0)
    rate_w = -light * derivative(pressure, 0)
    rate_w = rate_w.at[0].add(-inv_norm * light[0] * pressure[0])
    return jnp.stack([rate_p, rate_u, rate_v, rate_w])


def reference(solid_state, material, ocean_state, ocean_medium, offset_x, offset_y):
    highest = lax.Precision.HIGHEST
    plane = solid_state[2, 0]
    blend_x = blend_matrix(offset_x, 0, 0, NX, NX)
    blend_y = blend_matrix(offset_y, 0, 0, NY, NY)
    bed_speed = jnp.dot(jnp.dot(blend_x, plane, precision=highest), blend_y.T, precision=highest)
    bed_pressure = restrict(ocean_state[0, -1])
    rates = solid_rates(material,
                        lambda member: derivative(solid_state[member], 1),
                        lambda member: derivative(solid_state[member], 2),
                        lambda member: derivative(solid_state[member], 0))
    term_x, term_y, term_z = seafloor_terms(solid_state, material, bed_pressure)
    rates[0] = rates[0].at[0].add(term_x)
    rates[1] = rates[1].at[0].add(term_y)
    rates[2] = rates[2].at[0].add(term_z)
    solid_rate = step_size * jnp.stack(rates)
    solid_next = solid_state + section_weight * solid_rate
    ocean_rate = step_size * ocean_rates(ocean_state, ocean_medium,
                                         lambda member: derivative(ocean_state[member], 1),
                                         lambda member: derivative(ocean_state[member], 2),
                                         bed_speed)
    ocean_next = ocean_state + section_weight * ocean_rate
    return solid_next, solid_rate, ocean_next, ocean_rate
```

```python
import functools

import jax
import jax.numpy as jnp
from jax import lax
from jax.experimental import pallas as pl
from jax.experimental.pallas import tpu as pltpu
from jax.sharding import PartitionSpec as P

closure_rows = (
    (-24.0 / 17.0, 59.0 / 34.0, -4.0 / 17.0, -3.0 / 34.0, 0.0, 0.0),
    (-0.5, 0.0, 0.5, 0.0, 0.0, 0.0),
    (4.0 / 43.0, -59.0 / 86.0, 0.0, 59.0 / 86.0, -4.0 / 43.0, 0.0),
    (3.0 / 98.0, 0.0, -59.0 / 98.0, 0.0, 32.0 / 49.0, -4.0 / 49.0),
)
inner_row = {-2: 1.0 / 12.0, -1: -8.0 / 12.0, 1: 8.0 / 12.0, 2: -1.0 / 12.0}
inv_norm = 48.0 / 17.0
step_size = 0.25
section_weight = 0.1496590219993
gravity = 0.4

MESH = pl.DeviceIdType.MESH
F32 = jnp.float32
HIGHEST = lax.Precision.HIGHEST
REACH = range(-3, 4)

x_fields = (0, 1, 2, 3, 7, 8)
y_fields = (0, 1, 2, 4, 6, 8)
z_fields = (0, 1, 2, 5, 6, 7)


def low_weight(k, d):
    return closure_rows[k][k + d] if 0 <= k + d < 6 else 0.0


def high_weight(k, d):
    return -closure_rows[k][k - d] if 0 <= k - d < 6 else 0.0


def weights(pos, n, first, last, closed):
    at_low = pos + jnp.where(first, 0, 4096)
    at_high = (n - 1) - pos + jnp.where(last, 0, 4096)
    table = {}
    for d in REACH:
        w = jnp.full(pos.shape, inner_row.get(d, 0.0), F32)
        if closed and d < 0:
            w = jnp.where(pos + d >= 0, w, 0.0)
        if closed and d > 0:
            w = jnp.where(pos + d < n, w, 0.0)
        for k in range(4):
            w = jnp.where(at_low == k, low_weight(k, d), w)
            w = jnp.where(at_high == k, high_weight(k, d), w)
        table[d] = w
    return table


def level_weights(level, n, first, last):
    table = {}
    for d in REACH:
        w = inner_row.get(d, 0.0)
        if level < 4 and first is not False:
            c = low_weight(level, d)
            w = c if first is True else (jnp.where(first, c, w) if c != w else w)
        elif level >= n - 4 and last is not False:
            c = high_weight(n - 1 - level, d)
            w = c if last is True else (jnp.where(last, c, w) if c != w else w)
        if not (isinstance(w, float) and w == 0.0):
            table[d] = w
    return table


def total(terms):
    out = None
    for term in terms:
        out = term if out is None else out + term
    return out


def roll_lanes(x, shift):
    return pltpu.roll(x, shift % 128, x.ndim - 1)


def rim_from_sides(left, right, lane, first, last):
    s = lax.rem(lane, 4)
    twelfth = 1.0 / 12.0
    from_left = jnp.where(first, 0.0, twelfth)
    from_right = jnp.where(last, 0.0, twelfth)
    one_left = jnp.where(s >= 2, from_left, 0.0)
    eight_left = jnp.where(s == 2, -8.0 * from_left, 0.0)
    one_right = jnp.where(s < 2, -from_right, 0.0)
    eight_right = jnp.where(s == 1, 8.0 * from_right, 0.0)
    return (
        one_left * roll_lanes(left, 2)
        + eight_left * roll_lanes(left, 1)
        + one_right * roll_lanes(right, -2)
        + eight_right * roll_lanes(right, -1)
    )


def section_kernel(
    sizes,
    solid, material, ocean, medium, off_x, off_y,
    s_next, s_rate, o_next, o_rate,
    sb, mb, ob, ov, med, ox, oy,
    z_low, z_high, plane, bed_part,
    ys_out, ys_left, ys_right, yo_out, yo_left, yo_right, coarse_out,
    dys, dyo, dzs, txs, opre, cat,
    local_sem, send_sem, recv_sem,
):
    nx, ny, nz = sizes
    gx, gy, gz = lax.axis_index("gx"), lax.axis_index("gy"), lax.axis_index("gz")
    up_x, down_x = lax.rem(gx + 1, nx), lax.rem(gx + nx - 1, nx)
    up_y, down_y = lax.rem(gy + 1, ny), lax.rem(gy + ny - 1, ny)
    x_first, x_last = gx == 0, gx == nx - 1
    y_first, y_last = gy == 0, gy == ny - 1
    z_first, z_last = gz == 0, gz == nz - 1
    right = (gx, jnp.where(z_last, up_y, gy), jnp.where(z_last, 0, gz + 1))
    left = (gx, jnp.where(z_first, down_y, gy), jnp.where(z_first, nz - 1, gz - 1))
    xs = {-1: down_x, 0: gx, 1: up_x}

    barrier = pltpu.get_barrier_semaphore()

    def greet(x, y, z):
        pl.semaphore_signal(barrier, inc=1, device_id=(x, y, z), device_id_type=MESH)

    greet(up_x, gy, gz)
    greet(down_x, gy, gz)
    greet(gx, up_y, gz)
    greet(gx, down_y, gz)
    greet(*right)
    greet(*left)

    @pl.when(z_first)
    def _():
        for e in (-1, 1):
            greet(xs[e], down_y, 0)
        for k in range(2, nz):
            greet(gx, gy, k)

    @pl.when(gz > 0)
    def _():
        for e in (-1, 1):
            greet(xs[e], gy, 0)

    @pl.when(gz > 1)
    def _():
        greet(gx, gy, 0)

    @pl.when(z_last)
    def _():
        for e in (-1, 1):
            greet(xs[e], up_y, 0)

    loads = [
        pltpu.make_async_copy(src, dst, local_sem.at[i])
        for i, (src, dst) in enumerate(
            (
                (solid, sb.at[:, :, 8:16]),
                (ocean.at[0:2], ob.at[:, :, 8:24]),
                (ocean.at[2:4], ov),
                (material, mb),
                (medium, med),
                (off_x, ox),
                (off_y, oy),
            )
        )
    ]
    for load in loads:
        load.start()

    @pl.when(z_first)
    def _():
        z_low[...] = jnp.zeros_like(z_low)

    @pl.when(z_last)
    def _():
        z_high[...] = jnp.zeros_like(z_high)

    @pl.when(z_first)
    def _():
        pl.semaphore_wait(barrier, 6 + (nz - 2) + 2 * (nz - 1) + 4)

    @pl.when(gz == 1)
    def _():
        pl.semaphore_wait(barrier, 6)

    @pl.when(gz > 1)
    def _():
        pl.semaphore_wait(barrier, 7)

    counter = iter(range(64))

    def remote(src, dst, recv, device):
        return pltpu.make_async_remote_copy(
            src_ref=src, dst_ref=dst, send_sem=send_sem.at[next(counter)], recv_sem=recv_sem.at[recv],
            device_id=device, device_id_type=MESH,
        )

    x_copies = []
    for i, (a, b) in enumerate(((0, 4), (7, 9))):
        x_copies.append(remote(solid.at[a:b, :, 6:8], sb.at[a:b, :, 6:8], 2 * i, (up_x, gy, gz)))
        x_copies.append(remote(solid.at[a:b, :, 0:2], sb.at[a:b, :, 16:18], 2 * i + 1, (down_x, gy, gz)))
    x_copies.append(remote(ocean.at[0:2, :, 14:16], ob.at[:, :, 6:8], 4, (up_x, gy, gz)))
    x_copies.append(remote(ocean.at[0:2, :, 0:2], ob.at[:, :, 24:26], 5, (down_x, gy, gz)))
    for copy in x_copies:
        copy.start()

    z_up = [
        remote(solid.at[a : a + 3, 6:8], z_low.at[b : b + 3], 6 + i, (gx, gy, gz + 1))
        for i, (a, b) in enumerate(((0, 0), (5, 3)))
    ]
    z_down = [
        remote(solid.at[a : a + 3, 0:2], z_high.at[b : b + 3], 8 + i, (gx, gy, gz - 1))
        for i, (a, b) in enumerate(((0, 0), (5, 3)))
    ]

    @pl.when(gz < nz - 1)
    def _():
        for copy in z_up:
            copy.start()

    @pl.when(gz > 0)
    def _():
        for copy in z_down:
            copy.start()

    tile = solid.at[2, 0]
    plane_copies = []
    for e in (-1, 0, 1):
        x = xs[-e]
        for k in range(nz):
            if e != 0 or k != 0:
                plane_copies.append(remote(tile, plane.at[0, e + 1], 10 + e + 1, (x, gy, k)))
        plane_copies.append(remote(tile, plane.at[1, e + 1], 13 + e + 1, (x, up_y, 0)))
        plane_copies.append(remote(tile, plane.at[1, e + 1], 13 + e + 1, (x, down_y, nz - 1)))
    own_plane = pltpu.make_async_copy(tile, plane.at[0, 1], local_sem.at[7])

    @pl.when(z_first)
    def _():
        own_plane.start()
        for copy in plane_copies:
            copy.start()

    lane = lax.broadcasted_iota(jnp.int32, (8, 128), 1)

    loads[0].wait()
    for half, fields in enumerate((y_fields[:4], y_fields[4:])):
        packed = jnp.zeros((8, 128), F32)
        for i, f in enumerate(fields):
            for z in range(8):
                k = 8 * i + z
                packed = jnp.where(lane // 4 == k, roll_lanes(sb[f, z, 8:16, :], 4 * k + 2), packed)
        ys_out[half] = packed
    ys_copies = [
        remote(ys_out, ys_left, 16, (gx, up_y, gz)),
        remote(ys_out, ys_right, 17, (gx, down_y, gz)),
    ]
    for copy in ys_copies:
        copy.start()

    loads[1].wait()
    loads[2].wait()
    half_lane = lax.rem(lane, 64)
    for i in range(2):
        packed = jnp.zeros((8, 128), F32)
        for d in range(16):
            if i == 0:
                both = jnp.concatenate([ob[0, d, 8:16, :], ob[0, d, 16:24, :]], axis=1)
            else:
                both = jnp.concatenate([ov[0, d, 0:8, :], ov[0, d, 8:16, :]], axis=1)
            cat[i, d] = both
            packed = jnp.where(half_lane // 4 == d, roll_lanes(both, 4 * d + 2), packed)
        yo_out[i] = packed
    yo_copies = [remote(yo_out, yo_left, 18, right), remote(yo_out, yo_right, 19, left)]
    for copy in yo_copies:
        copy.start()

    row = lax.broadcasted_iota(jnp.int32, (8, 16), 0)
    col = lax.broadcasted_iota(jnp.int32, (8, 16), 1)
    pair = jnp.where(col // 2 == row, 0.5, 0.0)
    fine = lax.broadcasted_iota(jnp.int32, (64, 128), 0)
    out_lane = lax.broadcasted_iota(jnp.int32, (64, 128), 1)
    place = jnp.where(out_lane == 32 * gz + fine // 2, 0.5, 0.0)
    coarse = jnp.dot(pair, ob[0, 15, 8:24, :], precision=HIGHEST, preferred_element_type=F32)
    coarse = jnp.dot(coarse, place, precision=HIGHEST, preferred_element_type=F32)
    coarse_out[...] = coarse
    coarse_copies = [remote(coarse_out, bed_part.at[k], 20 + k, (gx, gy, 0)) for k in range(1, nz)]
    for k in range(1, nz):

        @pl.when(gz == k)
        def _(k=k):
            coarse_copies[k - 1].start()

    wy = weights(lane, 128, y_first, y_last, True)
    for i, f in enumerate(y_fields):
        own = sb[f, :, 8:16, :]
        dys[i] = total(wy[d] * (roll_lanes(own, -d) if d else own) for d in REACH)
    wo = weights(half_lane, 64, jnp.logical_and(y_first, z_first), jnp.logical_and(y_last, z_last), True)
    for i in range(2):
        for d0 in range(0, 16, 8):
            own = cat[i, d0 : d0 + 8]
            dyo[i, d0 : d0 + 8] = total(wo[d] * (roll_lanes(own, -d) if d else own) for d in REACH)
    sub = lax.broadcasted_iota(jnp.int32, (8, 128), 0)
    wx = weights(sub, 8, x_first, x_last, False)
    for i, f in enumerate(x_fields):
        own = sb[f, :, 8:16, :]
        txs[i] = wx[0] * own + wx[3] * pltpu.roll(own, 5, 1) + wx[-3] * pltpu.roll(own, 3, 1)

    for copy in ys_copies:
        copy.wait_recv()
    at_edge = jnp.logical_or(lane < 2, lane >= 126)
    for half, fields in enumerate((y_fields[:4], y_fields[4:])):
        rim = rim_from_sides(ys_left[half], ys_right[half], lane, y_first, y_last)
        for i in range(len(fields)):
            for z in range(8):
                k = 8 * i + z
                dys[4 * half + i, z] += jnp.where(at_edge, roll_lanes(rim, -4 * k - 2), 0.0)
    for copy in yo_copies:
        copy.wait_recv()
    at_half_edge = jnp.logical_or(half_lane < 2, half_lane >= 62)
    for i in range(2):
        rim = rim_from_sides(
            roll_lanes(yo_left[i], 64), roll_lanes(yo_right[i], 64), lane,
            jnp.logical_and(y_first, z_first), jnp.logical_and(y_last, z_last),
        )
        for d in range(16):
            dyo[i, d] += jnp.where(at_half_edge, roll_lanes(rim, -4 * d - 2), 0.0)

    loads[3].wait()

    @pl.when(gz > 0)
    def _():
        for copy in z_up:
            copy.wait_recv()

    @pl.when(gz < nz - 1)
    def _():
        for copy in z_down:
            copy.wait_recv()

    for i, f in enumerate(z_fields):
        def level(z, i=i, f=f):
            if z < 0:
                return z_low[i, z + 2]
            if z >= 8:
                return z_high[i, z - 8]
            return sb[f, z, 8:16, :]

        for z in range(8):
            table = level_weights(z, 8, z_first, z_last)
            dzs[i, z] = mb[3, z] * total(w * level(z + d) for d, w in table.items() if -2 <= z + d < 10)

    @pl.when(z_first)
    def _():
        for k in range(1, nz):
            pltpu.make_async_remote_copy(
                src_ref=coarse_out, dst_ref=bed_part.at[k], send_sem=send_sem.at[63], recv_sem=recv_sem.at[20 + k],
                device_id=(gx, up_y, gz), device_id_type=MESH,
            ).wait_recv()
        scale = inv_norm * mb[3, 0]
        bed_pressure = coarse_out[...] + total(bed_part[k] for k in range(1, nz))
        dzs[5, 0] += scale * sb[7, 0, 8:16, :]
        dzs[4, 0] += scale * sb[6, 0, 8:16, :]
        dzs[3, 0] += scale * (sb[5, 0, 8:16, :] + bed_pressure)

    loads[5].wait()
    loads[6].wait()

    def plane_wait(s, e):
        pltpu.make_async_remote_copy(
            src_ref=tile, dst_ref=plane.at[s, e + 1], send_sem=send_sem.at[63], recv_sem=recv_sem.at[10 + 3 * s + e + 1],
            device_id=(gx, up_y, gz), device_id_type=MESH,
        ).wait_recv()

    plane_wait(0, -1)
    plane_wait(0, 1)

    @pl.when(z_first)
    def _():
        own_plane.wait()
        for e in (-1, 0, 1):
            plane_wait(1, e)
            plane[0, e + 1] = jnp.where(lane == 127, plane[1, e + 1], plane[0, e + 1])

    @pl.when(gz > 0)
    def _():
        plane_wait(0, 0)

    @pl.when(z_last)
    def _():
        for e in (-1, 0, 1):
            plane_wait(1, e)
            plane[0, e + 1] = jnp.where(lane == 0, plane[1, e + 1], plane[0, e + 1])

    window = plane[0].reshape(24, 128)
    fine_x = lax.broadcasted_iota(jnp.int32, (24, 16), 1)
    coarse_x = lax.broadcasted_iota(jnp.int32, (24, 16), 0) + (8 * gx - 8)
    near_x = 8 * gx + fine_x // 2
    far_x = jnp.clip(near_x + ox[...], 0, 8 * nx - 1)
    blend_x = jnp.where(coarse_x == near_x, 0.75, 0.0) + jnp.where(coarse_x == far_x, 0.25, 0.0)
    fine_y = lax.broadcasted_iota(jnp.int32, (128, 64), 1)
    coarse_y = lax.broadcasted_iota(jnp.int32, (128, 64), 0)
    near_y = 128 * gy + 32 * gz + fine_y // 2
    far_y = jnp.clip(near_y + oy[...], 0, 128 * ny - 1)
    blend_y = jnp.where(coarse_y == lax.rem(near_y, 128), 0.75, 0.0)
    blend_y = blend_y + jnp.where(coarse_y == lax.rem(far_y, 128), 0.25, 0.0)
    bed_speed = lax.dot_general(
        blend_x, window, (((0,), (0,)), ((), ())), precision=HIGHEST, preferred_element_type=F32
    )
    bed_speed = jnp.dot(bed_speed, blend_y, precision=HIGHEST, preferred_element_type=F32)

    loads[4].wait()

    def unfold(i, d):
        both = dyo[i, d]
        return jnp.concatenate([both[:, 0:64], both[:, 64:128]], axis=0)

    for d in range(16):
        bulk = jnp.full((16, 64), med[0, d], F32)
        light = jnp.full((16, 64), med[1, d], F32)
        pressure, flow_v, flow_w = ob[0, d, 8:24, :], ov[0, d], ov[1, d]
        table = level_weights(d, 16, True, True)
        dz_w = total(w * ov[1, d + k] for k, w in table.items())
        dz_p = total(w * ob[0, d + k, 8:24, :] for k, w in table.items())
        part = -bulk * (2.0 * unfold(1, d) + dz_w) + gravity * flow_w / light
        if d == 15:
            part = part + inv_norm * bulk * (flow_w - bed_speed)
        opre[d] = step_size * part
        rate_v = (-2.0 * step_size) * light * unfold(0, d)
        rate_w = -light * dz_p
        if d == 0:
            rate_w = rate_w - inv_norm * light * pressure
        rate_w = step_size * rate_w
        o_rate[2, d] = rate_v
        o_rate[3, d] = rate_w
        o_next[2, d] = flow_v + section_weight * rate_v
        o_next[3, d] = flow_w + section_weight * rate_w

    for copy in x_copies:
        copy.wait_recv()

    def dx(i, f, z):
        out = txs[i, z]
        for d in (-2, -1, 1, 2):
            out = out + wx[d] * sb[f, z, 8 + d : 16 + d, :]
        return out

    for z in range(8):
        own = [sb[f, z, 8:16, :] for f in range(9)]
        b, lam, mu = step_size * mb[0, z], step_size * mb[1, z], step_size * mb[2, z]
        d_x = {f: dx(i, f, z) for i, f in enumerate(x_fields)}
        d_y = {f: dys[i, z] for i, f in enumerate(y_fields)}
        d_z = {f: dzs[i, z] for i, f in enumerate(z_fields)}
        dilation = lam * (d_x[0] + d_y[1] + d_z[2])
        mu2 = 2.0 * mu
        rates = [
            b * (d_x[3] + d_y[8] + d_z[7]),
            b * (d_x[8] + d_y[4] + d_z[6]),
            b * (d_x[7] + d_y[6] + d_z[5]),
            dilation + mu2 * d_x[0],
            dilation + mu2 * d_y[1],
            dilation + mu2 * d_z[2],
            mu * (d_z[1] + d_y[2]),
            mu * (d_z[0] + d_x[2]),
            mu * (d_y[0] + d_x[1]),
        ]
        for f in range(9):
            s_rate[f, z] = rates[f]
            s_next[f, z] = own[f] + section_weight * rates[f]

    pos = lax.broadcasted_iota(jnp.int32, (16, 64), 0)
    wp = weights(pos, 16, x_first, x_last, False)
    far_up, far_down = wp[3] != 0.0, wp[-3] != 0.0

    def dx_ocean(i, d):
        out = total(wp[k] * ob[i, d, 8 + k : 24 + k, :] for k in range(-2, 3))
        out = out + wp[3] * jnp.where(far_up, ob[i, d, 11:27, :], 0.0)
        return out + wp[-3] * jnp.where(far_down, ob[i, d, 5:21, :], 0.0)

    for d in range(16):
        bulk = jnp.full((16, 64), (-2.0 * step_size) * med[0, d], F32)
        light = jnp.full((16, 64), (-2.0 * step_size) * med[1, d], F32)
        rate_p = opre[d] + bulk * dx_ocean(1, d)
        rate_u = light * dx_ocean(0, d)
        o_rate[0, d] = rate_p
        o_rate[1, d] = rate_u
        o_next[0, d] = ob[0, d, 8:24, :] + section_weight * rate_p
        o_next[1, d] = ob[1, d, 8:24, :] + section_weight * rate_u

    for copy in x_copies + ys_copies + yo_copies:
        copy.wait_send()

    @pl.when(gz < nz - 1)
    def _():
        for copy in z_up:
            copy.wait_send()

    @pl.when(gz > 0)
    def _():
        for copy in z_down:
            copy.wait_send()

    @pl.when(z_first)
    def _():
        for copy in plane_copies:
            copy.wait_send()

    for k in range(1, nz):

        @pl.when(gz == k)
        def _(k=k):
            coarse_copies[k - 1].wait_send()


def write_kernel(*refs):
    count = (len(refs) - 1) // 2
    sem = refs[-1]
    copies = [pltpu.make_async_copy(refs[i], refs[count + i], sem.at[i]) for i in range(count)]
    for copy in copies:
        copy.start()
    for copy in copies:
        copy.wait()


def body(sizes, solid_state, material, ocean_state, ocean_medium, offset_x, offset_y):
    outs = (solid_state.shape, solid_state.shape, ocean_state.shape, ocean_state.shape)
    v = lambda *shape: pltpu.VMEM(shape, F32)
    held = pl.pallas_call(
        functools.partial(section_kernel, sizes),
        out_shape=[pltpu.VMEM(shape, F32) for shape in outs],
        in_specs=[pl.BlockSpec(memory_space=pltpu.HBM)] * 6,
        out_specs=[pl.BlockSpec(memory_space=pltpu.VMEM)] * 4,
        scratch_shapes=[
            v(9, 8, 24, 128), v(4, 8, 8, 128), v(2, 16, 32, 64), v(2, 16, 16, 64),
            pltpu.SMEM((2, 16), F32), pltpu.VMEM((1, 16), jnp.int32), pltpu.VMEM((1, 64), jnp.int32),
            v(6, 2, 8, 128), v(6, 2, 8, 128), v(2, 3, 8, 128), v(4, 8, 128),
            v(2, 8, 128), v(2, 8, 128), v(2, 8, 128), v(2, 8, 128), v(2, 8, 128), v(2, 8, 128), v(8, 128),
            v(6, 8, 8, 128), v(2, 16, 8, 128), v(6, 8, 8, 128), v(6, 8, 8, 128), v(16, 16, 64), v(2, 16, 8, 128),
            pltpu.SemaphoreType.DMA((8,)), pltpu.SemaphoreType.DMA((64,)), pltpu.SemaphoreType.DMA((24,)),
        ],
        compiler_params=pltpu.CompilerParams(
            vmem_limit_bytes=16 * 2**20, collective_id=0, has_side_effects=True
        ),
        name="section",
    )(solid_state, material, ocean_state, ocean_medium, offset_x.reshape(1, -1), offset_y.reshape(1, -1))
    return pl.pallas_call(
        write_kernel,
        out_shape=[jax.ShapeDtypeStruct(shape, F32) for shape in outs],
        in_specs=[pl.BlockSpec(memory_space=pltpu.VMEM)] * 4,
        out_specs=[pl.BlockSpec(memory_space=pl.ANY)] * 4,
        scratch_shapes=[pltpu.SemaphoreType.DMA((4,))],
        compiler_params=pltpu.CompilerParams(vmem_limit_bytes=4 * 2**20),
        name="write_out",
    )(*held)


def solution(mesh):
    sizes = (mesh.shape["gx"], mesh.shape["gy"], mesh.shape["gz"])
    solid = P(None, "gz", "gx", "gy")
    ocean = P(None, None, "gx", ("gy", "gz"))
    return jax.shard_map(
        functools.partial(body, sizes),
        mesh=mesh,
        in_specs=(solid, solid, ocean, P(), P("gx"), P(("gy", "gz"))),
        out_specs=(solid, solid, ocean, ocean),
        check_vma=False,
    )
```

```python
import functools

import jax
import jax.numpy as jnp
from jax import lax
from jax.experimental import pallas as pl
from jax.experimental.pallas import tpu as pltpu
from jax.sharding import PartitionSpec as P

closure_rows = (
    (-24.0 / 17.0, 59.0 / 34.0, -4.0 / 17.0, -3.0 / 34.0, 0.0, 0.0),
    (-0.5, 0.0, 0.5, 0.0, 0.0, 0.0),
    (4.0 / 43.0, -59.0 / 86.0, 0.0, 59.0 / 86.0, -4.0 / 43.0, 0.0),
    (3.0 / 98.0, 0.0, -59.0 / 98.0, 0.0, 32.0 / 49.0, -4.0 / 49.0),
)
inner_row = {-2: 1.0 / 12.0, -1: -8.0 / 12.0, 1: 8.0 / 12.0, 2: -1.0 / 12.0}
inv_norm = 48.0 / 17.0
step_size = 0.25
section_weight = 0.1496590219993
gravity = 0.4

MESH = pl.DeviceIdType.MESH
F32 = jnp.float32
HIGHEST = lax.Precision.HIGHEST
REACH = range(-3, 4)

x_fields = (0, 1, 2, 3, 7, 8)
y_fields = (0, 1, 2, 4, 6, 8)
z_fields = (0, 1, 2, 5, 6, 7)


def low_weight(k, d):
    return closure_rows[k][k + d] if 0 <= k + d < 6 else 0.0


def high_weight(k, d):
    return -closure_rows[k][k - d] if 0 <= k - d < 6 else 0.0


def weights(pos, n, first, last, closed):
    at_low = pos + jnp.where(first, 0, 4096)
    at_high = (n - 1) - pos + jnp.where(last, 0, 4096)
    table = {}
    for d in REACH:
        w = jnp.full(pos.shape, inner_row.get(d, 0.0), F32)
        if closed and d < 0:
            w = jnp.where(pos + d >= 0, w, 0.0)
        if closed and d > 0:
            w = jnp.where(pos + d < n, w, 0.0)
        for k in range(4):
            w = jnp.where(at_low == k, low_weight(k, d), w)
            w = jnp.where(at_high == k, high_weight(k, d), w)
        table[d] = w
    return table


def level_weights(level, n, first, last):
    table = {}
    for d in REACH:
        w = inner_row.get(d, 0.0)
        if level < 4 and first is not False:
            c = low_weight(level, d)
            w = c if first is True else (jnp.where(first, c, w) if c != w else w)
        elif level >= n - 4 and last is not False:
            c = high_weight(n - 1 - level, d)
            w = c if last is True else (jnp.where(last, c, w) if c != w else w)
        if not (isinstance(w, float) and w == 0.0):
            table[d] = w
    return table


def total(terms):
    out = None
    for term in terms:
        out = term if out is None else out + term
    return out


def roll_lanes(x, shift):
    return pltpu.roll(x, shift % 128, x.ndim - 1)


def rim_from_sides(left, right, lane, first, last):
    s = lax.rem(lane, 4)
    twelfth = 1.0 / 12.0
    from_left = jnp.where(first, 0.0, twelfth)
    from_right = jnp.where(last, 0.0, twelfth)
    one_left = jnp.where(s >= 2, from_left, 0.0)
    eight_left = jnp.where(s == 2, -8.0 * from_left, 0.0)
    one_right = jnp.where(s < 2, -from_right, 0.0)
    eight_right = jnp.where(s == 1, 8.0 * from_right, 0.0)
    return (
        one_left * roll_lanes(left, 2)
        + eight_left * roll_lanes(left, 1)
        + one_right * roll_lanes(right, -2)
        + eight_right * roll_lanes(right, -1)
    )


def when(pred, action):
    @pl.when(pred)
    def _():
        action()


def start(pred, *copies):
    when(pred, lambda: [copy.start() for copy in copies] and None)


def landed(pred, *copies):
    when(pred, lambda: [copy.wait_recv() for copy in copies] and None)


def sent(pred, *copies):
    when(pred, lambda: [copy.wait_send() for copy in copies] and None)


def section_kernel(
    sizes,
    solid, material, ocean, medium, off_x, off_y,
    s_next, s_rate, o_next, o_rate,
    sb, mb, ob, ov, med, ox, oy,
    z_low, z_high, plane, bed_part,
    ys_out, ys_left, ys_right, yo_out, yo_left, yo_right, coarse_out,
    dys, dyo, dzs, txs, opre, cat,
    local_sem, send_sem, recv_sem,
):
    nx, ny, nz = sizes
    gx, gy, gz = lax.axis_index("gx"), lax.axis_index("gy"), lax.axis_index("gz")
    up_x, down_x = lax.rem(gx + 1, nx), lax.rem(gx + nx - 1, nx)
    up_y, down_y = lax.rem(gy + 1, ny), lax.rem(gy + ny - 1, ny)
    x_first, x_last = gx == 0, gx == nx - 1
    y_first, y_last = gy == 0, gy == ny - 1
    z_first, z_last = gz == 0, gz == nz - 1
    right = (gx, jnp.where(z_last, up_y, gy), jnp.where(z_last, 0, gz + 1))
    left = (gx, jnp.where(z_first, down_y, gy), jnp.where(z_first, nz - 1, gz - 1))
    xs = {-1: down_x, 0: gx, 1: up_x}

    barrier = pltpu.get_barrier_semaphore()

    def greet(x, y, z):
        pl.semaphore_signal(barrier, inc=1, device_id=(x, y, z), device_id_type=MESH)

    x_down, x_up = gx > 0, gx < nx - 1
    y_down, y_up = gy > 0, gy < ny - 1
    z_down, z_up = gz > 0, gz < nz - 1
    has_left, has_right = jnp.logical_or(y_down, z_down), jnp.logical_or(y_up, z_up)
    both = jnp.logical_and
    has = {-1: x_down, 1: x_up}

    when(x_up, lambda: greet(up_x, gy, gz))
    when(x_down, lambda: greet(down_x, gy, gz))
    when(y_up, lambda: greet(gx, up_y, gz))
    when(y_down, lambda: greet(gx, down_y, gz))
    when(has_right, lambda: greet(*right))
    when(has_left, lambda: greet(*left))
    for k in range(2, nz):
        when(z_first, lambda: greet(gx, gy, k))
    when(gz > 1, lambda: greet(gx, gy, 0))
    for e in (-1, 1):
        when(both(has[e], z_down), lambda: greet(xs[e], gy, 0))
        when(both(has[e], both(z_first, y_down)), lambda: greet(xs[e], down_y, 0))
        when(both(has[e], both(z_last, y_up)), lambda: greet(xs[e], up_y, 0))

    loads = [
        pltpu.make_async_copy(src, dst, local_sem.at[i])
        for i, (src, dst) in enumerate(
            (
                (solid, sb.at[:, :, 8:16]),
                (ocean.at[0:2], ob.at[:, :, 8:24]),
                (ocean.at[2:4], ov),
                (material, mb),
                (medium, med),
                (off_x, ox),
                (off_y, oy),
            )
        )
    ]
    for load in loads:
        load.start()

    def clear(*places):
        for ref in places:
            ref[...] = jnp.zeros(ref.shape, F32)

    when(z_first, lambda: clear(z_low))
    when(z_last, lambda: clear(z_high))
    when(x_first, lambda: clear(sb.at[:, :, 6:8], ob.at[:, :, 6:8], plane.at[:, 0]))
    when(x_last, lambda: clear(sb.at[:, :, 16:18], ob.at[:, :, 24:26], plane.at[:, 2]))
    when(y_first, lambda: clear(ys_left))
    when(y_last, lambda: clear(ys_right))
    when(jnp.logical_not(has_left), lambda: clear(yo_left, plane.at[1]))
    when(jnp.logical_not(has_right), lambda: clear(yo_right, plane.at[1]))

    def count(*preds):
        return sum(jnp.where(p, 1, 0) for p in preds)

    n_x, n_y = count(x_down, x_up), count(y_down, y_up)
    n_side = count(has_left, has_right)
    first_extra = (nz - 2) + n_x * (nz - 1 + n_y)
    pl.semaphore_wait(barrier, n_x + n_y + n_side + jnp.where(z_first, first_extra, jnp.where(gz > 1, 1, 0)))

    counter = iter(range(64))

    def remote(src, dst, recv, device):
        return pltpu.make_async_remote_copy(
            src_ref=src, dst_ref=dst, send_sem=send_sem.at[next(counter)], recv_sem=recv_sem.at[recv],
            device_id=device, device_id_type=MESH,
        )

    up_copies, down_copies = [], []
    for i, (a, b) in enumerate(((0, 4), (7, 9))):
        up_copies.append(remote(solid.at[a:b, :, 6:8], sb.at[a:b, :, 6:8], 2 * i, (up_x, gy, gz)))
        down_copies.append(remote(solid.at[a:b, :, 0:2], sb.at[a:b, :, 16:18], 2 * i + 1, (down_x, gy, gz)))
    up_copies.append(remote(ocean.at[0:2, :, 14:16], ob.at[:, :, 6:8], 4, (up_x, gy, gz)))
    down_copies.append(remote(ocean.at[0:2, :, 0:2], ob.at[:, :, 24:26], 5, (down_x, gy, gz)))
    start(x_up, *up_copies)
    start(x_down, *down_copies)

    z_up_copies = [
        remote(solid.at[a : a + 3, 6:8], z_low.at[b : b + 3], 6 + i, (gx, gy, gz + 1))
        for i, (a, b) in enumerate(((0, 0), (5, 3)))
    ]
    z_down_copies = [
        remote(solid.at[a : a + 3, 0:2], z_high.at[b : b + 3], 8 + i, (gx, gy, gz - 1))
        for i, (a, b) in enumerate(((0, 0), (5, 3)))
    ]
    start(z_up, *z_up_copies)
    start(z_down, *z_down_copies)

    tile = solid.at[2, 0]
    plane_copies = []
    for e in (-1, 0, 1):
        x = xs[-e]
        there = z_first if e == 0 else both(z_first, has[-e])
        mine = [remote(tile, plane.at[0, e + 1], 10 + e + 1, (x, gy, k)) for k in range(1 if e == 0 else 0, nz)]
        plane_copies.append((there, mine))
        plane_copies.append((both(there, y_up), [remote(tile, plane.at[1, e + 1], 13 + e + 1, (x, up_y, 0))]))
        plane_copies.append((both(there, y_down), [remote(tile, plane.at[1, e + 1], 13 + e + 1, (x, down_y, nz - 1))]))
    own_plane = pltpu.make_async_copy(tile, plane.at[0, 1], local_sem.at[7])
    when(z_first, own_plane.start)
    for pred, copies in plane_copies:
        start(pred, *copies)

    lane = lax.broadcasted_iota(jnp.int32, (8, 128), 1)

    loads[0].wait()
    for half, fields in enumerate((y_fields[:4], y_fields[4:])):
        packed = jnp.zeros((8, 128), F32)
        for i, f in enumerate(fields):
            for z in range(8):
                k = 8 * i + z
                packed = jnp.where(lane // 4 == k, roll_lanes(sb[f, z, 8:16, :], 4 * k + 2), packed)
        ys_out[half] = packed
    ys_copies = [
        remote(ys_out, ys_left, 16, (gx, up_y, gz)),
        remote(ys_out, ys_right, 17, (gx, down_y, gz)),
    ]
    start(y_up, ys_copies[0])
    start(y_down, ys_copies[1])

    loads[1].wait()
    loads[2].wait()
    half_lane = lax.rem(lane, 64)
    for i in range(2):
        packed = jnp.zeros((8, 128), F32)
        for d in range(16):
            if i == 0:
                folded = jnp.concatenate([ob[0, d, 8:16, :], ob[0, d, 16:24, :]], axis=1)
            else:
                folded = jnp.concatenate([ov[0, d, 0:8, :], ov[0, d, 8:16, :]], axis=1)
            cat[i, d] = folded
            packed = jnp.where(half_lane // 4 == d, roll_lanes(folded, 4 * d + 2), packed)
        yo_out[i] = packed
    yo_copies = [remote(yo_out, yo_left, 18, right), remote(yo_out, yo_right, 19, left)]
    start(has_right, yo_copies[0])
    start(has_left, yo_copies[1])

    row = lax.broadcasted_iota(jnp.int32, (8, 16), 0)
    col = lax.broadcasted_iota(jnp.int32, (8, 16), 1)
    pair = jnp.where(col // 2 == row, 0.5, 0.0)
    fine = lax.broadcasted_iota(jnp.int32, (64, 128), 0)
    out_lane = lax.broadcasted_iota(jnp.int32, (64, 128), 1)
    place = jnp.where(out_lane == 32 * gz + fine // 2, 0.5, 0.0)
    coarse = jnp.dot(pair, ob[0, 15, 8:24, :], precision=HIGHEST, preferred_element_type=F32)
    coarse = jnp.dot(coarse, place, precision=HIGHEST, preferred_element_type=F32)
    coarse_out[...] = coarse
    coarse_copies = [remote(coarse_out, bed_part.at[k], 20 + k, (gx, gy, 0)) for k in range(1, nz)]
    for k in range(1, nz):
        start(gz == k, coarse_copies[k - 1])

    wy = weights(lane, 128, y_first, y_last, True)
    for i, f in enumerate(y_fields):
        own = sb[f, :, 8:16, :]
        dys[i] = total(wy[d] * (roll_lanes(own, -d) if d else own) for d in REACH)
    wo = weights(half_lane, 64, jnp.logical_and(y_first, z_first), jnp.logical_and(y_last, z_last), True)
    for i in range(2):
        for d0 in range(0, 16, 8):
            own = cat[i, d0 : d0 + 8]
            dyo[i, d0 : d0 + 8] = total(wo[d] * (roll_lanes(own, -d) if d else own) for d in REACH)
    sub = lax.broadcasted_iota(jnp.int32, (8, 128), 0)
    wx = weights(sub, 8, x_first, x_last, False)
    for i, f in enumerate(x_fields):
        own = sb[f, :, 8:16, :]
        txs[i] = wx[0] * own + wx[3] * pltpu.roll(own, 5, 1) + wx[-3] * pltpu.roll(own, 3, 1)

    landed(y_down, ys_copies[0])
    landed(y_up, ys_copies[1])
    at_edge = jnp.logical_or(lane < 2, lane >= 126)
    for half, fields in enumerate((y_fields[:4], y_fields[4:])):
        rim = rim_from_sides(ys_left[half], ys_right[half], lane, y_first, y_last)
        for i in range(len(fields)):
            for z in range(8):
                k = 8 * i + z
                dys[4 * half + i, z] += jnp.where(at_edge, roll_lanes(rim, -4 * k - 2), 0.0)
    landed(has_left, yo_copies[0])
    landed(has_right, yo_copies[1])
    at_half_edge = jnp.logical_or(half_lane < 2, half_lane >= 62)
    for i in range(2):
        rim = rim_from_sides(
            roll_lanes(yo_left[i], 64), roll_lanes(yo_right[i], 64), lane,
            jnp.logical_and(y_first, z_first), jnp.logical_and(y_last, z_last),
        )
        for d in range(16):
            dyo[i, d] += jnp.where(at_half_edge, roll_lanes(rim, -4 * d - 2), 0.0)

    loads[3].wait()

    landed(z_down, *z_up_copies)
    landed(z_up, *z_down_copies)

    for i, f in enumerate(z_fields):
        def level(z, i=i, f=f):
            if z < 0:
                return z_low[i, z + 2]
            if z >= 8:
                return z_high[i, z - 8]
            return sb[f, z, 8:16, :]

        for z in range(8):
            table = level_weights(z, 8, z_first, z_last)
            dzs[i, z] = mb[3, z] * total(w * level(z + d) for d, w in table.items() if -2 <= z + d < 10)

    @pl.when(z_first)
    def _():
        for k in range(1, nz):
            pltpu.make_async_remote_copy(
                src_ref=coarse_out, dst_ref=bed_part.at[k], send_sem=send_sem.at[63], recv_sem=recv_sem.at[20 + k],
                device_id=(gx, up_y, gz), device_id_type=MESH,
            ).wait_recv()
        scale = inv_norm * mb[3, 0]
        bed_pressure = coarse_out[...] + total(bed_part[k] for k in range(1, nz))
        dzs[5, 0] += scale * sb[7, 0, 8:16, :]
        dzs[4, 0] += scale * sb[6, 0, 8:16, :]
        dzs[3, 0] += scale * (sb[5, 0, 8:16, :] + bed_pressure)

    loads[5].wait()
    loads[6].wait()

    def plane_wait(s, e):
        pltpu.make_async_remote_copy(
            src_ref=tile, dst_ref=plane.at[s, e + 1], send_sem=send_sem.at[63], recv_sem=recv_sem.at[10 + 3 * s + e + 1],
            device_id=(gx, up_y, gz), device_id_type=MESH,
        ).wait_recv()

    when(z_first, own_plane.wait)
    when(z_down, lambda: plane_wait(0, 0))
    for e in (-1, 1):
        when(has[e], lambda: plane_wait(0, e))
    for pred, at in ((both(z_first, y_down), 127), (both(z_last, y_up), 0)):
        when(pred, lambda: plane_wait(1, 0))
        for e in (-1, 1):
            when(both(pred, has[e]), lambda: plane_wait(1, e))

        @pl.when(pred)
        def _(at=at):
            for e in range(3):
                plane[0, e] = jnp.where(lane == at, plane[1, e], plane[0, e])

    window = plane[0].reshape(24, 128)
    fine_x = lax.broadcasted_iota(jnp.int32, (24, 16), 1)
    coarse_x = lax.broadcasted_iota(jnp.int32, (24, 16), 0) + (8 * gx - 8)
    near_x = 8 * gx + fine_x // 2
    far_x = jnp.clip(near_x + ox[...], 0, 8 * nx - 1)
    blend_x = jnp.where(coarse_x == near_x, 0.75, 0.0) + jnp.where(coarse_x == far_x, 0.25, 0.0)
    fine_y = lax.broadcasted_iota(jnp.int32, (128, 64), 1)
    coarse_y = lax.broadcasted_iota(jnp.int32, (128, 64), 0)
    near_y = 128 * gy + 32 * gz + fine_y // 2
    far_y = jnp.clip(near_y + oy[...], 0, 128 * ny - 1)
    blend_y = jnp.where(coarse_y == lax.rem(near_y, 128), 0.75, 0.0)
    blend_y = blend_y + jnp.where(coarse_y == lax.rem(far_y, 128), 0.25, 0.0)
    bed_speed = lax.dot_general(
        blend_x, window, (((0,), (0,)), ((), ())), precision=HIGHEST, preferred_element_type=F32
    )
    bed_speed = jnp.dot(bed_speed, blend_y, precision=HIGHEST, preferred_element_type=F32)

    loads[4].wait()

    def unfold(i, d):
        folded = dyo[i, d]
        return jnp.concatenate([folded[:, 0:64], folded[:, 64:128]], axis=0)

    for d in range(16):
        bulk = jnp.full((16, 64), med[0, d], F32)
        light = jnp.full((16, 64), med[1, d], F32)
        pressure, flow_v, flow_w = ob[0, d, 8:24, :], ov[0, d], ov[1, d]
        table = level_weights(d, 16, True, True)
        dz_w = total(w * ov[1, d + k] for k, w in table.items())
        dz_p = total(w * ob[0, d + k, 8:24, :] for k, w in table.items())
        part = -bulk * (2.0 * unfold(1, d) + dz_w) + gravity * flow_w / light
        if d == 15:
            part = part + inv_norm * bulk * (flow_w - bed_speed)
        opre[d] = step_size * part
        rate_v = (-2.0 * step_size) * light * unfold(0, d)
        rate_w = -light * dz_p
        if d == 0:
            rate_w = rate_w - inv_norm * light * pressure
        rate_w = step_size * rate_w
        o_rate[2, d] = rate_v
        o_rate[3, d] = rate_w
        o_next[2, d] = flow_v + section_weight * rate_v
        o_next[3, d] = flow_w + section_weight * rate_w

    landed(x_down, *up_copies)
    landed(x_up, *down_copies)

    def dx(i, f, z):
        out = txs[i, z]
        for d in (-2, -1, 1, 2):
            out = out + wx[d] * sb[f, z, 8 + d : 16 + d, :]
        return out

    for z in range(8):
        own = [sb[f, z, 8:16, :] for f in range(9)]
        b, lam, mu = step_size * mb[0, z], step_size * mb[1, z], step_size * mb[2, z]
        d_x = {f: dx(i, f, z) for i, f in enumerate(x_fields)}
        d_y = {f: dys[i, z] for i, f in enumerate(y_fields)}
        d_z = {f: dzs[i, z] for i, f in enumerate(z_fields)}
        dilation = lam * (d_x[0] + d_y[1] + d_z[2])
        mu2 = 2.0 * mu
        rates = [
            b * (d_x[3] + d_y[8] + d_z[7]),
            b * (d_x[8] + d_y[4] + d_z[6]),
            b * (d_x[7] + d_y[6] + d_z[5]),
            dilation + mu2 * d_x[0],
            dilation + mu2 * d_y[1],
            dilation + mu2 * d_z[2],
            mu * (d_z[1] + d_y[2]),
            mu * (d_z[0] + d_x[2]),
            mu * (d_y[0] + d_x[1]),
        ]
        for f in range(9):
            s_rate[f, z] = rates[f]
            s_next[f, z] = own[f] + section_weight * rates[f]

    pos = lax.broadcasted_iota(jnp.int32, (16, 64), 0)
    wp = weights(pos, 16, x_first, x_last, False)
    far_up, far_down = wp[3] != 0.0, wp[-3] != 0.0

    def dx_ocean(i, d):
        out = total(wp[k] * ob[i, d, 8 + k : 24 + k, :] for k in range(-2, 3))
        out = out + wp[3] * jnp.where(far_up, ob[i, d, 11:27, :], 0.0)
        return out + wp[-3] * jnp.where(far_down, ob[i, d, 5:21, :], 0.0)

    for d in range(16):
        bulk = jnp.full((16, 64), (-2.0 * step_size) * med[0, d], F32)
        light = jnp.full((16, 64), (-2.0 * step_size) * med[1, d], F32)
        rate_p = opre[d] + bulk * dx_ocean(1, d)
        rate_u = light * dx_ocean(0, d)
        o_rate[0, d] = rate_p
        o_rate[1, d] = rate_u
        o_next[0, d] = ob[0, d, 8:24, :] + section_weight * rate_p
        o_next[1, d] = ob[1, d, 8:24, :] + section_weight * rate_u

    sent(x_up, *up_copies)
    sent(x_down, *down_copies)
    sent(y_up, ys_copies[0])
    sent(y_down, ys_copies[1])
    sent(has_right, yo_copies[0])
    sent(has_left, yo_copies[1])
    sent(z_up, *z_up_copies)
    sent(z_down, *z_down_copies)
    for pred, copies in plane_copies:
        sent(pred, *copies)
    for k in range(1, nz):
        sent(gz == k, coarse_copies[k - 1])


def write_kernel(*refs):
    count = (len(refs) - 1) // 2
    sem = refs[-1]
    copies = [pltpu.make_async_copy(refs[i], refs[count + i], sem.at[i]) for i in range(count)]
    for copy in copies:
        copy.start()
    for copy in copies:
        copy.wait()


def body(sizes, solid_state, material, ocean_state, ocean_medium, offset_x, offset_y):
    outs = (solid_state.shape, solid_state.shape, ocean_state.shape, ocean_state.shape)
    v = lambda *shape: pltpu.VMEM(shape, F32)
    held = pl.pallas_call(
        functools.partial(section_kernel, sizes),
        out_shape=[pltpu.VMEM(shape, F32) for shape in outs],
        in_specs=[pl.BlockSpec(memory_space=pltpu.HBM)] * 6,
        out_specs=[pl.BlockSpec(memory_space=pltpu.VMEM)] * 4,
        scratch_shapes=[
            v(9, 8, 24, 128), v(4, 8, 8, 128), v(2, 16, 32, 64), v(2, 16, 16, 64),
            pltpu.SMEM((2, 16), F32), pltpu.VMEM((1, 16), jnp.int32), pltpu.VMEM((1, 64), jnp.int32),
            v(6, 2, 8, 128), v(6, 2, 8, 128), v(2, 3, 8, 128), v(4, 8, 128),
            v(2, 8, 128), v(2, 8, 128), v(2, 8, 128), v(2, 8, 128), v(2, 8, 128), v(2, 8, 128), v(8, 128),
            v(6, 8, 8, 128), v(2, 16, 8, 128), v(6, 8, 8, 128), v(6, 8, 8, 128), v(16, 16, 64), v(2, 16, 8, 128),
            pltpu.SemaphoreType.DMA((8,)), pltpu.SemaphoreType.DMA((64,)), pltpu.SemaphoreType.DMA((24,)),
        ],
        compiler_params=pltpu.CompilerParams(
            vmem_limit_bytes=16 * 2**20, collective_id=0, has_side_effects=True
        ),
        name="section",
    )(*(
        pltpu.with_memory_space_constraint(a, pltpu.HBM)
        for a in (solid_state, material, ocean_state, ocean_medium, offset_x.reshape(1, -1), offset_y.reshape(1, -1))
    ))
    return pl.pallas_call(
        write_kernel,
        out_shape=[jax.ShapeDtypeStruct(shape, F32) for shape in outs],
        in_specs=[pl.BlockSpec(memory_space=pltpu.VMEM)] * 4,
        out_specs=[pl.BlockSpec(memory_space=pl.ANY)] * 4,
        scratch_shapes=[pltpu.SemaphoreType.DMA((4,))],
        compiler_params=pltpu.CompilerParams(vmem_limit_bytes=4 * 2**20),
        name="write_out",
    )(*held)


def solution(mesh):
    sizes = (mesh.shape["gx"], mesh.shape["gy"], mesh.shape["gz"])
    solid = P(None, "gz", "gx", "gy")
    ocean = P(None, None, "gx", ("gy", "gz"))
    return jax.shard_map(
        functools.partial(body, sizes),
        mesh=mesh,
        in_specs=(solid, solid, ocean, P(), P("gx"), P(("gy", "gz"))),
        out_specs=(solid, solid, ocean, ocean),
        check_vma=False,
    )
```

```python
import functools

import jax
import jax.numpy as jnp
from jax import lax
from jax.experimental import pallas as pl
from jax.experimental.pallas import tpu as pltpu
from jax.sharding import PartitionSpec as P

closure_rows = (
    (-24.0 / 17.0, 59.0 / 34.0, -4.0 / 17.0, -3.0 / 34.0, 0.0, 0.0),
    (-0.5, 0.0, 0.5, 0.0, 0.0, 0.0),
    (4.0 / 43.0, -59.0 / 86.0, 0.0, 59.0 / 86.0, -4.0 / 43.0, 0.0),
    (3.0 / 98.0, 0.0, -59.0 / 98.0, 0.0, 32.0 / 49.0, -4.0 / 49.0),
)
inner_row = {-2: 1.0 / 12.0, -1: -8.0 / 12.0, 1: 8.0 / 12.0, 2: -1.0 / 12.0}
inv_norm = 48.0 / 17.0
step_size = 0.25
section_weight = 0.1496590219993
gravity = 0.4

MESH = pl.DeviceIdType.MESH
F32 = jnp.float32
HIGHEST = lax.Precision.HIGHEST
REACH = range(-3, 4)

x_fields = (0, 1, 2, 3, 7, 8)
y_fields = (0, 1, 2, 4, 6, 8)
z_fields = (0, 1, 2, 5, 6, 7)


def low_weight(k, d):
    return closure_rows[k][k + d] if 0 <= k + d < 6 else 0.0


def high_weight(k, d):
    return -closure_rows[k][k - d] if 0 <= k - d < 6 else 0.0


def weights(pos, n, first, last, closed):
    at_low = pos + jnp.where(first, 0, 4096)
    at_high = (n - 1) - pos + jnp.where(last, 0, 4096)
    table = {}
    for d in REACH:
        w = jnp.full(pos.shape, inner_row.get(d, 0.0), F32)
        if closed and d < 0:
            w = jnp.where(pos + d >= 0, w, 0.0)
        if closed and d > 0:
            w = jnp.where(pos + d < n, w, 0.0)
        for k in range(4):
            w = jnp.where(at_low == k, low_weight(k, d), w)
            w = jnp.where(at_high == k, high_weight(k, d), w)
        table[d] = w
    return table


def level_weights(level, n, first, last):
    table = {}
    for d in REACH:
        w = inner_row.get(d, 0.0)
        if level < 4 and first is not False:
            c = low_weight(level, d)
            w = c if first is True else (jnp.where(first, c, w) if c != w else w)
        elif level >= n - 4 and last is not False:
            c = high_weight(n - 1 - level, d)
            w = c if last is True else (jnp.where(last, c, w) if c != w else w)
        if not (isinstance(w, float) and w == 0.0):
            table[d] = w
    return table


def total(terms):
    out = None
    for term in terms:
        out = term if out is None else out + term
    return out


def roll_lanes(x, shift):
    return pltpu.roll(x, shift % 128, x.ndim - 1)


def rim_from_sides(left, right, lane, first, last):
    s = lax.rem(lane, 4)
    twelfth = 1.0 / 12.0
    from_left = jnp.where(first, 0.0, twelfth)
    from_right = jnp.where(last, 0.0, twelfth)
    one_left = jnp.where(s >= 2, from_left, 0.0)
    eight_left = jnp.where(s == 2, -8.0 * from_left, 0.0)
    one_right = jnp.where(s < 2, -from_right, 0.0)
    eight_right = jnp.where(s == 1, 8.0 * from_right, 0.0)
    return (
        one_left * roll_lanes(left, 2)
        + eight_left * roll_lanes(left, 1)
        + one_right * roll_lanes(right, -2)
        + eight_right * roll_lanes(right, -1)
    )


def when(pred, action):
    @pl.when(pred)
    def _():
        action()


def start(pred, *copies):
    when(pred, lambda: [copy.start() for copy in copies] and None)


def landed(pred, *copies):
    when(pred, lambda: [copy.wait_recv() for copy in copies] and None)


def sent(pred, *copies):
    when(pred, lambda: [copy.wait_send() for copy in copies] and None)


def both(a, b):
    return jnp.logical_and(a, b)


def section_kernel(
    sizes,
    solid, material, ocean, medium, off_x, off_y,
    s_next, s_rate, o_next, o_rate,
    sb, mb, ob, ov, med, ox, oy,
    z_low, z_high, plane, bed_part,
    xo_out, xo_low, xo_high, ys_out, ys_left, ys_right, yo_out, yo_left, yo_right, coarse_out,
    dys, dyo, dzs, txs, opre, cat,
    local_sem, send_sem, recv_sem, there,
):
    nx, ny, nz = sizes
    gx, gy, gz = lax.axis_index("gx"), lax.axis_index("gy"), lax.axis_index("gz")
    up_x, down_x = lax.rem(gx + 1, nx), lax.rem(gx + nx - 1, nx)
    up_y, down_y = lax.rem(gy + 1, ny), lax.rem(gy + ny - 1, ny)
    x_first, x_last = gx == 0, gx == nx - 1
    y_first, y_last = gy == 0, gy == ny - 1
    z_first, z_last = gz == 0, gz == nz - 1
    right = (gx, jnp.where(z_last, up_y, gy), jnp.where(z_last, 0, gz + 1))
    left = (gx, jnp.where(z_first, down_y, gy), jnp.where(z_first, nz - 1, gz - 1))
    xs = {-1: down_x, 0: gx, 1: up_x}

    x_down, x_up = gx > 0, gx < nx - 1
    y_down, y_up = gy > 0, gy < ny - 1
    z_down, z_up = gz > 0, gz < nz - 1
    has_left, has_right = jnp.logical_or(y_down, z_down), jnp.logical_or(y_up, z_up)
    has = {-1: x_down, 1: x_up}

    run = max(nx // 4, 2)
    turn = lax.rem(gx, run)
    late = {1: turn < run // 2, -1: jnp.logical_or(turn == 0, turn > run // 2)}
    has_late = {e: both(has[e], late[e]) for e in (-1, 1)}
    has_early = {e: both(has[e], jnp.logical_not(late[e])) for e in (-1, 1)}
    odd = lax.rem(gz, 2) == 1
    even = jnp.logical_not(odd)
    barrier = pltpu.get_barrier_semaphore()

    def greet(x, y, z):
        pl.semaphore_signal(barrier, inc=1, device_id=(x, y, z), device_id_type=MESH)

    def tell(index, x, y, z):
        pl.semaphore_signal(there.at[index], inc=1, device_id=(x, y, z), device_id_type=MESH)

    plane[...] = jnp.zeros_like(plane)
    for e in (-1, 1):
        when(has_late[e], lambda: greet(xs[e], gy, gz))
    when(y_up, lambda: greet(gx, up_y, gz))
    when(odd, lambda: greet(gx, gy, gz - 1))
    when(gz < 2, lambda: greet(gx, gy, 2))
    for e in (-1, 1):
        when(both(has_late[e], z_down), lambda: greet(xs[e], gy, 0))
        when(both(has_late[e], both(z_first, y_down)), lambda: greet(xs[e], down_y, 0))
        when(both(has_late[e], both(z_last, y_up)), lambda: greet(xs[e], up_y, 0))

    loads = [
        pltpu.make_async_copy(src, dst, local_sem.at[i])
        for i, (src, dst) in enumerate(
            (
                (solid, sb.at[:, :, 8:16]),
                (ocean.at[0:2], ob.at[:, :, 8:24]),
                (ocean.at[2:4], ov),
                (material, mb),
                (medium, med),
                (off_x, ox),
                (off_y, oy),
            )
        )
    ]
    for load in loads:
        load.start()

    def clear(*places):
        for ref in places:
            ref[...] = jnp.zeros(ref.shape, F32)

    when(z_first, lambda: clear(z_low))
    when(z_last, lambda: clear(z_high))
    when(x_first, lambda: clear(sb.at[:, :, 6:8], xo_low))
    when(x_last, lambda: clear(sb.at[:, :, 16:18], xo_high))
    when(y_first, lambda: clear(ys_left))
    when(y_last, lambda: clear(ys_right))
    when(jnp.logical_not(has_left), lambda: clear(yo_left))
    when(jnp.logical_not(has_right), lambda: clear(yo_right))

    def count(*preds):
        return sum(jnp.where(p, 1, 0) for p in preds)

    n_early = count(*has_early.values())
    n_y = count(y_down, y_up)
    n_greet = count(y_down, even) + jnp.where(gz == 2, 2, 0)
    n_greet = n_greet + n_early * (1 + jnp.where(z_first, nz - 1 + n_y, 0))
    when(n_greet > 0, lambda: pl.semaphore_wait(barrier, n_greet))
    for e, index in ((1, 1), (-1, 0)):
        when(has_early[e], lambda: tell(index, xs[e], gy, gz))
    when(y_down, lambda: tell(2, gx, down_y, gz))
    when(gz == 2, lambda: tell(3, gx, gy, 1))
    when(even, lambda: tell(4, gx, gy, gz + 1))
    when(gz == 2, lambda: tell(5, gx, gy, 0))
    def await_partner(pred, index, amount=1):
        when(pred, lambda: pl.semaphore_wait(there.at[index], amount))

    counter = iter(range(64))

    def remote(src, dst, recv, device):
        return pltpu.make_async_remote_copy(
            src_ref=src, dst_ref=dst, send_sem=send_sem.at[next(counter)], recv_sem=recv_sem.at[recv],
            device_id=device, device_id_type=MESH,
        )

    up_copies, down_copies = [], []
    for i, (a, b) in enumerate(((0, 4), (7, 9))):
        up_copies.append(remote(solid.at[a:b, :, 6:8], sb.at[a:b, :, 6:8], 2 * i, (up_x, gy, gz)))
        down_copies.append(remote(solid.at[a:b, :, 0:2], sb.at[a:b, :, 16:18], 2 * i + 1, (down_x, gy, gz)))
    wave_up = remote(xo_out.at[1], xo_low, 4, (up_x, gy, gz))
    wave_down = remote(xo_out.at[0], xo_high, 5, (down_x, gy, gz))
    start(has_early[1], *up_copies)
    start(has_early[-1], *down_copies)

    z_up_copies = [
        remote(solid.at[a : a + 3, 6:8], z_low.at[b : b + 3], 6 + i, (gx, gy, gz + 1))
        for i, (a, b) in enumerate(((0, 0), (5, 3)))
    ]
    z_down_copies = [
        remote(solid.at[a : a + 3, 0:2], z_high.at[b : b + 3], 8 + i, (gx, gy, gz - 1))
        for i, (a, b) in enumerate(((0, 0), (5, 3)))
    ]

    tile = solid.at[2, 0]
    plane_early, plane_late = [], []
    rows = {-1: slice(7, 8), 0: slice(0, 8), 1: slice(0, 1)}
    for e in (-1, 0, 1):
        x, r = xs[-e], rows[e]
        part = solid.at[2, 0, r]
        mine = [remote(part, plane.at[0, e + 1, r], 10 + e + 1, (x, gy, k)) for k in range(1 if e == 0 else 0, nz)]
        above = remote(part, plane.at[1, e + 1, r], 13 + e + 1, (x, up_y, 0))
        below = remote(part, plane.at[1, e + 1, r], 13 + e + 1, (x, down_y, nz - 1))
        if e == 0:
            plane_early += [(z_first, mine[:1])]
            plane_late += [(z_first, mine[1:]), (both(z_first, y_up), [above]), (both(z_first, y_down), [below])]
        else:
            pred = both(z_first, has_early[-e])
            plane_early += [(pred, mine), (both(pred, y_up), [above]), (both(pred, y_down), [below])]
    plane_on = {
        e: remote(plane.at[0, 1, rows[-e]], plane.at[0, 1 - e, rows[-e]], 11 - e, (xs[e], gy, gz)) for e in (-1, 1)
    }
    own_plane = pltpu.make_async_copy(tile, plane.at[0, 1], local_sem.at[7])
    when(z_first, own_plane.start)
    for pred, copies in plane_early:
        start(pred, *copies)

    lane = lax.broadcasted_iota(jnp.int32, (8, 128), 1)

    loads[1].wait()
    for end, row in ((0, 8), (1, 22)):
        xo_out[end] = jnp.concatenate([ob[0, :, row : row + 2, :], ob[1, :, row : row + 2, :]], axis=2)
    start(has_early[1], wave_up)
    start(has_early[-1], wave_down)

    loads[0].wait()
    for half, fields in enumerate((y_fields[:4], y_fields[4:])):
        packed = jnp.zeros((8, 128), F32)
        for i, f in enumerate(fields):
            for z in range(8):
                k = 8 * i + z
                packed = jnp.where(lane // 4 == k, roll_lanes(sb[f, z, 8:16, :], 4 * k + 2), packed)
        ys_out[half] = packed
    ys_copies = [
        remote(ys_out, ys_left, 16, (gx, up_y, gz)),
        remote(ys_out, ys_right, 17, (gx, down_y, gz)),
    ]
    start(y_down, ys_copies[1])

    loads[2].wait()
    half_lane = lax.rem(lane, 64)
    for i in range(2):
        packed = jnp.zeros((8, 128), F32)
        for d in range(16):
            if i == 0:
                folded = jnp.concatenate([ob[0, d, 8:16, :], ob[0, d, 16:24, :]], axis=1)
            else:
                folded = jnp.concatenate([ov[0, d, 0:8, :], ov[0, d, 8:16, :]], axis=1)
            cat[i, d] = folded
            packed = jnp.where(half_lane // 4 == d, roll_lanes(folded, 4 * d + 2), packed)
        yo_out[i] = packed
    yo_copies = [remote(yo_out, yo_left, 18, right), remote(yo_out, yo_right, 19, left)]
    start(both(even, has_right), yo_copies[0])
    start(gz == 2, yo_copies[1])

    row = lax.broadcasted_iota(jnp.int32, (8, 16), 0)
    col = lax.broadcasted_iota(jnp.int32, (8, 16), 1)
    pair = jnp.where(col // 2 == row, 0.5, 0.0)
    fine = lax.broadcasted_iota(jnp.int32, (64, 128), 0)
    out_lane = lax.broadcasted_iota(jnp.int32, (64, 128), 1)
    place = jnp.where(out_lane == 32 * gz + fine // 2, 0.5, 0.0)
    coarse = jnp.dot(pair, ob[0, 15, 8:24, :], precision=HIGHEST, preferred_element_type=F32)
    coarse = jnp.dot(coarse, place, precision=HIGHEST, preferred_element_type=F32)
    coarse_out[...] = coarse
    coarse_copies = [remote(coarse_out, bed_part.at[k], 20 + k, (gx, gy, 0)) for k in range(1, nz)]
    start(gz == 2, coarse_copies[1])

    wy = weights(lane, 128, y_first, y_last, True)
    for i, f in enumerate(y_fields):
        own = sb[f, :, 8:16, :]
        dys[i] = total(wy[d] * (roll_lanes(own, -d) if d else own) for d in REACH)
    wo = weights(half_lane, 64, jnp.logical_and(y_first, z_first), jnp.logical_and(y_last, z_last), True)
    for i in range(2):
        for d0 in range(0, 16, 8):
            own = cat[i, d0 : d0 + 8]
            dyo[i, d0 : d0 + 8] = total(wo[d] * (roll_lanes(own, -d) if d else own) for d in REACH)
    sub = lax.broadcasted_iota(jnp.int32, (8, 128), 0)
    wx = weights(sub, 8, x_first, x_last, False)
    for i, f in enumerate(x_fields):
        own = sb[f, :, 8:16, :]
        txs[i] = wx[0] * own + wx[3] * pltpu.roll(own, 5, 1) + wx[-3] * pltpu.roll(own, 3, 1)

    start(even, *z_up_copies)
    start(gz == 2, *z_down_copies)
    await_partner(odd, 4)
    start(odd, *z_down_copies, yo_copies[1])
    for k in (1, 3):
        start(gz == k, coarse_copies[k - 1])
    await_partner(gz == 1, 3)
    start(gz == 1, *z_up_copies, yo_copies[0])
    await_partner(z_first, 5)
    start(*plane_late[0][:1], *plane_late[0][1])
    await_partner(y_up, 2)
    start(y_up, ys_copies[0])
    when(both(z_first, y_up), lambda: tell(7, gx, gy, nz - 1))
    when(both(z_first, y_up), lambda: tell(6, gx, up_y, 0))
    start(*plane_late[1][:1], *plane_late[1][1])
    await_partner(both(z_first, y_down), 6)
    start(both(z_first, y_down), yo_copies[1], *plane_late[2][1])
    await_partner(both(z_last, y_up), 7)
    start(both(z_last, y_up), yo_copies[0])
    for e, index, copies in ((1, 0, up_copies + [wave_up]), (-1, 1, down_copies + [wave_down])):
        await_partner(has_late[e], index)
        start(has_late[e], *copies)
    sides = ((both(z_first, y_down), 127), (both(z_last, y_up), 0))

    def plane_wait(s, e):
        pltpu.make_async_remote_copy(
            src_ref=solid.at[2, 0, rows[e]], dst_ref=plane.at[s, e + 1, rows[e]], send_sem=send_sem.at[63], recv_sem=recv_sem.at[10 + 3 * s + e + 1],
            device_id=(gx, up_y, gz), device_id_type=MESH,
        ).wait_recv()

    def merge(e):
        for pred, at in sides:

            @pl.when(pred)
            def _(at=at):
                plane_wait(1, e)
                plane[0, e + 1] = jnp.where(lane == at, plane[1, e + 1], plane[0, e + 1])

    when(z_first, own_plane.wait)
    when(z_down, lambda: plane_wait(0, 0))
    merge(0)
    for e in (-1, 1):
        start(has_late[e], plane_on[e])

    landed(y_down, ys_copies[0])
    landed(y_up, ys_copies[1])
    at_edge = jnp.logical_or(lane < 2, lane >= 126)
    for half, fields in enumerate((y_fields[:4], y_fields[4:])):
        rim = rim_from_sides(ys_left[half], ys_right[half], lane, y_first, y_last)
        for i in range(len(fields)):
            for z in range(8):
                k = 8 * i + z
                dys[4 * half + i, z] += jnp.where(at_edge, roll_lanes(rim, -4 * k - 2), 0.0)
    landed(has_left, yo_copies[0])
    landed(has_right, yo_copies[1])
    at_half_edge = jnp.logical_or(half_lane < 2, half_lane >= 62)
    for i in range(2):
        rim = rim_from_sides(
            roll_lanes(yo_left[i], 64), roll_lanes(yo_right[i], 64), lane,
            jnp.logical_and(y_first, z_first), jnp.logical_and(y_last, z_last),
        )
        for d in range(16):
            dyo[i, d] += jnp.where(at_half_edge, roll_lanes(rim, -4 * d - 2), 0.0)

    loads[3].wait()

    landed(z_down, *z_up_copies)
    landed(z_up, *z_down_copies)

    for i, f in enumerate(z_fields):
        def level(z, i=i, f=f):
            if z < 0:
                return z_low[i, z + 2]
            if z >= 8:
                return z_high[i, z - 8]
            return sb[f, z, 8:16, :]

        for z in range(8):
            table = level_weights(z, 8, z_first, z_last)
            dzs[i, z] = mb[3, z] * total(w * level(z + d) for d, w in table.items() if -2 <= z + d < 10)

    @pl.when(z_first)
    def _():
        for k in range(1, nz):
            pltpu.make_async_remote_copy(
                src_ref=coarse_out, dst_ref=bed_part.at[k], send_sem=send_sem.at[63], recv_sem=recv_sem.at[20 + k],
                device_id=(gx, up_y, gz), device_id_type=MESH,
            ).wait_recv()
        scale = inv_norm * mb[3, 0]
        bed_pressure = coarse_out[...] + total(bed_part[k] for k in range(1, nz))
        dzs[5, 0] += scale * sb[7, 0, 8:16, :]
        dzs[4, 0] += scale * sb[6, 0, 8:16, :]
        dzs[3, 0] += scale * (sb[5, 0, 8:16, :] + bed_pressure)

    loads[4].wait()

    def unfold(i, d):
        folded = dyo[i, d]
        return jnp.concatenate([folded[:, 0:64], folded[:, 64:128]], axis=0)

    for d in range(16):
        bulk = jnp.full((16, 64), med[0, d], F32)
        light = jnp.full((16, 64), med[1, d], F32)
        pressure, flow_v, flow_w = ob[0, d, 8:24, :], ov[0, d], ov[1, d]
        table = level_weights(d, 16, True, True)
        dz_w = total(w * ov[1, d + k] for k, w in table.items())
        dz_p = total(w * ob[0, d + k, 8:24, :] for k, w in table.items())
        part = -bulk * (2.0 * unfold(1, d) + dz_w) + gravity * flow_w / light
        opre[d] = step_size * part
        rate_v = (-2.0 * step_size) * light * unfold(0, d)
        rate_w = -light * dz_p
        if d == 0:
            rate_w = rate_w - inv_norm * light * pressure
        rate_w = step_size * rate_w
        o_rate[2, d] = rate_v
        o_rate[3, d] = rate_w
        o_next[2, d] = flow_v + section_weight * rate_v
        o_next[3, d] = flow_w + section_weight * rate_w

    landed(x_down, *up_copies, wave_up)
    landed(x_up, *down_copies, wave_down)
    for rim, row in ((xo_low, 6), (xo_high, 24)):
        for i in range(2):
            ob[i, :, row : row + 2, :] = rim[:, :, 64 * i : 64 * i + 64]

    def dx(i, f, z):
        out = txs[i, z]
        for d in (-2, -1, 1, 2):
            out = out + wx[d] * sb[f, z, 8 + d : 16 + d, :]
        return out

    for z in range(8):
        own = [sb[f, z, 8:16, :] for f in range(9)]
        b, lam, mu = step_size * mb[0, z], step_size * mb[1, z], step_size * mb[2, z]
        d_x = {f: dx(i, f, z) for i, f in enumerate(x_fields)}
        d_y = {f: dys[i, z] for i, f in enumerate(y_fields)}
        d_z = {f: dzs[i, z] for i, f in enumerate(z_fields)}
        dilation = lam * (d_x[0] + d_y[1] + d_z[2])
        mu2 = 2.0 * mu
        rates = [
            b * (d_x[3] + d_y[8] + d_z[7]),
            b * (d_x[8] + d_y[4] + d_z[6]),
            b * (d_x[7] + d_y[6] + d_z[5]),
            dilation + mu2 * d_x[0],
            dilation + mu2 * d_y[1],
            dilation + mu2 * d_z[2],
            mu * (d_z[1] + d_y[2]),
            mu * (d_z[0] + d_x[2]),
            mu * (d_y[0] + d_x[1]),
        ]
        for f in range(9):
            s_rate[f, z] = rates[f]
            s_next[f, z] = own[f] + section_weight * rates[f]

    pos = lax.broadcasted_iota(jnp.int32, (16, 64), 0)
    wp = weights(pos, 16, x_first, x_last, False)
    far_up, far_down = wp[3] != 0.0, wp[-3] != 0.0

    def dx_ocean(i, d):
        out = total(wp[k] * ob[i, d, 8 + k : 24 + k, :] for k in range(-2, 3))
        out = out + wp[3] * jnp.where(far_up, ob[i, d, 11:27, :], 0.0)
        return out + wp[-3] * jnp.where(far_down, ob[i, d, 5:21, :], 0.0)

    def ocean_out(i, d, rate):
        o_rate[i, d] = rate
        o_next[i, d] = ob[i, d, 8:24, :] + section_weight * rate

    for d in range(16):
        bulk = jnp.full((16, 64), (-2.0 * step_size) * med[0, d], F32)
        light = jnp.full((16, 64), (-2.0 * step_size) * med[1, d], F32)
        rate_p = opre[d] + bulk * dx_ocean(1, d)
        ocean_out(1, d, light * dx_ocean(0, d))
        if d < 15:
            ocean_out(0, d, rate_p)

    loads[5].wait()
    loads[6].wait()
    for e in (-1, 1):
        when(has[e], lambda: plane_wait(0, e))
        when(has_late[e], lambda: merge(e))

    window = plane[0].reshape(24, 128)
    fine_x = lax.broadcasted_iota(jnp.int32, (24, 16), 1)
    coarse_x = lax.broadcasted_iota(jnp.int32, (24, 16), 0) + (8 * gx - 8)
    near_x = 8 * gx + fine_x // 2
    far_x = jnp.clip(near_x + ox[...], 0, 8 * nx - 1)
    blend_x = jnp.where(coarse_x == near_x, 0.75, 0.0) + jnp.where(coarse_x == far_x, 0.25, 0.0)
    fine_y = lax.broadcasted_iota(jnp.int32, (128, 64), 1)
    coarse_y = lax.broadcasted_iota(jnp.int32, (128, 64), 0)
    near_y = 128 * gy + 32 * gz + fine_y // 2
    far_y = jnp.clip(near_y + oy[...], 0, 128 * ny - 1)
    blend_y = jnp.where(coarse_y == lax.rem(near_y, 128), 0.75, 0.0)
    blend_y = blend_y + jnp.where(coarse_y == lax.rem(far_y, 128), 0.25, 0.0)
    bed_speed = lax.dot_general(
        blend_x, window, (((0,), (0,)), ((), ())), precision=HIGHEST, preferred_element_type=F32
    )
    bed_speed = jnp.dot(bed_speed, blend_y, precision=HIGHEST, preferred_element_type=F32)

    bulk = jnp.full((16, 64), (step_size * inv_norm) * med[0, 15], F32)
    ocean_out(0, 15, rate_p + bulk * (ov[1, 15] - bed_speed))

    sent(x_up, *up_copies, wave_up)
    sent(x_down, *down_copies, wave_down)
    for e in (-1, 1):
        sent(has_late[e], plane_on[e])
    sent(y_up, ys_copies[0])
    sent(y_down, ys_copies[1])
    sent(has_right, yo_copies[0])
    sent(has_left, yo_copies[1])
    sent(z_up, *z_up_copies)
    sent(z_down, *z_down_copies)
    for pred, copies in plane_late:
        sent(pred, *copies)
    for pred, copies in plane_early:
        sent(pred, *copies)
    for k in range(1, nz):
        sent(gz == k, coarse_copies[k - 1])


def write_kernel(*refs):
    count = (len(refs) - 1) // 2
    sem = refs[-1]
    copies = [pltpu.make_async_copy(refs[i], refs[count + i], sem.at[i]) for i in range(count)]
    for copy in copies:
        copy.start()
    for copy in copies:
        copy.wait()


def body(sizes, solid_state, material, ocean_state, ocean_medium, offset_x, offset_y):
    outs = (solid_state.shape, solid_state.shape, ocean_state.shape, ocean_state.shape)
    v = lambda *shape: pltpu.VMEM(shape, F32)
    held = pl.pallas_call(
        functools.partial(section_kernel, sizes),
        out_shape=[pltpu.VMEM(shape, F32) for shape in outs],
        in_specs=[pl.BlockSpec(memory_space=pltpu.HBM)] * 6,
        out_specs=[pl.BlockSpec(memory_space=pltpu.VMEM)] * 4,
        scratch_shapes=[
            v(9, 8, 24, 128), v(4, 8, 8, 128), v(2, 16, 32, 64), v(2, 16, 16, 64),
            pltpu.SMEM((2, 16), F32), pltpu.VMEM((1, 16), jnp.int32), pltpu.VMEM((1, 64), jnp.int32),
            v(6, 2, 8, 128), v(6, 2, 8, 128), v(2, 3, 8, 128), v(4, 8, 128),
            v(2, 16, 2, 128), v(16, 2, 128), v(16, 2, 128),
            v(2, 8, 128), v(2, 8, 128), v(2, 8, 128), v(2, 8, 128), v(2, 8, 128), v(2, 8, 128), v(8, 128),
            v(6, 8, 8, 128), v(2, 16, 8, 128), v(6, 8, 8, 128), v(6, 8, 8, 128), v(16, 16, 64), v(2, 16, 8, 128),
            pltpu.SemaphoreType.DMA((8,)), pltpu.SemaphoreType.DMA((64,)), pltpu.SemaphoreType.DMA((24,)),
            pltpu.SemaphoreType.REGULAR((8,)),
        ],
        compiler_params=pltpu.CompilerParams(
            vmem_limit_bytes=16 * 2**20, collective_id=0, has_side_effects=True
        ),
        name="section",
    )(*(
        pltpu.with_memory_space_constraint(a, pltpu.HBM)
        for a in (solid_state, material, ocean_state, ocean_medium, offset_x.reshape(1, -1), offset_y.reshape(1, -1))
    ))
    return pl.pallas_call(
        write_kernel,
        out_shape=[jax.ShapeDtypeStruct(shape, F32) for shape in outs],
        in_specs=[pl.BlockSpec(memory_space=pltpu.VMEM)] * 4,
        out_specs=[pl.BlockSpec(memory_space=pl.ANY)] * 4,
        scratch_shapes=[pltpu.SemaphoreType.DMA((4,))],
        compiler_params=pltpu.CompilerParams(vmem_limit_bytes=4 * 2**20),
        name="write_out",
    )(*held)


def solution(mesh):
    sizes = (mesh.shape["gx"], mesh.shape["gy"], mesh.shape["gz"])
    solid = P(None, "gz", "gx", "gy")
    ocean = P(None, None, "gx", ("gy", "gz"))
    return jax.shard_map(
        functools.partial(body, sizes),
        mesh=mesh,
        in_specs=(solid, solid, ocean, P(), P("gx"), P(("gy", "gz"))),
        out_specs=(solid, solid, ocean, ocean),
        check_vma=False,
    )
```

```python
import functools

import jax
import jax.numpy as jnp
from jax import lax
from jax.experimental import pallas as pl
from jax.experimental.pallas import tpu as pltpu
from jax.sharding import PartitionSpec as P

closure_rows = (
    (-24.0 / 17.0, 59.0 / 34.0, -4.0 / 17.0, -3.0 / 34.0, 0.0, 0.0),
    (-0.5, 0.0, 0.5, 0.0, 0.0, 0.0),
    (4.0 / 43.0, -59.0 / 86.0, 0.0, 59.0 / 86.0, -4.0 / 43.0, 0.0),
    (3.0 / 98.0, 0.0, -59.0 / 98.0, 0.0, 32.0 / 49.0, -4.0 / 49.0),
)
inner_row = {-2: 1.0 / 12.0, -1: -8.0 / 12.0, 1: 8.0 / 12.0, 2: -1.0 / 12.0}
inv_norm = 48.0 / 17.0
step_size = 0.25
section_weight = 0.1496590219993
gravity = 0.4

MESH = pl.DeviceIdType.MESH
F32 = jnp.float32
HIGHEST = lax.Precision.HIGHEST
REACH = range(-3, 4)

x_fields = (0, 1, 2, 3, 7, 8)
y_fields = (0, 1, 2, 4, 6, 8)
z_fields = (0, 1, 2, 5, 6, 7)


def low_weight(k, d):
    return closure_rows[k][k + d] if 0 <= k + d < 6 else 0.0


def high_weight(k, d):
    return -closure_rows[k][k - d] if 0 <= k - d < 6 else 0.0


def weights(pos, n, first, last, closed):
    at_low = pos + jnp.where(first, 0, 4096)
    at_high = (n - 1) - pos + jnp.where(last, 0, 4096)
    table = {}
    for d in REACH:
        w = jnp.full(pos.shape, inner_row.get(d, 0.0), F32)
        if closed and d < 0:
            w = jnp.where(pos + d >= 0, w, 0.0)
        if closed and d > 0:
            w = jnp.where(pos + d < n, w, 0.0)
        for k in range(4):
            w = jnp.where(at_low == k, low_weight(k, d), w)
            w = jnp.where(at_high == k, high_weight(k, d), w)
        table[d] = w
    return table


def level_weights(level, n, first, last):
    table = {}
    for d in REACH:
        w = inner_row.get(d, 0.0)
        if level < 4 and first is not False:
            c = low_weight(level, d)
            w = c if first is True else (jnp.where(first, c, w) if c != w else w)
        elif level >= n - 4 and last is not False:
            c = high_weight(n - 1 - level, d)
            w = c if last is True else (jnp.where(last, c, w) if c != w else w)
        if not (isinstance(w, float) and w == 0.0):
            table[d] = w
    return table


def total(terms):
    out = None
    for term in terms:
        out = term if out is None else out + term
    return out


def roll_lanes(x, shift):
    return pltpu.roll(x, shift % 128, x.ndim - 1)


def rim_from_sides(left, right, lane, first, last):
    s = lax.rem(lane, 4)
    twelfth = 1.0 / 12.0
    from_left = jnp.where(first, 0.0, twelfth)
    from_right = jnp.where(last, 0.0, twelfth)
    one_left = jnp.where(s >= 2, from_left, 0.0)
    eight_left = jnp.where(s == 2, -8.0 * from_left, 0.0)
    one_right = jnp.where(s < 2, -from_right, 0.0)
    eight_right = jnp.where(s == 1, 8.0 * from_right, 0.0)
    return (
        one_left * roll_lanes(left, 2)
        + eight_left * roll_lanes(left, 1)
        + one_right * roll_lanes(right, -2)
        + eight_right * roll_lanes(right, -1)
    )


def when(pred, action):
    @pl.when(pred)
    def _():
        action()


def start(pred, *copies):
    when(pred, lambda: [copy.start() for copy in copies] and None)


def landed(pred, *copies):
    when(pred, lambda: [copy.wait_recv() for copy in copies] and None)


def sent(pred, *copies):
    when(pred, lambda: [copy.wait_send() for copy in copies] and None)


def both(a, b):
    return jnp.logical_and(a, b)


def section_kernel(
    sizes,
    solid, material, ocean, medium, off_x, off_y,
    s_next, s_rate, o_next, o_rate,
    sb, mb, ob, ov, med, ox, oy,
    z_low, z_high, plane, bed_part,
    xo_out, xo_low, xo_high, ys_out, ys_left, ys_right, yo_out, yo_left, yo_right, coarse_out,
    dys, dyo, dzs, txs, opre, cat,
    local_sem, send_sem, recv_sem, there,
):
    nx, ny, nz = sizes
    gx, gy, gz = lax.axis_index("gx"), lax.axis_index("gy"), lax.axis_index("gz")
    up_x, down_x = lax.rem(gx + 1, nx), lax.rem(gx + nx - 1, nx)
    up_y, down_y = lax.rem(gy + 1, ny), lax.rem(gy + ny - 1, ny)
    x_first, x_last = gx == 0, gx == nx - 1
    y_first, y_last = gy == 0, gy == ny - 1
    z_first, z_last = gz == 0, gz == nz - 1
    right = (gx, jnp.where(z_last, up_y, gy), jnp.where(z_last, 0, gz + 1))
    left = (gx, jnp.where(z_first, down_y, gy), jnp.where(z_first, nz - 1, gz - 1))
    xs = {-1: down_x, 0: gx, 1: up_x}

    x_down, x_up = gx > 0, gx < nx - 1
    y_down, y_up = gy > 0, gy < ny - 1
    z_down, z_up = gz > 0, gz < nz - 1
    has_left, has_right = jnp.logical_or(y_down, z_down), jnp.logical_or(y_up, z_up)
    has = {-1: x_down, 1: x_up}

    run = max(nx // 4, 2)
    turn = lax.rem(gx, run)
    late = {1: turn < run // 2, -1: jnp.logical_or(turn == 0, turn > run // 2)}
    has_late = {e: both(has[e], late[e]) for e in (-1, 1)}
    has_early = {e: both(has[e], jnp.logical_not(late[e])) for e in (-1, 1)}
    far_up, far_down = both(y_up, gy == ny - 2), both(y_down, gy == ny - 1)
    y_up_word, y_down_word = both(far_up, gz < 2), both(far_down, gz < 2)
    y_up_near, y_down_near = both(y_up, jnp.logical_not(y_up_word)), both(y_down, jnp.logical_not(y_down_word))
    odd = lax.rem(gz, 2) == 1
    even = jnp.logical_not(odd)
    barrier = pltpu.get_barrier_semaphore()

    def greet(x, y, z):
        pl.semaphore_signal(barrier, inc=1, device_id=(x, y, z), device_id_type=MESH)

    def tell(index, x, y, z):
        pl.semaphore_signal(there.at[index], inc=1, device_id=(x, y, z), device_id_type=MESH)

    plane[...] = jnp.zeros_like(plane)
    when(y_up_near, lambda: greet(gx, up_y, gz))
    for e in (-1, 1):
        when(has_late[e], lambda: greet(xs[e], gy, gz))
    when(odd, lambda: greet(gx, gy, gz - 1))
    when(gz < 2, lambda: greet(gx, gy, 2))
    for e in (-1, 1):
        when(both(has_late[e], z_down), lambda: greet(xs[e], gy, 0))
        when(both(has_late[e], both(z_first, y_down)), lambda: greet(xs[e], down_y, 0))
        when(both(has_late[e], both(z_last, y_up)), lambda: greet(xs[e], up_y, 0))

    loads = [
        pltpu.make_async_copy(src, dst, local_sem.at[i])
        for i, (src, dst) in enumerate(
            (
                (solid, sb.at[:, :, 8:16]),
                (ocean.at[0:2], ob.at[:, :, 8:24]),
                (ocean.at[2:4], ov),
                (material, mb),
                (medium, med),
                (off_x, ox),
                (off_y, oy),
            )
        )
    ]
    for load in loads:
        load.start()

    def clear(*places):
        for ref in places:
            ref[...] = jnp.zeros(ref.shape, F32)

    when(z_first, lambda: clear(z_low))
    when(z_last, lambda: clear(z_high))
    when(x_first, lambda: clear(sb.at[:, :, 6:8], xo_low))
    when(x_last, lambda: clear(sb.at[:, :, 16:18], xo_high))
    when(y_first, lambda: clear(ys_left))
    when(y_last, lambda: clear(ys_right))
    when(jnp.logical_not(has_left), lambda: clear(yo_left))
    when(jnp.logical_not(has_right), lambda: clear(yo_right))

    def count(*preds):
        return sum(jnp.where(p, 1, 0) for p in preds)

    n_early = count(*has_early.values())
    n_y = count(y_down, y_up)
    n_greet = count(y_down_near, even) + jnp.where(gz == 2, 2, 0)
    n_greet = n_greet + n_early * (1 + jnp.where(z_first, nz - 1 + n_y, 0))
    when(n_greet > 0, lambda: pl.semaphore_wait(barrier, n_greet))
    for e, index in ((1, 1), (-1, 0)):
        when(has_early[e], lambda: tell(index, xs[e], gy, gz))
    when(y_down_near, lambda: tell(2, gx, down_y, gz))
    when(gz == 2, lambda: tell(3, gx, gy, 1))
    when(even, lambda: tell(4, gx, gy, gz + 1))
    when(gz == 2, lambda: tell(5, gx, gy, 0))
    def await_partner(pred, index, amount=1):
        when(pred, lambda: pl.semaphore_wait(there.at[index], amount))

    counter = iter(range(64))

    def remote(src, dst, recv, device):
        return pltpu.make_async_remote_copy(
            src_ref=src, dst_ref=dst, send_sem=send_sem.at[next(counter)], recv_sem=recv_sem.at[recv],
            device_id=device, device_id_type=MESH,
        )

    up_copies, down_copies = [], []
    for i, (a, b) in enumerate(((0, 4), (7, 9))):
        up_copies.append(remote(solid.at[a:b, :, 6:8], sb.at[a:b, :, 6:8], 2 * i, (up_x, gy, gz)))
        down_copies.append(remote(solid.at[a:b, :, 0:2], sb.at[a:b, :, 16:18], 2 * i + 1, (down_x, gy, gz)))
    wave_up = remote(xo_out.at[1], xo_low, 4, (up_x, gy, gz))
    wave_down = remote(xo_out.at[0], xo_high, 5, (down_x, gy, gz))
    start(has_early[1], *up_copies)
    start(has_early[-1], *down_copies)

    z_up_copies = [
        remote(solid.at[a : a + 3, 6:8], z_low.at[b : b + 3], 6 + i, (gx, gy, gz + 1))
        for i, (a, b) in enumerate(((0, 0), (5, 3)))
    ]
    z_down_copies = [
        remote(solid.at[a : a + 3, 0:2], z_high.at[b : b + 3], 8 + i, (gx, gy, gz - 1))
        for i, (a, b) in enumerate(((0, 0), (5, 3)))
    ]

    tile = solid.at[2, 0]
    plane_early, plane_late = [], []
    rows = {-1: slice(7, 8), 0: slice(0, 8), 1: slice(0, 1)}
    for e in (-1, 0, 1):
        x, r = xs[-e], rows[e]
        part = solid.at[2, 0, r]
        mine = [remote(part, plane.at[0, e + 1, r], 10 + e + 1, (x, gy, k)) for k in range(1 if e == 0 else 0, nz)]
        above = remote(part, plane.at[1, e + 1, r], 13 + e + 1, (x, up_y, 0))
        below = remote(part, plane.at[1, e + 1, r], 13 + e + 1, (x, down_y, nz - 1))
        if e == 0:
            plane_early += [(z_first, mine[:1])]
            plane_late += [(z_first, mine[1:]), (both(z_first, y_up), [above]), (both(z_first, y_down), [below])]
        else:
            pred = both(z_first, has_early[-e])
            plane_early += [(pred, mine), (both(pred, y_up), [above]), (both(pred, y_down), [below])]
    plane_on = {
        e: remote(plane.at[0, 1, rows[-e]], plane.at[0, 1 - e, rows[-e]], 11 - e, (xs[e], gy, gz)) for e in (-1, 1)
    }
    own_plane = pltpu.make_async_copy(tile, plane.at[0, 1], local_sem.at[7])
    when(z_first, own_plane.start)
    for pred, copies in plane_early:
        start(pred, *copies)

    lane = lax.broadcasted_iota(jnp.int32, (8, 128), 1)

    loads[1].wait()
    for end, row in ((0, 8), (1, 22)):
        xo_out[end] = jnp.concatenate([ob[0, :, row : row + 2, :], ob[1, :, row : row + 2, :]], axis=2)
    start(has_early[1], wave_up)
    start(has_early[-1], wave_down)

    loads[0].wait()
    for half, fields in enumerate((y_fields[:4], y_fields[4:])):
        packed = jnp.zeros((8, 128), F32)
        for i, f in enumerate(fields):
            for z in range(8):
                k = 8 * i + z
                packed = jnp.where(lane // 4 == k, roll_lanes(sb[f, z, 8:16, :], 4 * k + 2), packed)
        ys_out[half] = packed
    ys_copies = [
        remote(ys_out, ys_left, 16, (gx, up_y, gz)),
        remote(ys_out, ys_right, 17, (gx, down_y, gz)),
    ]
    start(y_down_near, ys_copies[1])

    loads[2].wait()
    half_lane = lax.rem(lane, 64)
    for i in range(2):
        packed = jnp.zeros((8, 128), F32)
        for d in range(16):
            if i == 0:
                folded = jnp.concatenate([ob[0, d, 8:16, :], ob[0, d, 16:24, :]], axis=1)
            else:
                folded = jnp.concatenate([ov[0, d, 0:8, :], ov[0, d, 8:16, :]], axis=1)
            cat[i, d] = folded
            packed = jnp.where(half_lane // 4 == d, roll_lanes(folded, 4 * d + 2), packed)
        yo_out[i] = packed
    yo_copies = [remote(yo_out, yo_left, 18, right), remote(yo_out, yo_right, 19, left)]
    start(both(even, has_right), yo_copies[0])
    start(gz == 2, yo_copies[1])

    row = lax.broadcasted_iota(jnp.int32, (8, 16), 0)
    col = lax.broadcasted_iota(jnp.int32, (8, 16), 1)
    pair = jnp.where(col // 2 == row, 0.5, 0.0)
    fine = lax.broadcasted_iota(jnp.int32, (64, 128), 0)
    out_lane = lax.broadcasted_iota(jnp.int32, (64, 128), 1)
    place = jnp.where(out_lane == 32 * gz + fine // 2, 0.5, 0.0)
    coarse = jnp.dot(pair, ob[0, 15, 8:24, :], precision=HIGHEST, preferred_element_type=F32)
    coarse = jnp.dot(coarse, place, precision=HIGHEST, preferred_element_type=F32)
    coarse_out[...] = coarse
    coarse_copies = [remote(coarse_out, bed_part.at[k], 20 + k, (gx, gy, 0)) for k in range(1, nz)]
    start(gz == 2, coarse_copies[1])

    wy = weights(lane, 128, y_first, y_last, True)
    for i, f in enumerate(y_fields):
        own = sb[f, :, 8:16, :]
        dys[i] = total(wy[d] * (roll_lanes(own, -d) if d else own) for d in REACH)
    wo = weights(half_lane, 64, jnp.logical_and(y_first, z_first), jnp.logical_and(y_last, z_last), True)
    for i in range(2):
        for d0 in range(0, 16, 8):
            own = cat[i, d0 : d0 + 8]
            dyo[i, d0 : d0 + 8] = total(wo[d] * (roll_lanes(own, -d) if d else own) for d in REACH)
    sub = lax.broadcasted_iota(jnp.int32, (8, 128), 0)
    wx = weights(sub, 8, x_first, x_last, False)
    for i, f in enumerate(x_fields):
        own = sb[f, :, 8:16, :]
        txs[i] = wx[0] * own + wx[3] * pltpu.roll(own, 5, 1) + wx[-3] * pltpu.roll(own, 3, 1)

    start(even, *z_up_copies)
    start(gz == 2, *z_down_copies)
    await_partner(odd, 4)
    start(odd, *z_down_copies, yo_copies[1])
    for k in (1, 3):
        start(gz == k, coarse_copies[k - 1])
    await_partner(gz == 1, 3)
    start(gz == 1, *z_up_copies, yo_copies[0])
    await_partner(z_first, 5)
    start(*plane_late[0][:1], *plane_late[0][1])
    await_partner(y_up_near, 2)
    near_link = both(z_first, y_up_near)
    far_link = both(far_up, gz == 2)
    when(jnp.logical_or(near_link, far_link), lambda: tell(7, gx, gy, nz - 1))
    when(jnp.logical_or(near_link, far_link), lambda: tell(6, gx, up_y, 0))
    when(far_link, lambda: tell(6, gx, up_y, 1))
    for k in (0, 1):
        when(far_link, lambda: tell(7, gx, gy, k))
    await_partner(y_up_word, 7)
    start(y_up, ys_copies[0])
    start(*plane_late[1][:1], *plane_late[1][1])
    await_partner(jnp.logical_or(both(z_first, y_down), y_down_word), 6)
    start(y_down_word, ys_copies[1])
    start(both(z_first, y_down), yo_copies[1], *plane_late[2][1])
    await_partner(both(z_last, y_up), 7)
    start(both(z_last, y_up), yo_copies[0])
    for e, index, copies in ((1, 0, up_copies + [wave_up]), (-1, 1, down_copies + [wave_down])):
        await_partner(has_late[e], index)
        start(has_late[e], *copies)
    sides = ((both(z_first, y_down), 127), (both(z_last, y_up), 0))

    def plane_wait(s, e):
        pltpu.make_async_remote_copy(
            src_ref=solid.at[2, 0, rows[e]], dst_ref=plane.at[s, e + 1, rows[e]], send_sem=send_sem.at[63], recv_sem=recv_sem.at[10 + 3 * s + e + 1],
            device_id=(gx, up_y, gz), device_id_type=MESH,
        ).wait_recv()

    def merge(e):
        for pred, at in sides:

            @pl.when(pred)
            def _(at=at):
                plane_wait(1, e)
                plane[0, e + 1] = jnp.where(lane == at, plane[1, e + 1], plane[0, e + 1])

    when(z_first, own_plane.wait)
    when(z_down, lambda: plane_wait(0, 0))
    merge(0)
    for e in (-1, 1):
        start(has_late[e], plane_on[e])

    landed(y_down, ys_copies[0])
    landed(y_up, ys_copies[1])
    at_edge = jnp.logical_or(lane < 2, lane >= 126)
    for half, fields in enumerate((y_fields[:4], y_fields[4:])):
        rim = rim_from_sides(ys_left[half], ys_right[half], lane, y_first, y_last)
        for i in range(len(fields)):
            for z in range(8):
                k = 8 * i + z
                dys[4 * half + i, z] += jnp.where(at_edge, roll_lanes(rim, -4 * k - 2), 0.0)
    landed(has_left, yo_copies[0])
    landed(has_right, yo_copies[1])
    at_half_edge = jnp.logical_or(half_lane < 2, half_lane >= 62)
    for i in range(2):
        rim = rim_from_sides(
            roll_lanes(yo_left[i], 64), roll_lanes(yo_right[i], 64), lane,
            jnp.logical_and(y_first, z_first), jnp.logical_and(y_last, z_last),
        )
        for d in range(16):
            dyo[i, d] += jnp.where(at_half_edge, roll_lanes(rim, -4 * d - 2), 0.0)

    loads[3].wait()

    landed(z_down, *z_up_copies)
    landed(z_up, *z_down_copies)

    for i, f in enumerate(z_fields):
        def level(z, i=i, f=f):
            if z < 0:
                return z_low[i, z + 2]
            if z >= 8:
                return z_high[i, z - 8]
            return sb[f, z, 8:16, :]

        for z in range(8):
            table = level_weights(z, 8, z_first, z_last)
            dzs[i, z] = mb[3, z] * total(w * level(z + d) for d, w in table.items() if -2 <= z + d < 10)

    @pl.when(z_first)
    def _():
        for k in range(1, nz):
            pltpu.make_async_remote_copy(
                src_ref=coarse_out, dst_ref=bed_part.at[k], send_sem=send_sem.at[63], recv_sem=recv_sem.at[20 + k],
                device_id=(gx, up_y, gz), device_id_type=MESH,
            ).wait_recv()
        scale = inv_norm * mb[3, 0]
        bed_pressure = coarse_out[...] + total(bed_part[k] for k in range(1, nz))
        dzs[5, 0] += scale * sb[7, 0, 8:16, :]
        dzs[4, 0] += scale * sb[6, 0, 8:16, :]
        dzs[3, 0] += scale * (sb[5, 0, 8:16, :] + bed_pressure)

    loads[4].wait()

    def unfold(i, d):
        folded = dyo[i, d]
        return jnp.concatenate([folded[:, 0:64], folded[:, 64:128]], axis=0)

    for d in range(16):
        bulk = jnp.full((16, 64), med[0, d], F32)
        light = jnp.full((16, 64), med[1, d], F32)
        pressure, flow_v, flow_w = ob[0, d, 8:24, :], ov[0, d], ov[1, d]
        table = level_weights(d, 16, True, True)
        dz_w = total(w * ov[1, d + k] for k, w in table.items())
        dz_p = total(w * ob[0, d + k, 8:24, :] for k, w in table.items())
        part = -bulk * (2.0 * unfold(1, d) + dz_w) + gravity * flow_w / light
        opre[d] = step_size * part
        rate_v = (-2.0 * step_size) * light * unfold(0, d)
        rate_w = -light * dz_p
        if d == 0:
            rate_w = rate_w - inv_norm * light * pressure
        rate_w = step_size * rate_w
        o_rate[2, d] = rate_v
        o_rate[3, d] = rate_w
        o_next[2, d] = flow_v + section_weight * rate_v
        o_next[3, d] = flow_w + section_weight * rate_w

    landed(x_down, *up_copies, wave_up)
    landed(x_up, *down_copies, wave_down)
    for rim, row in ((xo_low, 6), (xo_high, 24)):
        for i in range(2):
            ob[i, :, row : row + 2, :] = rim[:, :, 64 * i : 64 * i + 64]

    def dx(i, f, z):
        out = txs[i, z]
        for d in (-2, -1, 1, 2):
            out = out + wx[d] * sb[f, z, 8 + d : 16 + d, :]
        return out

    for z in range(8):
        own = [sb[f, z, 8:16, :] for f in range(9)]
        b, lam, mu = step_size * mb[0, z], step_size * mb[1, z], step_size * mb[2, z]
        d_x = {f: dx(i, f, z) for i, f in enumerate(x_fields)}
        d_y = {f: dys[i, z] for i, f in enumerate(y_fields)}
        d_z = {f: dzs[i, z] for i, f in enumerate(z_fields)}
        dilation = lam * (d_x[0] + d_y[1] + d_z[2])
        mu2 = 2.0 * mu
        rates = [
            b * (d_x[3] + d_y[8] + d_z[7]),
            b * (d_x[8] + d_y[4] + d_z[6]),
            b * (d_x[7] + d_y[6] + d_z[5]),
            dilation + mu2 * d_x[0],
            dilation + mu2 * d_y[1],
            dilation + mu2 * d_z[2],
            mu * (d_z[1] + d_y[2]),
            mu * (d_z[0] + d_x[2]),
            mu * (d_y[0] + d_x[1]),
        ]
        for f in range(9):
            s_rate[f, z] = rates[f]
            s_next[f, z] = own[f] + section_weight * rates[f]

    pos = lax.broadcasted_iota(jnp.int32, (16, 64), 0)
    wp = weights(pos, 16, x_first, x_last, False)
    far_up, far_down = wp[3] != 0.0, wp[-3] != 0.0

    def dx_ocean(i, d):
        out = total(wp[k] * ob[i, d, 8 + k : 24 + k, :] for k in range(-2, 3))
        out = out + wp[3] * jnp.where(far_up, ob[i, d, 11:27, :], 0.0)
        return out + wp[-3] * jnp.where(far_down, ob[i, d, 5:21, :], 0.0)

    def ocean_out(i, d, rate):
        o_rate[i, d] = rate
        o_next[i, d] = ob[i, d, 8:24, :] + section_weight * rate

    for d in range(16):
        bulk = jnp.full((16, 64), (-2.0 * step_size) * med[0, d], F32)
        light = jnp.full((16, 64), (-2.0 * step_size) * med[1, d], F32)
        rate_p = opre[d] + bulk * dx_ocean(1, d)
        ocean_out(1, d, light * dx_ocean(0, d))
        if d < 15:
            ocean_out(0, d, rate_p)

    loads[5].wait()
    loads[6].wait()
    for e in (-1, 1):
        when(has[e], lambda: plane_wait(0, e))
        when(has_late[e], lambda: merge(e))

    window = plane[0].reshape(24, 128)
    fine_x = lax.broadcasted_iota(jnp.int32, (24, 16), 1)
    coarse_x = lax.broadcasted_iota(jnp.int32, (24, 16), 0) + (8 * gx - 8)
    near_x = 8 * gx + fine_x // 2
    far_x = jnp.clip(near_x + ox[...], 0, 8 * nx - 1)
    blend_x = jnp.where(coarse_x == near_x, 0.75, 0.0) + jnp.where(coarse_x == far_x, 0.25, 0.0)
    fine_y = lax.broadcasted_iota(jnp.int32, (128, 64), 1)
    coarse_y = lax.broadcasted_iota(jnp.int32, (128, 64), 0)
    near_y = 128 * gy + 32 * gz + fine_y // 2
    far_y = jnp.clip(near_y + oy[...], 0, 128 * ny - 1)
    blend_y = jnp.where(coarse_y == lax.rem(near_y, 128), 0.75, 0.0)
    blend_y = blend_y + jnp.where(coarse_y == lax.rem(far_y, 128), 0.25, 0.0)
    bed_speed = lax.dot_general(
        blend_x, window, (((0,), (0,)), ((), ())), precision=HIGHEST, preferred_element_type=F32
    )
    bed_speed = jnp.dot(bed_speed, blend_y, precision=HIGHEST, preferred_element_type=F32)

    bulk = jnp.full((16, 64), (step_size * inv_norm) * med[0, 15], F32)
    ocean_out(0, 15, rate_p + bulk * (ov[1, 15] - bed_speed))

    sent(x_up, *up_copies, wave_up)
    sent(x_down, *down_copies, wave_down)
    for e in (-1, 1):
        sent(has_late[e], plane_on[e])
    sent(y_up, ys_copies[0])
    sent(y_down, ys_copies[1])
    sent(has_right, yo_copies[0])
    sent(has_left, yo_copies[1])
    sent(z_up, *z_up_copies)
    sent(z_down, *z_down_copies)
    for pred, copies in plane_late:
        sent(pred, *copies)
    for pred, copies in plane_early:
        sent(pred, *copies)
    for k in range(1, nz):
        sent(gz == k, coarse_copies[k - 1])


def write_kernel(*refs):
    count = (len(refs) - 1) // 2
    sem = refs[-1]
    copies = [pltpu.make_async_copy(refs[i], refs[count + i], sem.at[i]) for i in range(count)]
    for copy in copies:
        copy.start()
    for copy in copies:
        copy.wait()


def body(sizes, solid_state, material, ocean_state, ocean_medium, offset_x, offset_y):
    outs = (solid_state.shape, solid_state.shape, ocean_state.shape, ocean_state.shape)
    v = lambda *shape: pltpu.VMEM(shape, F32)
    held = pl.pallas_call(
        functools.partial(section_kernel, sizes),
        out_shape=[pltpu.VMEM(shape, F32) for shape in outs],
        in_specs=[pl.BlockSpec(memory_space=pltpu.HBM)] * 6,
        out_specs=[pl.BlockSpec(memory_space=pltpu.VMEM)] * 4,
        scratch_shapes=[
            v(9, 8, 24, 128), v(4, 8, 8, 128), v(2, 16, 32, 64), v(2, 16, 16, 64),
            pltpu.SMEM((2, 16), F32), pltpu.VMEM((1, 16), jnp.int32), pltpu.VMEM((1, 64), jnp.int32),
            v(6, 2, 8, 128), v(6, 2, 8, 128), v(2, 3, 8, 128), v(4, 8, 128),
            v(2, 16, 2, 128), v(16, 2, 128), v(16, 2, 128),
            v(2, 8, 128), v(2, 8, 128), v(2, 8, 128), v(2, 8, 128), v(2, 8, 128), v(2, 8, 128), v(8, 128),
            v(6, 8, 8, 128), v(2, 16, 8, 128), v(6, 8, 8, 128), v(6, 8, 8, 128), v(16, 16, 64), v(2, 16, 8, 128),
            pltpu.SemaphoreType.DMA((8,)), pltpu.SemaphoreType.DMA((64,)), pltpu.SemaphoreType.DMA((24,)),
            pltpu.SemaphoreType.REGULAR((8,)),
        ],
        compiler_params=pltpu.CompilerParams(
            vmem_limit_bytes=16 * 2**20, collective_id=0, has_side_effects=True
        ),
        name="section",
    )(*(
        pltpu.with_memory_space_constraint(a, pltpu.HBM)
        for a in (solid_state, material, ocean_state, ocean_medium, offset_x.reshape(1, -1), offset_y.reshape(1, -1))
    ))
    return pl.pallas_call(
        write_kernel,
        out_shape=[jax.ShapeDtypeStruct(shape, F32) for shape in outs],
        in_specs=[pl.BlockSpec(memory_space=pltpu.VMEM)] * 4,
        out_specs=[pl.BlockSpec(memory_space=pl.ANY)] * 4,
        scratch_shapes=[pltpu.SemaphoreType.DMA((4,))],
        compiler_params=pltpu.CompilerParams(vmem_limit_bytes=4 * 2**20),
        name="write_out",
    )(*held)


def solution(mesh):
    sizes = (mesh.shape["gx"], mesh.shape["gy"], mesh.shape["gz"])
    solid = P(None, "gz", "gx", "gy")
    ocean = P(None, None, "gx", ("gy", "gz"))
    return jax.shard_map(
        functools.partial(body, sizes),
        mesh=mesh,
        in_specs=(solid, solid, ocean, P(), P("gx"), P(("gy", "gz"))),
        out_specs=(solid, solid, ocean, ocean),
        check_vma=False,
    )
```

```python
import functools

import jax
import jax.numpy as jnp
from jax import lax
from jax.experimental import pallas as pl
from jax.experimental.pallas import tpu as pltpu
from jax.sharding import PartitionSpec as P

closure_rows = (
    (-24.0 / 17.0, 59.0 / 34.0, -4.0 / 17.0, -3.0 / 34.0, 0.0, 0.0),
    (-0.5, 0.0, 0.5, 0.0, 0.0, 0.0),
    (4.0 / 43.0, -59.0 / 86.0, 0.0, 59.0 / 86.0, -4.0 / 43.0, 0.0),
    (3.0 / 98.0, 0.0, -59.0 / 98.0, 0.0, 32.0 / 49.0, -4.0 / 49.0),
)
inner_row = {-2: 1.0 / 12.0, -1: -8.0 / 12.0, 1: 8.0 / 12.0, 2: -1.0 / 12.0}
inv_norm = 48.0 / 17.0
step_size = 0.25
section_weight = 0.1496590219993
gravity = 0.4

MESH = pl.DeviceIdType.MESH
F32 = jnp.float32
HIGHEST = lax.Precision.HIGHEST
REACH = range(-3, 4)

x_fields = (0, 1, 2, 3, 7, 8)
y_fields = (0, 1, 2, 4, 6, 8)
z_fields = (0, 1, 2, 5, 6, 7)


def low_weight(k, d):
    return closure_rows[k][k + d] if 0 <= k + d < 6 else 0.0


def high_weight(k, d):
    return -closure_rows[k][k - d] if 0 <= k - d < 6 else 0.0


def weights(pos, n, first, last, closed):
    at_low = pos + jnp.where(first, 0, 4096)
    at_high = (n - 1) - pos + jnp.where(last, 0, 4096)
    table = {}
    for d in REACH:
        w = jnp.full(pos.shape, inner_row.get(d, 0.0), F32)
        if closed and d < 0:
            w = jnp.where(pos + d >= 0, w, 0.0)
        if closed and d > 0:
            w = jnp.where(pos + d < n, w, 0.0)
        for k in range(4):
            w = jnp.where(at_low == k, low_weight(k, d), w)
            w = jnp.where(at_high == k, high_weight(k, d), w)
        table[d] = w
    return table


def level_weights(level, n, first, last):
    table = {}
    for d in REACH:
        w = inner_row.get(d, 0.0)
        if level < 4 and first is not False:
            c = low_weight(level, d)
            w = c if first is True else (jnp.where(first, c, w) if c != w else w)
        elif level >= n - 4 and last is not False:
            c = high_weight(n - 1 - level, d)
            w = c if last is True else (jnp.where(last, c, w) if c != w else w)
        if not (isinstance(w, float) and w == 0.0):
            table[d] = w
    return table


def total(terms):
    out = None
    for term in terms:
        out = term if out is None else out + term
    return out


def roll_lanes(x, shift):
    return pltpu.roll(x, shift % 128, x.ndim - 1)


def rim_from_sides(left, right, lane, first, last):
    s = lax.rem(lane, 4)
    twelfth = 1.0 / 12.0
    from_left = jnp.where(first, 0.0, twelfth)
    from_right = jnp.where(last, 0.0, twelfth)
    one_left = jnp.where(s >= 2, from_left, 0.0)
    eight_left = jnp.where(s == 2, -8.0 * from_left, 0.0)
    one_right = jnp.where(s < 2, -from_right, 0.0)
    eight_right = jnp.where(s == 1, 8.0 * from_right, 0.0)
    return (
        one_left * roll_lanes(left, 2)
        + eight_left * roll_lanes(left, 1)
        + one_right * roll_lanes(right, -2)
        + eight_right * roll_lanes(right, -1)
    )


def when(pred, action):
    @pl.when(pred)
    def _():
        action()


def start(pred, *copies):
    when(pred, lambda: [copy.start() for copy in copies] and None)


def landed(pred, *copies):
    when(pred, lambda: [copy.wait_recv() for copy in copies] and None)


def sent(pred, *copies):
    when(pred, lambda: [copy.wait_send() for copy in copies] and None)


def both(a, b):
    return jnp.logical_and(a, b)


def section_kernel(
    sizes,
    solid, material, ocean, medium, off_x, off_y,
    o_next, o_rate, sb, mb, txs, dys, dzs,
    ob, ov, med, ox, oy,
    z_low, z_high, plane, bed_part,
    xo_out, xo_low, xo_high, ys_out, ys_left, ys_right, yo_out, yo_left, yo_right, coarse_out,
    dyo, opre, cat,
    local_sem, send_sem, recv_sem, there,
):
    nx, ny, nz = sizes
    gx, gy, gz = lax.axis_index("gx"), lax.axis_index("gy"), lax.axis_index("gz")
    up_x, down_x = lax.rem(gx + 1, nx), lax.rem(gx + nx - 1, nx)
    up_y, down_y = lax.rem(gy + 1, ny), lax.rem(gy + ny - 1, ny)
    x_first, x_last = gx == 0, gx == nx - 1
    y_first, y_last = gy == 0, gy == ny - 1
    z_first, z_last = gz == 0, gz == nz - 1
    right = (gx, jnp.where(z_last, up_y, gy), jnp.where(z_last, 0, gz + 1))
    left = (gx, jnp.where(z_first, down_y, gy), jnp.where(z_first, nz - 1, gz - 1))
    xs = {-1: down_x, 0: gx, 1: up_x}

    x_down, x_up = gx > 0, gx < nx - 1
    y_down, y_up = gy > 0, gy < ny - 1
    z_down, z_up = gz > 0, gz < nz - 1
    has_left, has_right = jnp.logical_or(y_down, z_down), jnp.logical_or(y_up, z_up)
    has = {-1: x_down, 1: x_up}

    run = max(nx // 4, 2)
    turn = lax.rem(gx, run)
    late = {1: turn < run // 2, -1: jnp.logical_or(turn == 0, turn > run // 2)}
    has_late = {e: both(has[e], late[e]) for e in (-1, 1)}
    has_early = {e: both(has[e], jnp.logical_not(late[e])) for e in (-1, 1)}
    far_up, far_down = both(y_up, gy == ny - 2), both(y_down, gy == ny - 1)
    y_up_word, y_down_word = both(far_up, gz < 2), both(far_down, gz < 2)
    y_up_near, y_down_near = both(y_up, jnp.logical_not(y_up_word)), both(y_down, jnp.logical_not(y_down_word))
    odd = lax.rem(gz, 2) == 1
    even = jnp.logical_not(odd)
    barrier = pltpu.get_barrier_semaphore()

    def greet(x, y, z):
        pl.semaphore_signal(barrier, inc=1, device_id=(x, y, z), device_id_type=MESH)

    def tell(index, x, y, z):
        pl.semaphore_signal(there.at[index], inc=1, device_id=(x, y, z), device_id_type=MESH)

    plane[...] = jnp.zeros_like(plane)
    when(y_up_near, lambda: greet(gx, up_y, gz))
    for e in (-1, 1):
        when(has_late[e], lambda: greet(xs[e], gy, gz))
    when(odd, lambda: greet(gx, gy, gz - 1))
    when(gz < 2, lambda: greet(gx, gy, 2))
    for e in (-1, 1):
        when(both(has_late[e], z_down), lambda: greet(xs[e], gy, 0))
        when(both(has_late[e], both(z_first, y_down)), lambda: greet(xs[e], down_y, 0))
        when(both(has_late[e], both(z_last, y_up)), lambda: greet(xs[e], up_y, 0))

    loads = [
        pltpu.make_async_copy(src, dst, local_sem.at[i])
        for i, (src, dst) in enumerate(
            (
                (solid, sb.at[:, :, 8:16]),
                (ocean.at[0:2], ob.at[:, :, 8:24]),
                (ocean.at[2:4], ov),
                (material, mb),
                (medium, med),
                (off_x, ox),
                (off_y, oy),
            )
        )
    ]
    for i in (1, 0, 2, 3, 4, 5, 6):
        loads[i].start()

    def clear(*places):
        for ref in places:
            ref[...] = jnp.zeros(ref.shape, F32)

    when(z_first, lambda: clear(z_low))
    when(z_last, lambda: clear(z_high))
    when(x_first, lambda: clear(sb.at[:, :, 6:8], xo_low))
    when(x_last, lambda: clear(sb.at[:, :, 16:18], xo_high))
    when(y_first, lambda: clear(ys_left))
    when(y_last, lambda: clear(ys_right))
    when(jnp.logical_not(has_left), lambda: clear(yo_left))
    when(jnp.logical_not(has_right), lambda: clear(yo_right))

    def count(*preds):
        return sum(jnp.where(p, 1, 0) for p in preds)

    n_early = count(*has_early.values())
    n_y = count(y_down, y_up)
    n_greet = count(y_down_near, even) + jnp.where(gz == 2, 2, 0)
    n_greet = n_greet + n_early * (1 + jnp.where(z_first, nz - 1 + n_y, 0))
    when(n_greet > 0, lambda: pl.semaphore_wait(barrier, n_greet))
    for e, index in ((1, 1), (-1, 0)):
        when(has_early[e], lambda: tell(index, xs[e], gy, gz))
    when(y_down_near, lambda: tell(2, gx, down_y, gz))
    when(gz == 2, lambda: tell(3, gx, gy, 1))
    when(even, lambda: tell(4, gx, gy, gz + 1))
    when(gz == 2, lambda: tell(5, gx, gy, 0))
    def await_partner(pred, index, amount=1):
        when(pred, lambda: pl.semaphore_wait(there.at[index], amount))

    counter = iter(range(64))

    def remote(src, dst, recv, device):
        return pltpu.make_async_remote_copy(
            src_ref=src, dst_ref=dst, send_sem=send_sem.at[next(counter)], recv_sem=recv_sem.at[recv],
            device_id=device, device_id_type=MESH,
        )

    up_copies, down_copies = [], []
    for i, (a, b) in enumerate(((0, 4), (7, 9))):
        up_copies.append(remote(solid.at[a:b, :, 6:8], sb.at[a:b, :, 6:8], 2 * i, (up_x, gy, gz)))
        down_copies.append(remote(solid.at[a:b, :, 0:2], sb.at[a:b, :, 16:18], 2 * i + 1, (down_x, gy, gz)))
    wave_up = remote(xo_out.at[1], xo_low, 4, (up_x, gy, gz))
    wave_down = remote(xo_out.at[0], xo_high, 5, (down_x, gy, gz))
    start(has_early[1], up_copies[0])
    start(has_early[-1], down_copies[0])

    z_up_copies = [
        remote(solid.at[a : a + 3, 6:8], z_low.at[b : b + 3], 6 + i, (gx, gy, gz + 1))
        for i, (a, b) in enumerate(((0, 0), (5, 3)))
    ]
    z_down_copies = [
        remote(solid.at[a : a + 3, 0:2], z_high.at[b : b + 3], 8 + i, (gx, gy, gz - 1))
        for i, (a, b) in enumerate(((0, 0), (5, 3)))
    ]

    tile = solid.at[2, 0]
    plane_early, plane_late = [], []
    rows = {-1: slice(7, 8), 0: slice(0, 8), 1: slice(0, 1)}
    for e in (-1, 0, 1):
        x, r = xs[-e], rows[e]
        part = solid.at[2, 0, r]
        mine = [remote(part, plane.at[0, e + 1, r], 10 + e + 1, (x, gy, k)) for k in range(1 if e == 0 else 0, nz)]
        above = remote(part, plane.at[1, e + 1, r], 13 + e + 1, (x, up_y, 0))
        below = remote(part, plane.at[1, e + 1, r], 13 + e + 1, (x, down_y, nz - 1))
        if e == 0:
            plane_early += [(z_first, mine[:1])]
            plane_late += [(z_first, mine[1:]), (both(z_first, y_up), [above]), (both(z_first, y_down), [below])]
        else:
            pred = both(z_first, has_early[-e])
            plane_early += [(pred, mine), (both(pred, y_up), [above]), (both(pred, y_down), [below])]
    plane_on = {
        e: remote(plane.at[0, 1, rows[-e]], plane.at[0, 1 - e, rows[-e]], 11 - e, (xs[e], gy, gz)) for e in (-1, 1)
    }
    own_plane = pltpu.make_async_copy(tile, plane.at[0, 1], local_sem.at[7])
    when(z_first, own_plane.start)
    for pred, copies in plane_early:
        start(pred, *copies)

    start(has_early[1], up_copies[1])
    start(has_early[-1], down_copies[1])

    lane = lax.broadcasted_iota(jnp.int32, (8, 128), 1)

    loads[1].wait()
    for end, row in ((0, 8), (1, 22)):
        xo_out[end] = jnp.concatenate([ob[0, :, row : row + 2, :], ob[1, :, row : row + 2, :]], axis=2)
    start(has_early[1], wave_up)
    start(has_early[-1], wave_down)

    loads[0].wait()
    for half, fields in enumerate((y_fields[:4], y_fields[4:])):
        packed = jnp.zeros((8, 128), F32)
        for i, f in enumerate(fields):
            for z in range(8):
                k = 8 * i + z
                packed = jnp.where(lane // 4 == k, roll_lanes(sb[f, z, 8:16, :], 4 * k + 2), packed)
        ys_out[half] = packed
    ys_copies = [
        remote(ys_out, ys_left, 16, (gx, up_y, gz)),
        remote(ys_out, ys_right, 17, (gx, down_y, gz)),
    ]
    start(y_down_near, ys_copies[1])

    loads[2].wait()
    half_lane = lax.rem(lane, 64)
    for i in range(2):
        packed = jnp.zeros((8, 128), F32)
        for d in range(16):
            if i == 0:
                folded = jnp.concatenate([ob[0, d, 8:16, :], ob[0, d, 16:24, :]], axis=1)
            else:
                folded = jnp.concatenate([ov[0, d, 0:8, :], ov[0, d, 8:16, :]], axis=1)
            cat[i, d] = folded
            packed = jnp.where(half_lane // 4 == d, roll_lanes(folded, 4 * d + 2), packed)
        yo_out[i] = packed
    yo_copies = [remote(yo_out, yo_left, 18, right), remote(yo_out, yo_right, 19, left)]
    start(both(even, has_right), yo_copies[0])
    start(gz == 2, yo_copies[1])

    row = lax.broadcasted_iota(jnp.int32, (8, 16), 0)
    col = lax.broadcasted_iota(jnp.int32, (8, 16), 1)
    pair = jnp.where(col // 2 == row, 0.5, 0.0)
    fine = lax.broadcasted_iota(jnp.int32, (64, 128), 0)
    out_lane = lax.broadcasted_iota(jnp.int32, (64, 128), 1)
    place = jnp.where(out_lane == 32 * gz + fine // 2, 0.5, 0.0)
    coarse = jnp.dot(pair, ob[0, 15, 8:24, :], precision=HIGHEST, preferred_element_type=F32)
    coarse = jnp.dot(coarse, place, precision=HIGHEST, preferred_element_type=F32)
    coarse_out[...] = coarse
    coarse_copies = [remote(coarse_out, bed_part.at[k], 20 + k, (gx, gy, 0)) for k in range(1, nz)]
    start(gz == 2, coarse_copies[1])

    wy = weights(lane, 128, y_first, y_last, True)
    for i, f in enumerate(y_fields):
        own = sb[f, :, 8:16, :]
        dys[i] = total(wy[d] * (roll_lanes(own, -d) if d else own) for d in REACH)
    wo = weights(half_lane, 64, jnp.logical_and(y_first, z_first), jnp.logical_and(y_last, z_last), True)
    for i in range(2):
        for d0 in range(0, 16, 8):
            own = cat[i, d0 : d0 + 8]
            dyo[i, d0 : d0 + 8] = total(wo[d] * (roll_lanes(own, -d) if d else own) for d in REACH)
    sub = lax.broadcasted_iota(jnp.int32, (8, 128), 0)
    wx = weights(sub, 8, x_first, x_last, False)
    for i, f in enumerate(x_fields):
        own = sb[f, :, 8:16, :]
        txs[i] = wx[0] * own + wx[3] * pltpu.roll(own, 5, 1) + wx[-3] * pltpu.roll(own, 3, 1)

    start(even, *z_up_copies)
    start(gz == 2, *z_down_copies)
    await_partner(odd, 4)
    start(odd, *z_down_copies, yo_copies[1])
    for k in (1, 3):
        start(gz == k, coarse_copies[k - 1])
    await_partner(gz == 1, 3)
    start(gz == 1, *z_up_copies, yo_copies[0])
    await_partner(z_first, 5)
    start(*plane_late[0][:1], *plane_late[0][1])
    await_partner(y_up_near, 2)
    near_link = both(z_first, y_up_near)
    far_link = both(far_up, gz == 2)
    when(jnp.logical_or(near_link, far_link), lambda: tell(7, gx, gy, nz - 1))
    when(jnp.logical_or(near_link, far_link), lambda: tell(6, gx, up_y, 0))
    when(far_link, lambda: tell(6, gx, up_y, 1))
    for k in (0, 1):
        when(far_link, lambda: tell(7, gx, gy, k))
    await_partner(y_up_word, 7)
    start(y_up, ys_copies[0])
    start(*plane_late[1][:1], *plane_late[1][1])
    await_partner(jnp.logical_or(both(z_first, y_down), y_down_word), 6)
    start(y_down_word, ys_copies[1])
    start(both(z_first, y_down), yo_copies[1], *plane_late[2][1])
    await_partner(both(z_last, y_up), 7)
    start(both(z_last, y_up), yo_copies[0])
    for e, index, copies in ((1, 0, up_copies + [wave_up]), (-1, 1, down_copies + [wave_down])):
        await_partner(has_late[e], index)
        start(has_late[e], *copies)
    sides = ((both(z_first, y_down), 127), (both(z_last, y_up), 0))

    def plane_wait(s, e):
        pltpu.make_async_remote_copy(
            src_ref=solid.at[2, 0, rows[e]], dst_ref=plane.at[s, e + 1, rows[e]], send_sem=send_sem.at[63], recv_sem=recv_sem.at[10 + 3 * s + e + 1],
            device_id=(gx, up_y, gz), device_id_type=MESH,
        ).wait_recv()

    def merge(e):
        for pred, at in sides:

            @pl.when(pred)
            def _(at=at):
                plane_wait(1, e)
                plane[0, e + 1] = jnp.where(lane == at, plane[1, e + 1], plane[0, e + 1])

    when(z_first, own_plane.wait)
    when(z_down, lambda: plane_wait(0, 0))
    merge(0)
    for e in (-1, 1):
        start(has_late[e], plane_on[e])

    landed(y_down, ys_copies[0])
    landed(y_up, ys_copies[1])
    at_edge = jnp.logical_or(lane < 2, lane >= 126)
    for half, fields in enumerate((y_fields[:4], y_fields[4:])):
        rim = rim_from_sides(ys_left[half], ys_right[half], lane, y_first, y_last)
        for i in range(len(fields)):
            for z in range(8):
                k = 8 * i + z
                dys[4 * half + i, z] += jnp.where(at_edge, roll_lanes(rim, -4 * k - 2), 0.0)
    landed(has_left, yo_copies[0])
    landed(has_right, yo_copies[1])
    at_half_edge = jnp.logical_or(half_lane < 2, half_lane >= 62)
    for i in range(2):
        rim = rim_from_sides(
            roll_lanes(yo_left[i], 64), roll_lanes(yo_right[i], 64), lane,
            jnp.logical_and(y_first, z_first), jnp.logical_and(y_last, z_last),
        )
        for d in range(16):
            dyo[i, d] += jnp.where(at_half_edge, roll_lanes(rim, -4 * d - 2), 0.0)

    loads[3].wait()

    landed(z_down, *z_up_copies)
    landed(z_up, *z_down_copies)

    for i, f in enumerate(z_fields):
        def level(z, i=i, f=f):
            if z < 0:
                return z_low[i, z + 2]
            if z >= 8:
                return z_high[i, z - 8]
            return sb[f, z, 8:16, :]

        for z in range(8):
            table = level_weights(z, 8, z_first, z_last)
            dzs[i, z] = mb[3, z] * total(w * level(z + d) for d, w in table.items() if -2 <= z + d < 10)

    @pl.when(z_first)
    def _():
        for k in range(1, nz):
            pltpu.make_async_remote_copy(
                src_ref=coarse_out, dst_ref=bed_part.at[k], send_sem=send_sem.at[63], recv_sem=recv_sem.at[20 + k],
                device_id=(gx, up_y, gz), device_id_type=MESH,
            ).wait_recv()
        scale = inv_norm * mb[3, 0]
        bed_pressure = coarse_out[...] + total(bed_part[k] for k in range(1, nz))
        dzs[5, 0] += scale * sb[7, 0, 8:16, :]
        dzs[4, 0] += scale * sb[6, 0, 8:16, :]
        dzs[3, 0] += scale * (sb[5, 0, 8:16, :] + bed_pressure)

    loads[4].wait()

    def unfold(i, d):
        folded = dyo[i, d]
        return jnp.concatenate([folded[:, 0:64], folded[:, 64:128]], axis=0)

    for d in range(16):
        bulk = jnp.full((16, 64), med[0, d], F32)
        light = jnp.full((16, 64), med[1, d], F32)
        pressure, flow_v, flow_w = ob[0, d, 8:24, :], ov[0, d], ov[1, d]
        table = level_weights(d, 16, True, True)
        dz_w = total(w * ov[1, d + k] for k, w in table.items())
        dz_p = total(w * ob[0, d + k, 8:24, :] for k, w in table.items())
        part = -bulk * (2.0 * unfold(1, d) + dz_w) + gravity * flow_w / light
        opre[d] = step_size * part
        rate_v = (-2.0 * step_size) * light * unfold(0, d)
        rate_w = -light * dz_p
        if d == 0:
            rate_w = rate_w - inv_norm * light * pressure
        rate_w = step_size * rate_w
        o_rate[2, d] = rate_v
        o_rate[3, d] = rate_w
        o_next[2, d] = flow_v + section_weight * rate_v
        o_next[3, d] = flow_w + section_weight * rate_w

    loads[5].wait()
    loads[6].wait()
    fine_x = lax.broadcasted_iota(jnp.int32, (24, 16), 1)
    coarse_x = lax.broadcasted_iota(jnp.int32, (24, 16), 0) + (8 * gx - 8)
    near_x = 8 * gx + fine_x // 2
    far_x = jnp.clip(near_x + ox[...], 0, 8 * nx - 1)
    blend_x = jnp.where(coarse_x == near_x, 0.75, 0.0) + jnp.where(coarse_x == far_x, 0.25, 0.0)
    fine_y = lax.broadcasted_iota(jnp.int32, (128, 64), 1)
    coarse_y = lax.broadcasted_iota(jnp.int32, (128, 64), 0)
    near_y = 128 * gy + 32 * gz + fine_y // 2
    far_y = jnp.clip(near_y + oy[...], 0, 128 * ny - 1)
    blend_y = jnp.where(coarse_y == lax.rem(near_y, 128), 0.75, 0.0)
    blend_y = blend_y + jnp.where(coarse_y == lax.rem(far_y, 128), 0.25, 0.0)

    landed(x_down, *up_copies, wave_up)
    landed(x_up, *down_copies, wave_down)
    for rim, row in ((xo_low, 6), (xo_high, 24)):
        for i in range(2):
            ob[i, :, row : row + 2, :] = rim[:, :, 64 * i : 64 * i + 64]

    pos = lax.broadcasted_iota(jnp.int32, (16, 64), 0)
    wp = weights(pos, 16, x_first, x_last, False)
    far_up, far_down = wp[3] != 0.0, wp[-3] != 0.0

    def dx_ocean(i, d):
        out = total(wp[k] * ob[i, d, 8 + k : 24 + k, :] for k in range(-2, 3))
        out = out + wp[3] * jnp.where(far_up, ob[i, d, 11:27, :], 0.0)
        return out + wp[-3] * jnp.where(far_down, ob[i, d, 5:21, :], 0.0)

    def ocean_out(i, d, rate):
        o_rate[i, d] = rate
        o_next[i, d] = ob[i, d, 8:24, :] + section_weight * rate

    for d in range(16):
        bulk = jnp.full((16, 64), (-2.0 * step_size) * med[0, d], F32)
        light = jnp.full((16, 64), (-2.0 * step_size) * med[1, d], F32)
        rate_p = opre[d] + bulk * dx_ocean(1, d)
        ocean_out(1, d, light * dx_ocean(0, d))
        if d < 15:
            ocean_out(0, d, rate_p)

    for e in (-1, 1):
        when(has[e], lambda: plane_wait(0, e))
        when(has_late[e], lambda: merge(e))

    window = plane[0].reshape(24, 128)
    bed_speed = lax.dot_general(
        blend_x, window, (((0,), (0,)), ((), ())), precision=HIGHEST, preferred_element_type=F32
    )
    bed_speed = jnp.dot(bed_speed, blend_y, precision=HIGHEST, preferred_element_type=F32)

    bulk = jnp.full((16, 64), (step_size * inv_norm) * med[0, 15], F32)
    ocean_out(0, 15, rate_p + bulk * (ov[1, 15] - bed_speed))

    sent(x_up, *up_copies, wave_up)
    sent(x_down, *down_copies, wave_down)
    for e in (-1, 1):
        sent(has_late[e], plane_on[e])
    sent(y_up, ys_copies[0])
    sent(y_down, ys_copies[1])
    sent(has_right, yo_copies[0])
    sent(has_left, yo_copies[1])
    sent(z_up, *z_up_copies)
    sent(z_down, *z_down_copies)
    for pred, copies in plane_late:
        sent(pred, *copies)
    for pred, copies in plane_early:
        sent(pred, *copies)
    for k in range(1, nz):
        sent(gz == k, coarse_copies[k - 1])


def finish_kernel(nx, o_next, o_rate, sb, mb, txs, dys, dzs, s_next_out, s_rate_out, o_next_out, o_rate_out, s_next, s_rate, sem):
    copies = [
        pltpu.make_async_copy(o_next, o_next_out, sem.at[0]),
        pltpu.make_async_copy(o_rate, o_rate_out, sem.at[1]),
    ]
    for copy in copies:
        copy.start()
    gx = lax.axis_index("gx")
    sub = lax.broadcasted_iota(jnp.int32, (8, 128), 0)
    wx = weights(sub, 8, gx == 0, gx == nx - 1, False)

    def dx(i, f, z):
        out = txs[i, z]
        for d in (-2, -1, 1, 2):
            out = out + wx[d] * sb[f, z, 8 + d : 16 + d, :]
        return out

    for z in range(8):
        own = [sb[f, z, 8:16, :] for f in range(9)]
        b, lam, mu = step_size * mb[0, z], step_size * mb[1, z], step_size * mb[2, z]
        d_x = {f: dx(i, f, z) for i, f in enumerate(x_fields)}
        d_y = {f: dys[i, z] for i, f in enumerate(y_fields)}
        d_z = {f: dzs[i, z] for i, f in enumerate(z_fields)}
        dilation = lam * (d_x[0] + d_y[1] + d_z[2])
        mu2 = 2.0 * mu
        rates = [
            b * (d_x[3] + d_y[8] + d_z[7]),
            b * (d_x[8] + d_y[4] + d_z[6]),
            b * (d_x[7] + d_y[6] + d_z[5]),
            dilation + mu2 * d_x[0],
            dilation + mu2 * d_y[1],
            dilation + mu2 * d_z[2],
            mu * (d_z[1] + d_y[2]),
            mu * (d_z[0] + d_x[2]),
            mu * (d_y[0] + d_x[1]),
        ]
        for f in range(9):
            s_rate[f, z] = rates[f]
            s_next[f, z] = own[f] + section_weight * rates[f]
        if z % 2 == 1:
            for i, (held, out) in enumerate(((s_next, s_next_out), (s_rate, s_rate_out))):
                copy = pltpu.make_async_copy(held.at[:, z - 1 : z + 1], out.at[:, z - 1 : z + 1], sem.at[1 + z + i])
                copy.start()
                copies.append(copy)
    for copy in copies:
        copy.wait()


def body(sizes, solid_state, material, ocean_state, ocean_medium, offset_x, offset_y):
    outs = (solid_state.shape, solid_state.shape, ocean_state.shape, ocean_state.shape)
    v = lambda *shape: pltpu.VMEM(shape, F32)
    held = pl.pallas_call(
        functools.partial(section_kernel, sizes),
        out_shape=[pltpu.VMEM(shape, F32) for shape in outs[2:]]
        + [v(9, 8, 24, 128), v(4, 8, 8, 128), v(6, 8, 8, 128), v(6, 8, 8, 128), v(6, 8, 8, 128)],
        in_specs=[pl.BlockSpec(memory_space=pltpu.HBM)] * 6,
        out_specs=[pl.BlockSpec(memory_space=pltpu.VMEM)] * 7,
        scratch_shapes=[
            v(2, 16, 32, 64), v(2, 16, 16, 64),
            pltpu.SMEM((2, 16), F32), pltpu.VMEM((1, 16), jnp.int32), pltpu.VMEM((1, 64), jnp.int32),
            v(6, 2, 8, 128), v(6, 2, 8, 128), v(2, 3, 8, 128), v(4, 8, 128),
            v(2, 16, 2, 128), v(16, 2, 128), v(16, 2, 128),
            v(2, 8, 128), v(2, 8, 128), v(2, 8, 128), v(2, 8, 128), v(2, 8, 128), v(2, 8, 128), v(8, 128),
            v(2, 16, 8, 128), v(16, 16, 64), v(2, 16, 8, 128),
            pltpu.SemaphoreType.DMA((8,)), pltpu.SemaphoreType.DMA((64,)), pltpu.SemaphoreType.DMA((24,)),
            pltpu.SemaphoreType.REGULAR((8,)),
        ],
        compiler_params=pltpu.CompilerParams(
            vmem_limit_bytes=16 * 2**20, collective_id=0, has_side_effects=True
        ),
        name="section",
    )(*(
        pltpu.with_memory_space_constraint(a, pltpu.HBM)
        for a in (solid_state, material, ocean_state, ocean_medium, offset_x.reshape(1, -1), offset_y.reshape(1, -1))
    ))
    return pl.pallas_call(
        functools.partial(finish_kernel, sizes[0]),
        out_shape=[jax.ShapeDtypeStruct(shape, F32) for shape in outs],
        in_specs=[pl.BlockSpec(memory_space=pltpu.VMEM)] * 7,
        out_specs=[pl.BlockSpec(memory_space=pl.ANY)] * 4,
        scratch_shapes=[v(*outs[0]), v(*outs[0]), pltpu.SemaphoreType.DMA((10,))],
        compiler_params=pltpu.CompilerParams(vmem_limit_bytes=4 * 2**20),
        name="finish",
    )(*held)


def solution(mesh):
    sizes = (mesh.shape["gx"], mesh.shape["gy"], mesh.shape["gz"])
    solid = P(None, "gz", "gx", "gy")
    ocean = P(None, None, "gx", ("gy", "gz"))
    return jax.shard_map(
        functools.partial(body, sizes),
        mesh=mesh,
        in_specs=(solid, solid, ocean, P(), P("gx"), P(("gy", "gz"))),
        out_specs=(solid, solid, ocean, ocean),
        check_vma=False,
    )
```

```python
import functools

import jax
import jax.numpy as jnp
from jax import lax
from jax.experimental import pallas as pl
from jax.experimental.pallas import tpu as pltpu
from jax.sharding import PartitionSpec as P

closure_rows = (
    (-24.0 / 17.0, 59.0 / 34.0, -4.0 / 17.0, -3.0 / 34.0, 0.0, 0.0),
    (-0.5, 0.0, 0.5, 0.0, 0.0, 0.0),
    (4.0 / 43.0, -59.0 / 86.0, 0.0, 59.0 / 86.0, -4.0 / 43.0, 0.0),
    (3.0 / 98.0, 0.0, -59.0 / 98.0, 0.0, 32.0 / 49.0, -4.0 / 49.0),
)
inner_row = {-2: 1.0 / 12.0, -1: -8.0 / 12.0, 1: 8.0 / 12.0, 2: -1.0 / 12.0}
inv_norm = 48.0 / 17.0
step_size = 0.25
section_weight = 0.1496590219993
gravity = 0.4

MESH = pl.DeviceIdType.MESH
F32 = jnp.float32
HIGHEST = lax.Precision.HIGHEST
REACH = range(-3, 4)

x_fields = (0, 1, 2, 3, 7, 8)
y_fields = (0, 1, 2, 4, 6, 8)
z_fields = (0, 1, 2, 5, 6, 7)


def low_weight(k, d):
    return closure_rows[k][k + d] if 0 <= k + d < 6 else 0.0


def high_weight(k, d):
    return -closure_rows[k][k - d] if 0 <= k - d < 6 else 0.0


def weights(pos, n, first, last, closed):
    at_low = pos + jnp.where(first, 0, 4096)
    at_high = (n - 1) - pos + jnp.where(last, 0, 4096)
    table = {}
    for d in REACH:
        w = jnp.full(pos.shape, inner_row.get(d, 0.0), F32)
        if closed and d < 0:
            w = jnp.where(pos + d >= 0, w, 0.0)
        if closed and d > 0:
            w = jnp.where(pos + d < n, w, 0.0)
        for k in range(4):
            w = jnp.where(at_low == k, low_weight(k, d), w)
            w = jnp.where(at_high == k, high_weight(k, d), w)
        table[d] = w
    return table


def level_weights(level, n, first, last):
    table = {}
    for d in REACH:
        w = inner_row.get(d, 0.0)
        if level < 4 and first is not False:
            c = low_weight(level, d)
            w = c if first is True else (jnp.where(first, c, w) if c != w else w)
        elif level >= n - 4 and last is not False:
            c = high_weight(n - 1 - level, d)
            w = c if last is True else (jnp.where(last, c, w) if c != w else w)
        if not (isinstance(w, float) and w == 0.0):
            table[d] = w
    return table


def total(terms):
    out = None
    for term in terms:
        out = term if out is None else out + term
    return out


def roll_lanes(x, shift):
    return pltpu.roll(x, shift % 128, x.ndim - 1)


def rim_from_sides(left, right, lane, first, last):
    s = lax.rem(lane, 4)
    twelfth = 1.0 / 12.0
    from_left = jnp.where(first, 0.0, twelfth)
    from_right = jnp.where(last, 0.0, twelfth)
    one_left = jnp.where(s >= 2, from_left, 0.0)
    eight_left = jnp.where(s == 2, -8.0 * from_left, 0.0)
    one_right = jnp.where(s < 2, -from_right, 0.0)
    eight_right = jnp.where(s == 1, 8.0 * from_right, 0.0)
    return (
        one_left * roll_lanes(left, 2)
        + eight_left * roll_lanes(left, 1)
        + one_right * roll_lanes(right, -2)
        + eight_right * roll_lanes(right, -1)
    )


def when(pred, action):
    @pl.when(pred)
    def _():
        action()


def start(pred, *copies):
    when(pred, lambda: [copy.start() for copy in copies] and None)


def landed(pred, *copies):
    when(pred, lambda: [copy.wait_recv() for copy in copies] and None)


def sent(pred, *copies):
    when(pred, lambda: [copy.wait_send() for copy in copies] and None)


def both(a, b):
    return jnp.logical_and(a, b)


def section_kernel(
    sizes,
    solid, material, ocean, medium, off_x, off_y,
    o_next, o_rate, sb, mb, txs, dys, dzs,
    ob, ov, med, ox, oy,
    z_low, z_high, plane, bed_part,
    xo_out, xo_low, xo_high, ys_out, ys_left, ys_right, yo_out, yo_left, yo_right, coarse_out,
    dyo, opre, cat,
    local_sem, send_sem, recv_sem, there,
):
    nx, ny, nz = sizes
    gx, gy, gz = lax.axis_index("gx"), lax.axis_index("gy"), lax.axis_index("gz")
    up_x, down_x = lax.rem(gx + 1, nx), lax.rem(gx + nx - 1, nx)
    up_y, down_y = lax.rem(gy + 1, ny), lax.rem(gy + ny - 1, ny)
    x_first, x_last = gx == 0, gx == nx - 1
    y_first, y_last = gy == 0, gy == ny - 1
    z_first, z_last = gz == 0, gz == nz - 1
    right = (gx, jnp.where(z_last, up_y, gy), jnp.where(z_last, 0, gz + 1))
    left = (gx, jnp.where(z_first, down_y, gy), jnp.where(z_first, nz - 1, gz - 1))
    xs = {-1: down_x, 0: gx, 1: up_x}

    x_down, x_up = gx > 0, gx < nx - 1
    y_down, y_up = gy > 0, gy < ny - 1
    z_down, z_up = gz > 0, gz < nz - 1
    has_left, has_right = jnp.logical_or(y_down, z_down), jnp.logical_or(y_up, z_up)
    has = {-1: x_down, 1: x_up}

    run = max(nx // 4, 2)
    turn = lax.rem(gx, run)
    late = {1: turn < run // 2, -1: jnp.logical_or(turn == 0, turn > run // 2)}
    has_late = {e: both(has[e], late[e]) for e in (-1, 1)}
    has_early = {e: both(has[e], jnp.logical_not(late[e])) for e in (-1, 1)}
    far_up, far_down = both(y_up, gy == ny - 2), both(y_down, gy == ny - 1)
    y_up_word, y_down_word = both(far_up, gz < 2), both(far_down, gz < 2)
    y_up_near, y_down_near = both(y_up, jnp.logical_not(y_up_word)), both(y_down, jnp.logical_not(y_down_word))
    odd = lax.rem(gz, 2) == 1
    even = jnp.logical_not(odd)
    barrier = pltpu.get_barrier_semaphore()

    def greet(x, y, z):
        pl.semaphore_signal(barrier, inc=1, device_id=(x, y, z), device_id_type=MESH)

    def tell(index, x, y, z):
        pl.semaphore_signal(there.at[index], inc=1, device_id=(x, y, z), device_id_type=MESH)

    plane[...] = jnp.zeros_like(plane)
    when(y_up_near, lambda: greet(gx, up_y, gz))
    for e in (-1, 1):
        when(has_late[e], lambda: greet(xs[e], gy, gz))
    when(odd, lambda: greet(gx, gy, gz - 1))
    when(gz < 2, lambda: greet(gx, gy, 2))
    for e in (-1, 1):
        when(both(has_late[e], z_down), lambda: greet(xs[e], gy, 0))
        when(both(has_late[e], both(z_first, y_down)), lambda: greet(xs[e], down_y, 0))
        when(both(has_late[e], both(z_last, y_up)), lambda: greet(xs[e], up_y, 0))

    loads = [
        pltpu.make_async_copy(src, dst, local_sem.at[i])
        for i, (src, dst) in enumerate(
            (
                (solid, sb.at[:, :, 8:16]),
                (ocean.at[0:2], ob.at[:, :, 8:24]),
                (ocean.at[2:4], ov),
                (material, mb),
                (medium, med),
                (off_x, ox),
                (off_y, oy),
            )
        )
    ]
    for i in (1, 0, 2, 3, 4, 5, 6):
        loads[i].start()

    def clear(*places):
        for ref in places:
            ref[...] = jnp.zeros(ref.shape, F32)

    when(z_first, lambda: clear(z_low))
    when(z_last, lambda: clear(z_high))
    when(x_first, lambda: clear(sb.at[:, :, 6:8], xo_low))
    when(x_last, lambda: clear(sb.at[:, :, 16:18], xo_high))
    when(y_first, lambda: clear(ys_left))
    when(y_last, lambda: clear(ys_right))
    when(jnp.logical_not(has_left), lambda: clear(yo_left))
    when(jnp.logical_not(has_right), lambda: clear(yo_right))

    def count(*preds):
        return sum(jnp.where(p, 1, 0) for p in preds)

    n_early = count(*has_early.values())
    n_y = count(y_down, y_up)
    n_greet = count(y_down_near, even) + jnp.where(gz == 2, 2, 0)
    n_greet = n_greet + n_early * (1 + jnp.where(z_first, nz - 1 + n_y, 0))
    when(n_greet > 0, lambda: pl.semaphore_wait(barrier, n_greet))
    def await_partner(pred, index, amount=1):
        when(pred, lambda: pl.semaphore_wait(there.at[index], amount))

    counter = iter(range(64))

    def remote(src, dst, recv, device):
        return pltpu.make_async_remote_copy(
            src_ref=src, dst_ref=dst, send_sem=send_sem.at[next(counter)], recv_sem=recv_sem.at[recv],
            device_id=device, device_id_type=MESH,
        )

    up_copies, down_copies = [], []
    for i, (a, b) in enumerate(((0, 4), (7, 9))):
        up_copies.append(remote(solid.at[a:b, :, 6:8], sb.at[a:b, :, 6:8], 2 * i, (up_x, gy, gz)))
        down_copies.append(remote(solid.at[a:b, :, 0:2], sb.at[a:b, :, 16:18], 2 * i + 1, (down_x, gy, gz)))
    wave_up = remote(xo_out.at[1], xo_low, 4, (up_x, gy, gz))
    wave_down = remote(xo_out.at[0], xo_high, 5, (down_x, gy, gz))
    start(has_early[1], up_copies[0])
    start(has_early[-1], down_copies[0])
    for e, index in ((1, 1), (-1, 0)):
        when(has_early[e], lambda: tell(index, xs[e], gy, gz))
    when(y_down_near, lambda: tell(2, gx, down_y, gz))
    when(gz == 2, lambda: tell(3, gx, gy, 1))
    when(even, lambda: tell(4, gx, gy, gz + 1))
    when(gz == 2, lambda: tell(5, gx, gy, 0))

    z_up_copies = [
        remote(solid.at[a : a + 3, 6:8], z_low.at[b : b + 3], 6 + i, (gx, gy, gz + 1))
        for i, (a, b) in enumerate(((0, 0), (5, 3)))
    ]
    z_down_copies = [
        remote(solid.at[a : a + 3, 0:2], z_high.at[b : b + 3], 8 + i, (gx, gy, gz - 1))
        for i, (a, b) in enumerate(((0, 0), (5, 3)))
    ]

    tile = solid.at[2, 0]
    plane_early, plane_late = [], []
    rows = {-1: slice(7, 8), 0: slice(0, 8), 1: slice(0, 1)}
    for e in (-1, 0, 1):
        x, r = xs[-e], rows[e]
        part = solid.at[2, 0, r]
        mine = [remote(part, plane.at[0, e + 1, r], 10 + e + 1, (x, gy, k)) for k in range(1 if e == 0 else 0, nz)]
        above = remote(part, plane.at[1, e + 1, r], 13 + e + 1, (x, up_y, 0))
        below = remote(part, plane.at[1, e + 1, r], 13 + e + 1, (x, down_y, nz - 1))
        if e == 0:
            plane_early += [(z_first, mine[:1])]
            plane_late += [(z_first, mine[1:]), (both(z_first, y_up), [above]), (both(z_first, y_down), [below])]
        else:
            pred = both(z_first, has_early[-e])
            plane_early += [(pred, mine), (both(pred, y_up), [above]), (both(pred, y_down), [below])]
    plane_on = {
        e: remote(plane.at[0, 1, rows[-e]], plane.at[0, 1 - e, rows[-e]], 11 - e, (xs[e], gy, gz)) for e in (-1, 1)
    }
    own_plane = pltpu.make_async_copy(tile, plane.at[0, 1], local_sem.at[7])
    when(z_first, own_plane.start)
    for pred, copies in plane_early:
        start(pred, *copies)

    start(has_early[1], up_copies[1])
    start(has_early[-1], down_copies[1])

    lane = lax.broadcasted_iota(jnp.int32, (8, 128), 1)

    loads[1].wait()
    for end, row in ((0, 8), (1, 22)):
        xo_out[end] = jnp.concatenate([ob[0, :, row : row + 2, :], ob[1, :, row : row + 2, :]], axis=2)
    start(has_early[1], wave_up)
    start(has_early[-1], wave_down)

    loads[0].wait()
    for half, fields in enumerate((y_fields[:4], y_fields[4:])):
        packed = jnp.zeros((8, 128), F32)
        for i, f in enumerate(fields):
            for z in range(8):
                k = 8 * i + z
                packed = jnp.where(lane // 4 == k, roll_lanes(sb[f, z, 8:16, :], 4 * k + 2), packed)
        ys_out[half] = packed
    ys_copies = [
        remote(ys_out, ys_left, 16, (gx, up_y, gz)),
        remote(ys_out, ys_right, 17, (gx, down_y, gz)),
    ]
    start(y_down_near, ys_copies[1])

    loads[2].wait()
    half_lane = lax.rem(lane, 64)
    for i in range(2):
        packed = jnp.zeros((8, 128), F32)
        for d in range(16):
            if i == 0:
                folded = jnp.concatenate([ob[0, d, 8:16, :], ob[0, d, 16:24, :]], axis=1)
            else:
                folded = jnp.concatenate([ov[0, d, 0:8, :], ov[0, d, 8:16, :]], axis=1)
            cat[i, d] = folded
            packed = jnp.where(half_lane // 4 == d, roll_lanes(folded, 4 * d + 2), packed)
        yo_out[i] = packed
    yo_copies = [remote(yo_out, yo_left, 18, right), remote(yo_out, yo_right, 19, left)]
    start(both(even, has_right), yo_copies[0])
    start(gz == 2, yo_copies[1])

    row = lax.broadcasted_iota(jnp.int32, (8, 16), 0)
    col = lax.broadcasted_iota(jnp.int32, (8, 16), 1)
    pair = jnp.where(col // 2 == row, 0.5, 0.0)
    fine = lax.broadcasted_iota(jnp.int32, (64, 128), 0)
    out_lane = lax.broadcasted_iota(jnp.int32, (64, 128), 1)
    place = jnp.where(out_lane == 32 * gz + fine // 2, 0.5, 0.0)
    coarse = jnp.dot(pair, ob[0, 15, 8:24, :], precision=HIGHEST, preferred_element_type=F32)
    coarse = jnp.dot(coarse, place, precision=HIGHEST, preferred_element_type=F32)
    coarse_out[...] = coarse
    coarse_copies = [remote(coarse_out, bed_part.at[k], 20 + k, (gx, gy, 0)) for k in range(1, nz)]
    start(gz == 2, coarse_copies[1])

    wy = weights(lane, 128, y_first, y_last, True)
    for i, f in enumerate(y_fields):
        own = sb[f, :, 8:16, :]
        dys[i] = total(wy[d] * (roll_lanes(own, -d) if d else own) for d in REACH)
    wo = weights(half_lane, 64, jnp.logical_and(y_first, z_first), jnp.logical_and(y_last, z_last), True)
    for i in range(2):
        for d0 in range(0, 16, 8):
            own = cat[i, d0 : d0 + 8]
            dyo[i, d0 : d0 + 8] = total(wo[d] * (roll_lanes(own, -d) if d else own) for d in REACH)
    sub = lax.broadcasted_iota(jnp.int32, (8, 128), 0)
    wx = weights(sub, 8, x_first, x_last, False)
    for i, f in enumerate(x_fields):
        own = sb[f, :, 8:16, :]
        txs[i] = wx[0] * own + wx[3] * pltpu.roll(own, 5, 1) + wx[-3] * pltpu.roll(own, 3, 1)

    start(even, *z_up_copies)
    start(gz == 2, *z_down_copies)
    await_partner(odd, 4)
    start(odd, *z_down_copies, yo_copies[1])
    for k in (1, 3):
        start(gz == k, coarse_copies[k - 1])
    await_partner(gz == 1, 3)
    start(gz == 1, *z_up_copies, yo_copies[0])
    await_partner(z_first, 5)
    start(*plane_late[0][:1], *plane_late[0][1])
    await_partner(y_up_near, 2)
    near_link = both(z_first, y_up_near)
    far_link = both(far_up, gz == 2)
    when(jnp.logical_or(near_link, far_link), lambda: tell(7, gx, gy, nz - 1))
    when(jnp.logical_or(near_link, far_link), lambda: tell(6, gx, up_y, 0))
    when(far_link, lambda: tell(6, gx, up_y, 1))
    for k in (0, 1):
        when(far_link, lambda: tell(7, gx, gy, k))
    await_partner(y_up_word, 7)
    start(y_up, ys_copies[0])
    start(*plane_late[1][:1], *plane_late[1][1])
    await_partner(jnp.logical_or(both(z_first, y_down), y_down_word), 6)
    start(y_down_word, ys_copies[1])
    start(both(z_first, y_down), yo_copies[1], *plane_late[2][1])
    await_partner(both(z_last, y_up), 7)
    start(both(z_last, y_up), yo_copies[0])
    for e, index, copies in ((1, 0, up_copies + [wave_up]), (-1, 1, down_copies + [wave_down])):
        await_partner(has_late[e], index)
        start(has_late[e], *copies)
    sides = ((both(z_first, y_down), 127), (both(z_last, y_up), 0))

    def plane_wait(s, e):
        pltpu.make_async_remote_copy(
            src_ref=solid.at[2, 0, rows[e]], dst_ref=plane.at[s, e + 1, rows[e]], send_sem=send_sem.at[63], recv_sem=recv_sem.at[10 + 3 * s + e + 1],
            device_id=(gx, up_y, gz), device_id_type=MESH,
        ).wait_recv()

    def merge(e):
        for pred, at in sides:

            @pl.when(pred)
            def _(at=at):
                plane_wait(1, e)
                plane[0, e + 1] = jnp.where(lane == at, plane[1, e + 1], plane[0, e + 1])

    when(z_first, own_plane.wait)
    when(z_down, lambda: plane_wait(0, 0))
    merge(0)
    for e in (-1, 1):
        start(has_late[e], plane_on[e])

    landed(y_down, ys_copies[0])
    landed(y_up, ys_copies[1])
    at_edge = jnp.logical_or(lane < 2, lane >= 126)
    for half, fields in enumerate((y_fields[:4], y_fields[4:])):
        rim = rim_from_sides(ys_left[half], ys_right[half], lane, y_first, y_last)
        for i in range(len(fields)):
            for z in range(8):
                k = 8 * i + z
                dys[4 * half + i, z] += jnp.where(at_edge, roll_lanes(rim, -4 * k - 2), 0.0)
    landed(has_left, yo_copies[0])
    landed(has_right, yo_copies[1])
    at_half_edge = jnp.logical_or(half_lane < 2, half_lane >= 62)
    for i in range(2):
        rim = rim_from_sides(
            roll_lanes(yo_left[i], 64), roll_lanes(yo_right[i], 64), lane,
            jnp.logical_and(y_first, z_first), jnp.logical_and(y_last, z_last),
        )
        for d in range(16):
            dyo[i, d] += jnp.where(at_half_edge, roll_lanes(rim, -4 * d - 2), 0.0)

    loads[3].wait()

    landed(z_down, *z_up_copies)
    landed(z_up, *z_down_copies)

    for i, f in enumerate(z_fields):
        def level(z, i=i, f=f):
            if z < 0:
                return z_low[i, z + 2]
            if z >= 8:
                return z_high[i, z - 8]
            return sb[f, z, 8:16, :]

        for z in range(8):
            table = level_weights(z, 8, z_first, z_last)
            dzs[i, z] = mb[3, z] * total(w * level(z + d) for d, w in table.items() if -2 <= z + d < 10)

    @pl.when(z_first)
    def _():
        for k in range(1, nz):
            pltpu.make_async_remote_copy(
                src_ref=coarse_out, dst_ref=bed_part.at[k], send_sem=send_sem.at[63], recv_sem=recv_sem.at[20 + k],
                device_id=(gx, up_y, gz), device_id_type=MESH,
            ).wait_recv()
        scale = inv_norm * mb[3, 0]
        bed_pressure = coarse_out[...] + total(bed_part[k] for k in range(1, nz))
        dzs[5, 0] += scale * sb[7, 0, 8:16, :]
        dzs[4, 0] += scale * sb[6, 0, 8:16, :]
        dzs[3, 0] += scale * (sb[5, 0, 8:16, :] + bed_pressure)

    loads[4].wait()

    def unfold(i, d):
        folded = dyo[i, d]
        return jnp.concatenate([folded[:, 0:64], folded[:, 64:128]], axis=0)

    for d in range(16):
        bulk = jnp.full((16, 64), med[0, d], F32)
        light = jnp.full((16, 64), med[1, d], F32)
        pressure, flow_v, flow_w = ob[0, d, 8:24, :], ov[0, d], ov[1, d]
        table = level_weights(d, 16, True, True)
        dz_w = total(w * ov[1, d + k] for k, w in table.items())
        dz_p = total(w * ob[0, d + k, 8:24, :] for k, w in table.items())
        part = -bulk * (2.0 * unfold(1, d) + dz_w) + gravity * flow_w / light
        opre[d] = step_size * part
        rate_v = (-2.0 * step_size) * light * unfold(0, d)
        rate_w = -light * dz_p
        if d == 0:
            rate_w = rate_w - inv_norm * light * pressure
        rate_w = step_size * rate_w
        o_rate[2, d] = rate_v
        o_rate[3, d] = rate_w
        o_next[2, d] = flow_v + section_weight * rate_v
        o_next[3, d] = flow_w + section_weight * rate_w

    loads[5].wait()
    loads[6].wait()
    fine_x = lax.broadcasted_iota(jnp.int32, (24, 16), 1)
    coarse_x = lax.broadcasted_iota(jnp.int32, (24, 16), 0) + (8 * gx - 8)
    near_x = 8 * gx + fine_x // 2
    far_x = jnp.clip(near_x + ox[...], 0, 8 * nx - 1)
    blend_x = jnp.where(coarse_x == near_x, 0.75, 0.0) + jnp.where(coarse_x == far_x, 0.25, 0.0)
    fine_y = lax.broadcasted_iota(jnp.int32, (128, 64), 1)
    coarse_y = lax.broadcasted_iota(jnp.int32, (128, 64), 0)
    near_y = 128 * gy + 32 * gz + fine_y // 2
    far_y = jnp.clip(near_y + oy[...], 0, 128 * ny - 1)
    blend_y = jnp.where(coarse_y == lax.rem(near_y, 128), 0.75, 0.0)
    blend_y = blend_y + jnp.where(coarse_y == lax.rem(far_y, 128), 0.25, 0.0)

    landed(x_down, *up_copies, wave_up)
    landed(x_up, *down_copies, wave_down)
    for rim, row in ((xo_low, 6), (xo_high, 24)):
        for i in range(2):
            ob[i, :, row : row + 2, :] = rim[:, :, 64 * i : 64 * i + 64]

    pos = lax.broadcasted_iota(jnp.int32, (16, 64), 0)
    wp = weights(pos, 16, x_first, x_last, False)
    far_up, far_down = wp[3] != 0.0, wp[-3] != 0.0

    def dx_ocean(i, d):
        out = total(wp[k] * ob[i, d, 8 + k : 24 + k, :] for k in range(-2, 3))
        out = out + wp[3] * jnp.where(far_up, ob[i, d, 11:27, :], 0.0)
        return out + wp[-3] * jnp.where(far_down, ob[i, d, 5:21, :], 0.0)

    def ocean_out(i, d, rate):
        o_rate[i, d] = rate
        o_next[i, d] = ob[i, d, 8:24, :] + section_weight * rate

    for d in range(16):
        bulk = jnp.full((16, 64), (-2.0 * step_size) * med[0, d], F32)
        light = jnp.full((16, 64), (-2.0 * step_size) * med[1, d], F32)
        rate_p = opre[d] + bulk * dx_ocean(1, d)
        ocean_out(1, d, light * dx_ocean(0, d))
        if d < 15:
            ocean_out(0, d, rate_p)

    for e in (-1, 1):
        when(has[e], lambda: plane_wait(0, e))
        when(has_late[e], lambda: merge(e))

    window = plane[0].reshape(24, 128)
    bed_speed = lax.dot_general(
        blend_x, window, (((0,), (0,)), ((), ())), precision=HIGHEST, preferred_element_type=F32
    )
    bed_speed = jnp.dot(bed_speed, blend_y, precision=HIGHEST, preferred_element_type=F32)

    bulk = jnp.full((16, 64), (step_size * inv_norm) * med[0, 15], F32)
    ocean_out(0, 15, rate_p + bulk * (ov[1, 15] - bed_speed))

    sent(x_up, *up_copies, wave_up)
    sent(x_down, *down_copies, wave_down)
    for e in (-1, 1):
        sent(has_late[e], plane_on[e])
    sent(y_up, ys_copies[0])
    sent(y_down, ys_copies[1])
    sent(has_right, yo_copies[0])
    sent(has_left, yo_copies[1])
    sent(z_up, *z_up_copies)
    sent(z_down, *z_down_copies)
    for pred, copies in plane_late:
        sent(pred, *copies)
    for pred, copies in plane_early:
        sent(pred, *copies)
    for k in range(1, nz):
        sent(gz == k, coarse_copies[k - 1])


def finish_kernel(nx, o_next, o_rate, sb, mb, txs, dys, dzs, s_next_out, s_rate_out, o_next_out, o_rate_out, s_next, s_rate, sem):
    copies = [
        pltpu.make_async_copy(o_next, o_next_out, sem.at[0]),
        pltpu.make_async_copy(o_rate, o_rate_out, sem.at[1]),
    ]
    for copy in copies:
        copy.start()
    gx = lax.axis_index("gx")
    sub = lax.broadcasted_iota(jnp.int32, (8, 128), 0)
    wx = weights(sub, 8, gx == 0, gx == nx - 1, False)

    def dx(i, f, z):
        out = txs[i, z]
        for d in (-2, -1, 1, 2):
            out = out + wx[d] * sb[f, z, 8 + d : 16 + d, :]
        return out

    for z in range(8):
        own = [sb[f, z, 8:16, :] for f in range(9)]
        b, lam, mu = step_size * mb[0, z], step_size * mb[1, z], step_size * mb[2, z]
        d_x = {f: dx(i, f, z) for i, f in enumerate(x_fields)}
        d_y = {f: dys[i, z] for i, f in enumerate(y_fields)}
        d_z = {f: dzs[i, z] for i, f in enumerate(z_fields)}
        dilation = lam * (d_x[0] + d_y[1] + d_z[2])
        mu2 = 2.0 * mu
        rates = [
            b * (d_x[3] + d_y[8] + d_z[7]),
            b * (d_x[8] + d_y[4] + d_z[6]),
            b * (d_x[7] + d_y[6] + d_z[5]),
            dilation + mu2 * d_x[0],
            dilation + mu2 * d_y[1],
            dilation + mu2 * d_z[2],
            mu * (d_z[1] + d_y[2]),
            mu * (d_z[0] + d_x[2]),
            mu * (d_y[0] + d_x[1]),
        ]
        for f in range(9):
            s_rate[f, z] = rates[f]
            s_next[f, z] = own[f] + section_weight * rates[f]
        if z % 2 == 1:
            for i, (held, out) in enumerate(((s_next, s_next_out), (s_rate, s_rate_out))):
                copy = pltpu.make_async_copy(held.at[:, z - 1 : z + 1], out.at[:, z - 1 : z + 1], sem.at[1 + z + i])
                copy.start()
                copies.append(copy)
    for copy in copies:
        copy.wait()


def body(sizes, solid_state, material, ocean_state, ocean_medium, offset_x, offset_y):
    outs = (solid_state.shape, solid_state.shape, ocean_state.shape, ocean_state.shape)
    v = lambda *shape: pltpu.VMEM(shape, F32)
    held = pl.pallas_call(
        functools.partial(section_kernel, sizes),
        out_shape=[pltpu.VMEM(shape, F32) for shape in outs[2:]]
        + [v(9, 8, 24, 128), v(4, 8, 8, 128), v(6, 8, 8, 128), v(6, 8, 8, 128), v(6, 8, 8, 128)],
        in_specs=[pl.BlockSpec(memory_space=pltpu.HBM)] * 6,
        out_specs=[pl.BlockSpec(memory_space=pltpu.VMEM)] * 7,
        scratch_shapes=[
            v(2, 16, 32, 64), v(2, 16, 16, 64),
            pltpu.SMEM((2, 16), F32), pltpu.VMEM((1, 16), jnp.int32), pltpu.VMEM((1, 64), jnp.int32),
            v(6, 2, 8, 128), v(6, 2, 8, 128), v(2, 3, 8, 128), v(4, 8, 128),
            v(2, 16, 2, 128), v(16, 2, 128), v(16, 2, 128),
            v(2, 8, 128), v(2, 8, 128), v(2, 8, 128), v(2, 8, 128), v(2, 8, 128), v(2, 8, 128), v(8, 128),
            v(2, 16, 8, 128), v(16, 16, 64), v(2, 16, 8, 128),
            pltpu.SemaphoreType.DMA((8,)), pltpu.SemaphoreType.DMA((64,)), pltpu.SemaphoreType.DMA((24,)),
            pltpu.SemaphoreType.REGULAR((8,)),
        ],
        compiler_params=pltpu.CompilerParams(
            vmem_limit_bytes=16 * 2**20, collective_id=0, has_side_effects=True
        ),
        name="section",
    )(*(
        pltpu.with_memory_space_constraint(a, pltpu.HBM)
        for a in (solid_state, material, ocean_state, ocean_medium, offset_x.reshape(1, -1), offset_y.reshape(1, -1))
    ))
    return pl.pallas_call(
        functools.partial(finish_kernel, sizes[0]),
        out_shape=[jax.ShapeDtypeStruct(shape, F32) for shape in outs],
        in_specs=[pl.BlockSpec(memory_space=pltpu.VMEM)] * 7,
        out_specs=[pl.BlockSpec(memory_space=pl.ANY)] * 4,
        scratch_shapes=[v(*outs[0]), v(*outs[0]), pltpu.SemaphoreType.DMA((10,))],
        compiler_params=pltpu.CompilerParams(vmem_limit_bytes=4 * 2**20),
        name="finish",
    )(*held)


def solution(mesh):
    sizes = (mesh.shape["gx"], mesh.shape["gy"], mesh.shape["gz"])
    solid = P(None, "gz", "gx", "gy")
    ocean = P(None, None, "gx", ("gy", "gz"))
    return jax.shard_map(
        functools.partial(body, sizes),
        mesh=mesh,
        in_specs=(solid, solid, ocean, P(), P("gx"), P(("gy", "gz"))),
        out_specs=(solid, solid, ocean, ocean),
        check_vma=False,
    )
```

```python
import functools

import jax
import jax.numpy as jnp
from jax import lax
from jax.experimental import pallas as pl
from jax.experimental.pallas import tpu as pltpu
from jax.sharding import PartitionSpec as P

closure_rows = (
    (-24.0 / 17.0, 59.0 / 34.0, -4.0 / 17.0, -3.0 / 34.0, 0.0, 0.0),
    (-0.5, 0.0, 0.5, 0.0, 0.0, 0.0),
    (4.0 / 43.0, -59.0 / 86.0, 0.0, 59.0 / 86.0, -4.0 / 43.0, 0.0),
    (3.0 / 98.0, 0.0, -59.0 / 98.0, 0.0, 32.0 / 49.0, -4.0 / 49.0),
)
inner_row = {-2: 1.0 / 12.0, -1: -8.0 / 12.0, 1: 8.0 / 12.0, 2: -1.0 / 12.0}
inv_norm = 48.0 / 17.0
step_size = 0.25
section_weight = 0.1496590219993
gravity = 0.4

MESH = pl.DeviceIdType.MESH
F32 = jnp.float32
HIGHEST = lax.Precision.HIGHEST
REACH = range(-3, 4)

x_fields = (0, 1, 2, 3, 7, 8)
y_fields = (0, 1, 2, 4, 6, 8)
z_fields = (0, 1, 2, 5, 6, 7)


def low_weight(k, d):
    return closure_rows[k][k + d] if 0 <= k + d < 6 else 0.0


def high_weight(k, d):
    return -closure_rows[k][k - d] if 0 <= k - d < 6 else 0.0


def weights(pos, n, first, last, closed):
    at_low = pos + jnp.where(first, 0, 4096)
    at_high = (n - 1) - pos + jnp.where(last, 0, 4096)
    table = {}
    for d in REACH:
        w = jnp.full(pos.shape, inner_row.get(d, 0.0), F32)
        if closed and d < 0:
            w = jnp.where(pos + d >= 0, w, 0.0)
        if closed and d > 0:
            w = jnp.where(pos + d < n, w, 0.0)
        for k in range(4):
            w = jnp.where(at_low == k, low_weight(k, d), w)
            w = jnp.where(at_high == k, high_weight(k, d), w)
        table[d] = w
    return table


def level_weights(level, n, first, last):
    table = {}
    for d in REACH:
        w = inner_row.get(d, 0.0)
        if level < 4 and first is not False:
            c = low_weight(level, d)
            w = c if first is True else (jnp.where(first, c, w) if c != w else w)
        elif level >= n - 4 and last is not False:
            c = high_weight(n - 1 - level, d)
            w = c if last is True else (jnp.where(last, c, w) if c != w else w)
        if not (isinstance(w, float) and w == 0.0):
            table[d] = w
    return table


def total(terms):
    out = None
    for term in terms:
        out = term if out is None else out + term
    return out


def roll_lanes(x, shift):
    return pltpu.roll(x, shift % 128, x.ndim - 1)


def rim_from_sides(left, right, lane, first, last):
    s = lax.rem(lane, 4)
    twelfth = 1.0 / 12.0
    from_left = jnp.where(first, 0.0, twelfth)
    from_right = jnp.where(last, 0.0, twelfth)
    one_left = jnp.where(s >= 2, from_left, 0.0)
    eight_left = jnp.where(s == 2, -8.0 * from_left, 0.0)
    one_right = jnp.where(s < 2, -from_right, 0.0)
    eight_right = jnp.where(s == 1, 8.0 * from_right, 0.0)
    return (
        one_left * roll_lanes(left, 2)
        + eight_left * roll_lanes(left, 1)
        + one_right * roll_lanes(right, -2)
        + eight_right * roll_lanes(right, -1)
    )


def when(pred, action):
    @pl.when(pred)
    def _():
        action()


def start(pred, *copies):
    when(pred, lambda: [copy.start() for copy in copies] and None)


def landed(pred, *copies):
    when(pred, lambda: [copy.wait_recv() for copy in copies] and None)


def sent(pred, *copies):
    when(pred, lambda: [copy.wait_send() for copy in copies] and None)


def both(a, b):
    return jnp.logical_and(a, b)


def section_kernel(
    sizes,
    solid, material, ocean, medium, off_x, off_y,
    o_next, o_rate, sb, mb, txs, dys, dzs,
    ob, ov, med, ox, oy,
    z_low, z_high, plane, bed_part,
    xo_out, xo_low, xo_high, ys_out, ys_left, ys_right, yo_out, yo_left, yo_right, coarse_out,
    dyo, opre, cat,
    local_sem, send_sem, recv_sem, there,
):
    nx, ny, nz = sizes
    gx, gy, gz = lax.axis_index("gx"), lax.axis_index("gy"), lax.axis_index("gz")
    up_x, down_x = lax.rem(gx + 1, nx), lax.rem(gx + nx - 1, nx)
    up_y, down_y = lax.rem(gy + 1, ny), lax.rem(gy + ny - 1, ny)
    x_first, x_last = gx == 0, gx == nx - 1
    y_first, y_last = gy == 0, gy == ny - 1
    z_first, z_last = gz == 0, gz == nz - 1
    right = (gx, jnp.where(z_last, up_y, gy), jnp.where(z_last, 0, gz + 1))
    left = (gx, jnp.where(z_first, down_y, gy), jnp.where(z_first, nz - 1, gz - 1))
    xs = {-1: down_x, 0: gx, 1: up_x}

    x_down, x_up = gx > 0, gx < nx - 1
    y_down, y_up = gy > 0, gy < ny - 1
    z_down, z_up = gz > 0, gz < nz - 1
    has_left, has_right = jnp.logical_or(y_down, z_down), jnp.logical_or(y_up, z_up)
    has = {-1: x_down, 1: x_up}

    run = max(nx // 4, 2)
    turn = lax.rem(gx, run)
    late = {1: turn < run // 2, -1: jnp.logical_or(turn == 0, turn > run // 2)}
    has_late = {e: both(has[e], late[e]) for e in (-1, 1)}
    has_early = {e: both(has[e], jnp.logical_not(late[e])) for e in (-1, 1)}
    far_up, far_down = both(y_up, gy == ny - 2), both(y_down, gy == ny - 1)
    y_up_word, y_down_word = both(far_up, gz < 2), both(far_down, gz < 2)
    y_up_near, y_down_near = both(y_up, jnp.logical_not(y_up_word)), both(y_down, jnp.logical_not(y_down_word))
    odd = lax.rem(gz, 2) == 1
    even = jnp.logical_not(odd)
    barrier = pltpu.get_barrier_semaphore()

    def greet(x, y, z):
        pl.semaphore_signal(barrier, inc=1, device_id=(x, y, z), device_id_type=MESH)

    def tell(index, x, y, z):
        pl.semaphore_signal(there.at[index], inc=1, device_id=(x, y, z), device_id_type=MESH)

    plane[...] = jnp.zeros_like(plane)
    when(y_up_near, lambda: greet(gx, up_y, gz))
    for e in (-1, 1):
        when(has_late[e], lambda: greet(xs[e], gy, gz))
    when(odd, lambda: greet(gx, gy, gz - 1))
    when(gz < 2, lambda: greet(gx, gy, 2))
    for e in (-1, 1):
        when(both(has_late[e], z_down), lambda: greet(xs[e], gy, 0))
        when(both(has_late[e], both(z_first, y_down)), lambda: greet(xs[e], down_y, 0))
        when(both(has_late[e], both(z_last, y_up)), lambda: greet(xs[e], up_y, 0))

    loads = [
        pltpu.make_async_copy(src, dst, local_sem.at[i])
        for i, (src, dst) in enumerate(
            (
                (solid, sb.at[:, :, 8:16]),
                (ocean.at[0:2], ob.at[:, :, 8:24]),
                (ocean.at[2:4], ov),
                (material, mb),
                (medium, med),
                (off_x, ox),
                (off_y, oy),
            )
        )
    ]
    for i in (1, 0, 2, 3, 4, 5, 6):
        loads[i].start()

    def clear(*places):
        for ref in places:
            ref[...] = jnp.zeros(ref.shape, F32)

    when(z_first, lambda: clear(z_low))
    when(z_last, lambda: clear(z_high))
    when(x_first, lambda: clear(sb.at[:, :, 6:8], xo_low))
    when(x_last, lambda: clear(sb.at[:, :, 16:18], xo_high))
    when(y_first, lambda: clear(ys_left))
    when(y_last, lambda: clear(ys_right))
    when(jnp.logical_not(has_left), lambda: clear(yo_left))
    when(jnp.logical_not(has_right), lambda: clear(yo_right))

    def count(*preds):
        return sum(jnp.where(p, 1, 0) for p in preds)

    n_early = count(*has_early.values())
    n_y = count(y_down, y_up)
    n_greet = count(y_down_near, even) + jnp.where(gz == 2, 2, 0)
    n_greet = n_greet + n_early * (1 + jnp.where(z_first, nz - 1 + n_y, 0))
    when(n_greet > 0, lambda: pl.semaphore_wait(barrier, n_greet))
    for e, index in ((1, 1), (-1, 0)):
        when(has_early[e], lambda: tell(index, xs[e], gy, gz))
    when(y_down_near, lambda: tell(2, gx, down_y, gz))
    when(gz == 2, lambda: tell(3, gx, gy, 1))
    when(even, lambda: tell(4, gx, gy, gz + 1))
    when(gz == 2, lambda: tell(5, gx, gy, 0))
    def await_partner(pred, index, amount=1):
        when(pred, lambda: pl.semaphore_wait(there.at[index], amount))

    counter = iter(range(64))

    def remote(src, dst, recv, device):
        return pltpu.make_async_remote_copy(
            src_ref=src, dst_ref=dst, send_sem=send_sem.at[next(counter)], recv_sem=recv_sem.at[recv],
            device_id=device, device_id_type=MESH,
        )

    up_copies, down_copies = [], []
    for i, (a, b) in enumerate(((0, 4), (7, 9))):
        up_copies.append(remote(solid.at[a:b, :, 6:8], sb.at[a:b, :, 6:8], 2 * i, (up_x, gy, gz)))
        down_copies.append(remote(solid.at[a:b, :, 0:2], sb.at[a:b, :, 16:18], 2 * i + 1, (down_x, gy, gz)))
    wave_up = remote(xo_out.at[1], xo_low, 4, (up_x, gy, gz))
    wave_down = remote(xo_out.at[0], xo_high, 5, (down_x, gy, gz))
    start(has_early[1], up_copies[0])
    start(has_early[-1], down_copies[0])

    z_up_copies = [
        remote(solid.at[a : a + 3, 6:8], z_low.at[b : b + 3], 6 + i, (gx, gy, gz + 1))
        for i, (a, b) in enumerate(((0, 0), (5, 3)))
    ]
    z_down_copies = [
        remote(solid.at[a : a + 3, 0:2], z_high.at[b : b + 3], 8 + i, (gx, gy, gz - 1))
        for i, (a, b) in enumerate(((0, 0), (5, 3)))
    ]

    tile = solid.at[2, 0]
    plane_early, plane_late = [], []
    rows = {-1: slice(7, 8), 0: slice(0, 8), 1: slice(0, 1)}
    for e in (-1, 0, 1):
        x, r = xs[-e], rows[e]
        part = solid.at[2, 0, r]
        mine = [remote(part, plane.at[0, e + 1, r], 10 + e + 1, (x, gy, k)) for k in range(1 if e == 0 else 0, nz)]
        above = remote(part, plane.at[1, e + 1, r], 13 + e + 1, (x, up_y, 0))
        below = remote(part, plane.at[1, e + 1, r], 13 + e + 1, (x, down_y, nz - 1))
        if e == 0:
            plane_early += [(z_first, mine[:1])]
            plane_late += [(z_first, mine[1:]), (both(z_first, y_up), [above]), (both(z_first, y_down), [below])]
        else:
            pred = both(z_first, has_early[-e])
            plane_early += [(pred, mine), (both(pred, y_up), [above]), (both(pred, y_down), [below])]
    plane_on = {
        e: remote(plane.at[0, 1, rows[-e]], plane.at[0, 1 - e, rows[-e]], 11 - e, (xs[e], gy, gz)) for e in (-1, 1)
    }
    own_plane = pltpu.make_async_copy(tile, plane.at[0, 1], local_sem.at[7])
    when(z_first, own_plane.start)
    for pred, copies in plane_early:
        start(pred, *copies)

    start(has_early[1], up_copies[1])
    start(has_early[-1], down_copies[1])

    lane = lax.broadcasted_iota(jnp.int32, (8, 128), 1)

    loads[1].wait()
    for end, row in ((0, 8), (1, 22)):
        xo_out[end] = jnp.concatenate([ob[0, :, row : row + 2, :], ob[1, :, row : row + 2, :]], axis=2)
    start(has_early[1], wave_up)
    start(has_early[-1], wave_down)

    loads[0].wait()
    for half, fields in enumerate((y_fields[:4], y_fields[4:])):
        packed = jnp.zeros((8, 128), F32)
        for i, f in enumerate(fields):
            for z in range(8):
                k = 8 * i + z
                packed = jnp.where(lane // 4 == k, roll_lanes(sb[f, z, 8:16, :], 4 * k + 2), packed)
        ys_out[half] = packed
    ys_copies = [
        remote(ys_out, ys_left, 16, (gx, up_y, gz)),
        remote(ys_out, ys_right, 17, (gx, down_y, gz)),
    ]
    start(y_down_near, ys_copies[1])

    loads[2].wait()
    half_lane = lax.rem(lane, 64)
    for i in range(2):
        packed = jnp.zeros((8, 128), F32)
        for d in range(16):
            if i == 0:
                folded = jnp.concatenate([ob[0, d, 8:16, :], ob[0, d, 16:24, :]], axis=1)
            else:
                folded = jnp.concatenate([ov[0, d, 0:8, :], ov[0, d, 8:16, :]], axis=1)
            cat[i, d] = folded
            packed = jnp.where(half_lane // 4 == d, roll_lanes(folded, 4 * d + 2), packed)
        yo_out[i] = packed
    yo_copies = [remote(yo_out, yo_left, 18, right), remote(yo_out, yo_right, 19, left)]
    start(both(even, has_right), yo_copies[0])
    start(gz == 2, yo_copies[1])

    row = lax.broadcasted_iota(jnp.int32, (8, 16), 0)
    col = lax.broadcasted_iota(jnp.int32, (8, 16), 1)
    pair = jnp.where(col // 2 == row, 0.5, 0.0)
    fine = lax.broadcasted_iota(jnp.int32, (64, 128), 0)
    out_lane = lax.broadcasted_iota(jnp.int32, (64, 128), 1)
    place = jnp.where(out_lane == 32 * gz + fine // 2, 0.5, 0.0)
    coarse = jnp.dot(pair, ob[0, 15, 8:24, :], precision=HIGHEST, preferred_element_type=F32)
    coarse = jnp.dot(coarse, place, precision=HIGHEST, preferred_element_type=F32)
    coarse_out[...] = coarse
    coarse_copies = [remote(coarse_out, bed_part.at[k], 20 + k, (gx, gy, 0)) for k in range(1, nz)]
    start(gz == 2, coarse_copies[1])

    wy = weights(lane, 128, y_first, y_last, True)
    for i, f in enumerate(y_fields):
        own = sb[f, :, 8:16, :]
        dys[i] = total(wy[d] * (roll_lanes(own, -d) if d else own) for d in REACH)
    wo = weights(half_lane, 64, jnp.logical_and(y_first, z_first), jnp.logical_and(y_last, z_last), True)
    for i in range(2):
        for d0 in range(0, 16, 8):
            own = cat[i, d0 : d0 + 8]
            dyo[i, d0 : d0 + 8] = total(wo[d] * (roll_lanes(own, -d) if d else own) for d in REACH)
    sub = lax.broadcasted_iota(jnp.int32, (8, 128), 0)
    wx = weights(sub, 8, x_first, x_last, False)
    for i, f in enumerate(x_fields):
        own = sb[f, :, 8:16, :]
        txs[i] = wx[0] * own + wx[3] * pltpu.roll(own, 5, 1) + wx[-3] * pltpu.roll(own, 3, 1)

    start(even, *z_up_copies)
    start(gz == 2, *z_down_copies)
    await_partner(odd, 4)
    start(odd, *z_down_copies, yo_copies[1])
    for k in (1, 3):
        start(gz == k, coarse_copies[k - 1])
    await_partner(gz == 1, 3)
    start(gz == 1, *z_up_copies, yo_copies[0])
    await_partner(z_first, 5)
    start(*plane_late[0][:1], *plane_late[0][1])
    await_partner(y_up_near, 2)
    near_link = both(z_first, y_up_near)
    far_link = both(far_up, gz == 2)
    when(jnp.logical_or(near_link, far_link), lambda: tell(7, gx, gy, nz - 1))
    when(jnp.logical_or(near_link, far_link), lambda: tell(6, gx, up_y, 0))
    when(far_link, lambda: tell(6, gx, up_y, 1))
    for k in (0, 1):
        when(far_link, lambda: tell(7, gx, gy, k))
    await_partner(y_up_word, 7)
    start(y_up, ys_copies[0])
    start(*plane_late[1][:1], *plane_late[1][1])
    await_partner(jnp.logical_or(both(z_first, y_down), y_down_word), 6)
    start(y_down_word, ys_copies[1])
    start(both(z_first, y_down), yo_copies[1], *plane_late[2][1])
    await_partner(both(z_last, y_up), 7)
    start(both(z_last, y_up), yo_copies[0])
    for e, index, copies in ((1, 0, up_copies + [wave_up]), (-1, 1, down_copies + [wave_down])):
        await_partner(has_late[e], index)
        start(has_late[e], *copies)
    sides = ((both(z_first, y_down), 127), (both(z_last, y_up), 0))

    def plane_wait(s, e):
        pltpu.make_async_remote_copy(
            src_ref=solid.at[2, 0, rows[e]], dst_ref=plane.at[s, e + 1, rows[e]], send_sem=send_sem.at[63], recv_sem=recv_sem.at[10 + 3 * s + e + 1],
            device_id=(gx, up_y, gz), device_id_type=MESH,
        ).wait_recv()

    def merge(e):
        for pred, at in sides:

            @pl.when(pred)
            def _(at=at):
                plane_wait(1, e)
                plane[0, e + 1] = jnp.where(lane == at, plane[1, e + 1], plane[0, e + 1])

    when(z_first, own_plane.wait)
    when(z_down, lambda: plane_wait(0, 0))
    merge(0)
    for e in (-1, 1):
        start(has_late[e], plane_on[e])

    landed(y_down, ys_copies[0])
    landed(y_up, ys_copies[1])
    at_edge = jnp.logical_or(lane < 2, lane >= 126)
    for half, fields in enumerate((y_fields[:4], y_fields[4:])):
        rim = rim_from_sides(ys_left[half], ys_right[half], lane, y_first, y_last)
        for i in range(len(fields)):
            for z in range(8):
                k = 8 * i + z
                dys[4 * half + i, z] += jnp.where(at_edge, roll_lanes(rim, -4 * k - 2), 0.0)
    landed(has_left, yo_copies[0])
    landed(has_right, yo_copies[1])
    at_half_edge = jnp.logical_or(half_lane < 2, half_lane >= 62)
    for i in range(2):
        rim = rim_from_sides(
            roll_lanes(yo_left[i], 64), roll_lanes(yo_right[i], 64), lane,
            jnp.logical_and(y_first, z_first), jnp.logical_and(y_last, z_last),
        )
        for d in range(16):
            dyo[i, d] += jnp.where(at_half_edge, roll_lanes(rim, -4 * d - 2), 0.0)

    loads[3].wait()

    landed(z_down, *z_up_copies)
    landed(z_up, *z_down_copies)

    for i, f in enumerate(z_fields):
        def level(z, i=i, f=f):
            if z < 0:
                return z_low[i, z + 2]
            if z >= 8:
                return z_high[i, z - 8]
            return sb[f, z, 8:16, :]

        for z in range(8):
            table = level_weights(z, 8, z_first, z_last)
            dzs[i, z] = mb[3, z] * total(w * level(z + d) for d, w in table.items() if -2 <= z + d < 10)

    @pl.when(z_first)
    def _():
        for k in range(1, nz):
            pltpu.make_async_remote_copy(
                src_ref=coarse_out, dst_ref=bed_part.at[k], send_sem=send_sem.at[63], recv_sem=recv_sem.at[20 + k],
                device_id=(gx, up_y, gz), device_id_type=MESH,
            ).wait_recv()
        scale = inv_norm * mb[3, 0]
        bed_pressure = coarse_out[...] + total(bed_part[k] for k in range(1, nz))
        dzs[5, 0] += scale * sb[7, 0, 8:16, :]
        dzs[4, 0] += scale * sb[6, 0, 8:16, :]
        dzs[3, 0] += scale * (sb[5, 0, 8:16, :] + bed_pressure)

    loads[4].wait()

    def unfold(i, d):
        folded = dyo[i, d]
        return jnp.concatenate([folded[:, 0:64], folded[:, 64:128]], axis=0)

    for d in range(16):
        bulk = jnp.full((16, 64), med[0, d], F32)
        light = jnp.full((16, 64), med[1, d], F32)
        pressure, flow_v, flow_w = ob[0, d, 8:24, :], ov[0, d], ov[1, d]
        table = level_weights(d, 16, True, True)
        dz_w = total(w * ov[1, d + k] for k, w in table.items())
        dz_p = total(w * ob[0, d + k, 8:24, :] for k, w in table.items())
        part = -bulk * (2.0 * unfold(1, d) + dz_w) + gravity * flow_w / light
        opre[d] = step_size * part
        rate_v = (-2.0 * step_size) * light * unfold(0, d)
        rate_w = -light * dz_p
        if d == 0:
            rate_w = rate_w - inv_norm * light * pressure
        rate_w = step_size * rate_w
        o_rate[2, d] = rate_v
        o_rate[3, d] = rate_w
        o_next[2, d] = flow_v + section_weight * rate_v
        o_next[3, d] = flow_w + section_weight * rate_w

    loads[5].wait()
    loads[6].wait()
    fine_x = lax.broadcasted_iota(jnp.int32, (24, 16), 1)
    coarse_x = lax.broadcasted_iota(jnp.int32, (24, 16), 0) + (8 * gx - 8)
    near_x = 8 * gx + fine_x // 2
    far_x = jnp.clip(near_x + ox[...], 0, 8 * nx - 1)
    blend_x = jnp.where(coarse_x == near_x, 0.75, 0.0) + jnp.where(coarse_x == far_x, 0.25, 0.0)
    fine_y = lax.broadcasted_iota(jnp.int32, (128, 64), 1)
    coarse_y = lax.broadcasted_iota(jnp.int32, (128, 64), 0)
    near_y = 128 * gy + 32 * gz + fine_y // 2
    far_y = jnp.clip(near_y + oy[...], 0, 128 * ny - 1)
    blend_y = jnp.where(coarse_y == lax.rem(near_y, 128), 0.75, 0.0)
    blend_y = blend_y + jnp.where(coarse_y == lax.rem(far_y, 128), 0.25, 0.0)

    landed(x_down, *up_copies, wave_up)
    landed(x_up, *down_copies, wave_down)
    for rim, row in ((xo_low, 6), (xo_high, 24)):
        for i in range(2):
            ob[i, :, row : row + 2, :] = rim[:, :, 64 * i : 64 * i + 64]

    pos = lax.broadcasted_iota(jnp.int32, (16, 64), 0)
    wp = weights(pos, 16, x_first, x_last, False)
    far_up, far_down = wp[3] != 0.0, wp[-3] != 0.0

    def dx_ocean(i, d):
        out = total(wp[k] * ob[i, d, 8 + k : 24 + k, :] for k in range(-2, 3))
        out = out + wp[3] * jnp.where(far_up, ob[i, d, 11:27, :], 0.0)
        return out + wp[-3] * jnp.where(far_down, ob[i, d, 5:21, :], 0.0)

    def ocean_out(i, d, rate):
        o_rate[i, d] = rate
        o_next[i, d] = ob[i, d, 8:24, :] + section_weight * rate

    for d in range(16):
        bulk = jnp.full((16, 64), (-2.0 * step_size) * med[0, d], F32)
        light = jnp.full((16, 64), (-2.0 * step_size) * med[1, d], F32)
        rate_p = opre[d] + bulk * dx_ocean(1, d)
        ocean_out(1, d, light * dx_ocean(0, d))
        if d < 15:
            ocean_out(0, d, rate_p)

    for e in (-1, 1):
        when(has[e], lambda: plane_wait(0, e))
        when(has_late[e], lambda: merge(e))

    window = plane[0].reshape(24, 128)
    bed_speed = lax.dot_general(
        blend_x, window, (((0,), (0,)), ((), ())), precision=HIGHEST, preferred_element_type=F32
    )
    bed_speed = jnp.dot(bed_speed, blend_y, precision=HIGHEST, preferred_element_type=F32)

    bulk = jnp.full((16, 64), (step_size * inv_norm) * med[0, 15], F32)
    ocean_out(0, 15, rate_p + bulk * (ov[1, 15] - bed_speed))

    sent(x_up, *up_copies, wave_up)
    sent(x_down, *down_copies, wave_down)
    for e in (-1, 1):
        sent(has_late[e], plane_on[e])
    sent(y_up, ys_copies[0])
    sent(y_down, ys_copies[1])
    sent(has_right, yo_copies[0])
    sent(has_left, yo_copies[1])
    sent(z_up, *z_up_copies)
    sent(z_down, *z_down_copies)
    for pred, copies in plane_late:
        sent(pred, *copies)
    for pred, copies in plane_early:
        sent(pred, *copies)
    for k in range(1, nz):
        sent(gz == k, coarse_copies[k - 1])


def finish_kernel(nx, o_next, o_rate, sb, mb, txs, dys, dzs, s_next_out, s_rate_out, o_next_out, o_rate_out, s_next, s_rate, sem):
    copies = [
        pltpu.make_async_copy(o_next, o_next_out, sem.at[0]),
        pltpu.make_async_copy(o_rate, o_rate_out, sem.at[1]),
    ]
    for copy in copies:
        copy.start()
    gx = lax.axis_index("gx")
    sub = lax.broadcasted_iota(jnp.int32, (8, 128), 0)
    wx = weights(sub, 8, gx == 0, gx == nx - 1, False)

    def dx(i, f, z):
        out = txs[i, z]
        for d in (-2, -1, 1, 2):
            out = out + wx[d] * sb[f, z, 8 + d : 16 + d, :]
        return out

    for z in range(8):
        own = [sb[f, z, 8:16, :] for f in range(9)]
        b, lam, mu = step_size * mb[0, z], step_size * mb[1, z], step_size * mb[2, z]
        d_x = {f: dx(i, f, z) for i, f in enumerate(x_fields)}
        d_y = {f: dys[i, z] for i, f in enumerate(y_fields)}
        d_z = {f: dzs[i, z] for i, f in enumerate(z_fields)}
        dilation = lam * (d_x[0] + d_y[1] + d_z[2])
        mu2 = 2.0 * mu
        rates = [
            b * (d_x[3] + d_y[8] + d_z[7]),
            b * (d_x[8] + d_y[4] + d_z[6]),
            b * (d_x[7] + d_y[6] + d_z[5]),
            dilation + mu2 * d_x[0],
            dilation + mu2 * d_y[1],
            dilation + mu2 * d_z[2],
            mu * (d_z[1] + d_y[2]),
            mu * (d_z[0] + d_x[2]),
            mu * (d_y[0] + d_x[1]),
        ]
        for f in range(9):
            s_rate[f, z] = rates[f]
            s_next[f, z] = own[f] + section_weight * rates[f]
        if z % 4 == 3:
            for i, (held, out) in enumerate(((s_next, s_next_out), (s_rate, s_rate_out))):
                copy = pltpu.make_async_copy(held.at[:, z - 3 : z + 1], out.at[:, z - 3 : z + 1], sem.at[1 + z + i])
                copy.start()
                copies.append(copy)
    for copy in copies:
        copy.wait()


def body(sizes, solid_state, material, ocean_state, ocean_medium, offset_x, offset_y):
    outs = (solid_state.shape, solid_state.shape, ocean_state.shape, ocean_state.shape)
    v = lambda *shape: pltpu.VMEM(shape, F32)
    held = pl.pallas_call(
        functools.partial(section_kernel, sizes),
        out_shape=[pltpu.VMEM(shape, F32) for shape in outs[2:]]
        + [v(9, 8, 24, 128), v(4, 8, 8, 128), v(6, 8, 8, 128), v(6, 8, 8, 128), v(6, 8, 8, 128)],
        in_specs=[pl.BlockSpec(memory_space=pltpu.HBM)] * 6,
        out_specs=[pl.BlockSpec(memory_space=pltpu.VMEM)] * 7,
        scratch_shapes=[
            v(2, 16, 32, 64), v(2, 16, 16, 64),
            pltpu.SMEM((2, 16), F32), pltpu.VMEM((1, 16), jnp.int32), pltpu.VMEM((1, 64), jnp.int32),
            v(6, 2, 8, 128), v(6, 2, 8, 128), v(2, 3, 8, 128), v(4, 8, 128),
            v(2, 16, 2, 128), v(16, 2, 128), v(16, 2, 128),
            v(2, 8, 128), v(2, 8, 128), v(2, 8, 128), v(2, 8, 128), v(2, 8, 128), v(2, 8, 128), v(8, 128),
            v(2, 16, 8, 128), v(16, 16, 64), v(2, 16, 8, 128),
            pltpu.SemaphoreType.DMA((8,)), pltpu.SemaphoreType.DMA((64,)), pltpu.SemaphoreType.DMA((24,)),
            pltpu.SemaphoreType.REGULAR((8,)),
        ],
        compiler_params=pltpu.CompilerParams(
            vmem_limit_bytes=16 * 2**20, collective_id=0, has_side_effects=True
        ),
        name="section",
    )(*(
        pltpu.with_memory_space_constraint(a, pltpu.HBM)
        for a in (solid_state, material, ocean_state, ocean_medium, offset_x.reshape(1, -1), offset_y.reshape(1, -1))
    ))
    return pl.pallas_call(
        functools.partial(finish_kernel, sizes[0]),
        out_shape=[jax.ShapeDtypeStruct(shape, F32) for shape in outs],
        in_specs=[pl.BlockSpec(memory_space=pltpu.VMEM)] * 7,
        out_specs=[pl.BlockSpec(memory_space=pl.ANY)] * 4,
        scratch_shapes=[v(*outs[0]), v(*outs[0]), pltpu.SemaphoreType.DMA((10,))],
        compiler_params=pltpu.CompilerParams(vmem_limit_bytes=4 * 2**20),
        name="finish",
    )(*held)


def solution(mesh):
    sizes = (mesh.shape["gx"], mesh.shape["gy"], mesh.shape["gz"])
    solid = P(None, "gz", "gx", "gy")
    ocean = P(None, None, "gx", ("gy", "gz"))
    return jax.shard_map(
        functools.partial(body, sizes),
        mesh=mesh,
        in_specs=(solid, solid, ocean, P(), P("gx"), P(("gy", "gz"))),
        out_specs=(solid, solid, ocean, ocean),
        check_vma=False,
    )
```
